32 devices in a mesh: seq: 8 (over y, x, core), wsh: 4 (over z).
Axes of the slice: x: 2, y: 2, z: 4, core: 2. Of those that a mesh axis runs over, the one named last changes fastest.
Arguments:
- tokens: bfloat16 [4, 4096, 1024], P('wsh', 'seq'), may hold values from -6 to 6
- doc_start: int32 [4, 4096], P('wsh', 'seq'), may hold values from 0 to 4095, as said below
- norm1_gain: float32 [1024], P('wsh'), may hold values from 0.5 to 1.5
- in_weight: float32 [1024, 3072], P('wsh'), may hold values from -0.1875 to 0.1875
- conv_weight: float32 [1024, 3], P('wsh'), may hold values from -3 to 3
- out_weight: float32 [1024, 1024], P('wsh'), may hold values from -0.1875 to 0.1875
- norm2_gain: float32 [1024], P('wsh'), may hold values from 0.5 to 1.5
- gate_up_weight: float32 [1024, 9216], P('wsh'), may hold values from -0.1875 to 0.1875
- down_weight: float32 [4608, 1024], P('wsh'), may hold values from -0.09375 to 0.09375
- out_grad: bfloat16 [4, 4096, 1024], P('wsh', 'seq'), may hold values from -6 to 6
Outputs:
- block_out: bfloat16 [4, 4096, 1024], P('wsh', 'seq')
- input_grad: bfloat16 [4, 4096, 1024], P('wsh', 'seq')
- norm1_grad: float32 [1024], P('wsh')
- in_grad: float32 [1024, 3072], P('wsh')
- conv_grad: float32 [1024, 3], P('wsh')
- out_proj_grad: float32 [1024, 1024], P('wsh')
- norm2_grad: float32 [1024], P('wsh')
- gate_up_grad: float32 [1024, 9216], P('wsh')
- down_grad: float32 [4608, 1024], P('wsh')
The draws below stay inside these ranges and needn't reach their ends.
Inputs may be any that keep to these rules, and one draw needn't show every extreme that they name: `doc_start`: each value is the position of its token's document's first token; a document begins at position 0, at the last position 4095, and at least once in every run of 512 positions that starts at a multiple of 512, never at the first two positions of such a run after the first.
All inputs are finite; a program needn't handle non-finite values.
Results may differ from the reference program's by a relative error of at most 0.012.
The reference program's roundings to bfloat16 on the way count: a program that leaves them out, or rounds other values in their place, can miss the bound.
Values may be sent and summed in bfloat16 or wider, within the bound.
A program may use at most 256 MiB of HBM per device.

```python
import jax
import jax.numpy as jnp
from jax import lax

D = 1024
FF = 4608
TOK_DEV = 512
SEQS = 4
LEN = 4096


def draw_doc_start(key, part):
    key_one, key_two = jax.random.split(jax.random.fold_in(key, 17))
    shards = LEN // TOK_DEV
    forced = jax.random.randint(key_one, (SEQS, shards), 2, TOK_DEV)
    local = jnp.arange(TOK_DEV, dtype=jnp.int32)
    hit = local[None, None, :] == forced[:, :, None]
    extra = jax.random.randint(key_two, (SEQS, shards, TOK_DEV), 0, 256) == 0
    mark = (hit | extra & (local >= 2)[None, None, :]).reshape(SEQS, LEN)
    place = jnp.arange(LEN, dtype=jnp.int32)
    mark = mark | (place == LEN - 1)[None, :]
    marked = jnp.where(mark, place[None, :], 0).astype(jnp.int32)
    return lax.cummax(marked, axis=1)


def block_scale(own_key, shape, cuts, least, high):
    gain = 1.0
    for dim, parts in cuts:
        draws = jax.random.uniform(jax.random.fold_in(jax.random.fold_in(own_key, 6), dim), (parts,), jnp.float32, least / len(cuts), high / len(cuts))
        gain = gain * jnp.repeat(jnp.exp(draws), shape[dim] // parts).reshape((-1,) + (1,) * (len(shape) - 1 - dim))
    return gain


def gaussian(own_key, shape, deviation, limit, pieces=(), held_as=jnp.bfloat16):
    values = deviation * jax.random.normal(own_key, shape, jnp.float32)
    if pieces:
        values = values * block_scale(own_key, shape, pieces, -0.22, 0.18)
    return jnp.clip(values, -limit, limit).astype(held_as)


def setup_inputs(seed: int = 0) -> dict:
    splits = jax.random.split(jax.random.key(seed), 11)
    tokens = gaussian(splits[0], (SEQS, LEN, D), 1.0, 6.0, ((0, 4), (1, 8)))
    doc_start = draw_doc_start(jax.random.fold_in(splits[10], 71), 0)
    norm1_gain = jnp.clip(1.0 + 0.1 * jax.random.normal(splits[2], (D,), jnp.float32), 0.5, 1.5)
    in_weight = gaussian(splits[3], (D, 3 * D), D ** -0.5, 0.1875, ((0, 4),), jnp.float32)
    conv_weight = gaussian(splits[4], (D, 3), 0.6, 3.0, ((0, 4),), jnp.float32)
    out_weight = gaussian(splits[5], (D, D), D ** -0.5, 0.1875, ((0, 4),), jnp.float32)
    norm2_gain = jnp.clip(1.0 + 0.1 * jax.random.normal(splits[6], (D,), jnp.float32), 0.5, 1.5)
    gate_up_weight = gaussian(splits[7], (D, 2 * FF), D ** -0.5, 0.1875, ((0, 4),), jnp.float32)
    down_weight = gaussian(splits[8], (FF, D), FF ** -0.5, 0.09375, ((0, 4),), jnp.float32)
    out_grad = gaussian(splits[9], (SEQS, LEN, D), 1.0, 6.0, ((0, 4), (1, 8)))
    return {"tokens": tokens, "doc_start": doc_start, "norm1_gain": norm1_gain, "in_weight": in_weight, "conv_weight": conv_weight, "out_weight": out_weight, "norm2_gain": norm2_gain, "gate_up_weight": gate_up_weight, "down_weight": down_weight, "out_grad": out_grad}


@jax.custom_vjp
def low(v):
    return lax.optimization_barrier(v.astype(jnp.bfloat16)).astype(jnp.float32)

@jax.custom_vjp
def low_back(v):
    return v

def low_keep(v):
    return (low(v), None)

def low_pass(kept, grad):
    return (grad,)

def back_keep(v):
    return (v, None)

def back_low(kept, grad):
    return (low(grad),)
low.defvjp(low_keep, low_pass)
low_back.defvjp(back_keep, back_low)
epsilon = 1e-06

def matmul(left, right):
    return jnp.dot(left, right, precision=lax.Precision.HIGHEST, preferred_element_type=jnp.float32)

def forward(xf, starts, gain_one, w_in, conv_w, w_out, gain_two, w_gu, w_down):
    width = xf.shape[1]
    hidden = w_down.shape[0]
    rate_one = lax.rsqrt(lax.optimization_barrier(jnp.mean(xf * xf, axis=-1, keepdims=True)) + epsilon)
    normed = low(xf * rate_one * low(gain_one))
    proj = low_back(matmul(normed, low(w_in)))
    bpart = proj[:, :width]
    cpart = proj[:, width:2 * width]
    xpart = proj[:, 2 * width:]
    gated = low(bpart * xpart)
    taps = low(conv_w)
    place = jnp.arange(xf.shape[0], dtype=jnp.int32)
    mixed = taps[:, 0] * gated
    for lag in (1, 2):
        moved = jnp.concatenate([jnp.zeros((lag, width), jnp.float32), gated[:-lag]], 0)
        keep = (place - lag >= starts).astype(jnp.float32)[:, None]
        mixed = mixed + keep * taps[:, lag] * moved
    zed = low(cpart * mixed)
    first = xf + low_back(matmul(zed, low(w_out)))
    rate_two = lax.rsqrt(lax.optimization_barrier(jnp.mean(first * first, axis=-1, keepdims=True)) + epsilon)
    normed_two = low(first * rate_two * low(gain_two))
    both = low_back(matmul(normed_two, low(w_gu)))
    gate = both[:, :hidden]
    upper = both[:, hidden:]
    act = low(jax.nn.silu(gate) * upper)
    return first + matmul(act, low(w_down))

def reference(tokens, doc_start, norm1_gain, in_weight, conv_weight, out_weight, norm2_gain, gate_up_weight, down_weight, out_grad):
    params = (norm1_gain, in_weight, conv_weight, out_weight, norm2_gain, gate_up_weight, down_weight)

    def one_seq(acc, item):
        rows, starts, cot = item
        xf = rows.astype(jnp.float32)

        def run(x_in, *weights):
            return forward(x_in, starts, *weights)
        value, pull = jax.vjp(run, xf, *params)
        grads = pull(cot.astype(jnp.float32))
        acc = tuple((a + g for a, g in zip(acc, grads[1:])))
        return (acc, (value.astype(jnp.bfloat16), grads[0].astype(jnp.bfloat16)))
    init = tuple((jnp.zeros(p.shape, jnp.float32) for p in params))
    acc, (outs, grads_in) = lax.scan(one_seq, init, (tokens, doc_start, out_grad))
    return (outs, grads_in, acc[0], acc[1], acc[2], acc[3], acc[4], acc[5], acc[6])
```

```python
import jax
import jax.numpy as jnp
from jax import lax
from jax.sharding import PartitionSpec as P

epsilon = 1e-06
low = jnp.bfloat16
full = jnp.float32


def inner(left, right):
    return lax.dot_general(left, right, (((0,), (0,)), ((), ())), preferred_element_type=full)


def outer(left, right):
    return lax.dot_general(left, right, (((1,), (1,)), ((), ())), preferred_element_type=full)


def plain(left, right):
    return jnp.dot(left, right, preferred_element_type=full)


def build(seq, wsh):
    def flip(value, bit):
        return lax.ppermute(value, "seq", [(i, i ^ (1 << bit)) for i in range(seq)])

    def zflip(value, mask):
        return lax.ppermute(value, "wsh", [(i, i ^ mask) for i in range(wsh)])

    def chosen(value, pairs):
        return lax.ppermute(
            value, ("seq", "wsh"), [(a * wsh + b, c * wsh + d) for (a, b), (c, d) in pairs]
        )

    def take(buf, at):
        start, size = [], []
        for dim in range(buf.ndim):
            index = at[dim] if dim < len(at) else None
            start.append(0 if index is None else index)
            size.append(buf.shape[dim] if index is None else 1)
        return lax.dynamic_slice(buf, start, size)

    def put(buf, value, at):
        start = [
            0 if dim >= len(at) or at[dim] is None else at[dim] for dim in range(buf.ndim)
        ]
        return lax.dynamic_update_slice(buf, value, start)

    def local(
        tokens,
        doc_start,
        norm1_gain,
        in_weight,
        conv_weight,
        out_weight,
        norm2_gain,
        gate_up_weight,
        down_weight,
        out_grad,
    ):
        me = lax.axis_index("seq")
        z = lax.axis_index("wsh")
        core, xbit, ybit = me % 2, (me // 2) % 2, (me // 4) % 2
        quarter = me % 4
        cot = out_grad[0]
        rows, width = cot.shape
        part = width // wsh
        hidden = down_weight.shape[0] * wsh
        hq = hidden // 4

        def by_z(value):
            return jnp.concatenate(
                [lax.dynamic_slice_in_dim(value, (z ^ j) * part, part, 1) for j in range(wsh)], 1
            )

        extra = jnp.concatenate(
            [norm1_gain[:, None], norm2_gain[:, None], conv_weight], 1
        ).astype(low)
        extra = jnp.pad(extra, ((0, 0), (0, 128 - extra.shape[1])))
        shard_a = in_weight[:, : 2 * width].astype(low)
        shard_b = jnp.concatenate(
            [in_weight[:, 2 * width :].astype(low), out_weight.astype(low), extra], 1
        )

        def gather_conv(shard, order):
            cols = shard.shape[1]
            buf = jnp.zeros((2, 2, 2, 2, 2, part // 8, cols), low)
            buf = put(buf, shard.reshape(1, 1, 2, 2, 2, part // 8, cols), ())
            got = zflip(take(buf, (0, 0, ybit, xbit, core)), 2)
            buf = put(buf, got, (1, 0, ybit, xbit, core))
            got = zflip(take(buf, (None, 0, ybit, xbit, core)), 1)
            buf = put(buf, got, (None, 1, ybit, xbit, core))
            buf = buf.reshape(4, 2, 2, 2, part // 8, cols)
            away = buf[1:]
            for step in order:
                index = [None, ybit, xbit, core]
                for done in order[: order.index(step)]:
                    index[{2: 1, 1: 2, 0: 3}[done]] = None
                got = flip(take(away, index), step)
                spot = {2: 1, 1: 2, 0: 3}[step]
                index[spot] = 1 - index[spot]
                away = put(away, got, index)
            return jnp.concatenate([shard, away.reshape(3 * part, cols)], 0)

        w_a = gather_conv(shard_a, (1, 2, 0))
        w_b = gather_conv(shard_b, (2, 1, 0))
        w_x = w_b[:, :width]
        w_out = w_b[:, width : 2 * width]
        small = w_b[:, 2 * width : 2 * width + 8].astype(full).T
        gain_one, gain_two = small[0:1], small[1:2]
        taps = [by_z(small[k : k + 1]) for k in (2, 3, 4)]

        def gather_group(value):
            pair = jnp.concatenate([value, flip(value, 1)], 0)
            return jnp.concatenate([pair, flip(pair, 0)], 0)

        cot_all = gather_group(cot)

        gate_up = jnp.concatenate(
            [
                lax.dynamic_slice_in_dim(gate_up_weight, quarter * hq, hq, 1),
                lax.dynamic_slice_in_dim(gate_up_weight, hidden + quarter * hq, hq, 1),
            ],
            1,
        ).astype(low)
        buf = jnp.zeros((2, 2, 2, part // 2, 2 * hq), low)
        buf = put(buf, gate_up.reshape(1, 1, 2, part // 2, 2 * hq), ())
        buf = put(buf, zflip(take(buf, (0, 0, ybit)), 2), (1, 0, ybit))
        buf = put(buf, zflip(take(buf, (None, 0, ybit)), 1), (None, 1, ybit))
        buf = buf.reshape(4, 2, part // 2, 2 * hq)
        away = put(buf[1:], flip(take(buf[1:], (None, ybit)), 2), (None, 1 - ybit))
        w_gu = jnp.concatenate([gate_up, away.reshape(3 * part, 2 * hq)], 0)

        halves = down_weight.astype(low).reshape(2, hq // 2, width)
        half = take(halves, (ybit,))
        got = chosen(half, [((s, s % 4), (s, s % 4 ^ 2)) for s in range(seq)])
        half = jnp.where((z ^ quarter) == 2, got, half)
        got = chosen(
            half, [((s, s % 4 ^ m), (s, s % 4 ^ m ^ 1)) for s in range(seq) for m in (0, 2)]
        )
        half = jnp.where((z ^ quarter) % 2 == 1, got, half)
        other = flip(half, 2)
        w_down = put(put(halves, half, (ybit,)), other, (1 - ybit,)).reshape(hq, width)

        xf = tokens[0].astype(full)
        starts = doc_start[0]
        rate_one = lax.rsqrt(jnp.mean(xf * xf, axis=-1, keepdims=True) + epsilon)
        normed = xf * rate_one
        normed_z = by_z(normed)
        h = (normed_z * gain_one).astype(low)
        proj_a = plain(h, w_a)
        bpart, cpart = proj_a[:, :width], proj_a[:, width:]
        xpart = plain(h, w_x)
        gated = (bpart * xpart).astype(low)
        edge = lax.ppermute(gated[rows - 2 :], "seq", [(i, i + 1) for i in range(seq - 1)])
        extended = jnp.concatenate([edge, gated], 0).astype(full)
        place = me * rows + jnp.arange(rows, dtype=jnp.int32)
        keep_one = (place - 1 >= starts).astype(full)[:, None]
        keep_two = (place - 2 >= starts).astype(full)[:, None]
        current = extended[2:]
        lag_one = extended[1:-1]
        lag_two = extended[:-2]
        mixed = taps[0] * current + keep_one * taps[1] * lag_one + keep_two * taps[2] * lag_two
        zed = by_z((cpart * mixed).astype(low))
        first = xf + plain(zed, w_out)
        rate_two = lax.rsqrt(jnp.mean(first * first, axis=-1, keepdims=True) + epsilon)
        normed_two = by_z(first * rate_two)
        second = (normed_two * gain_two).astype(low)

        second_all = gather_group(second)
        both = plain(second_all, w_gu)
        gate, upper = both[:, :hq], both[:, hq:]
        sigma = jax.nn.sigmoid(gate)
        swish = gate * sigma
        act = (swish * upper).astype(low)
        grad_act = outer(cot_all, w_down)
        grad_gate = grad_act * upper * (sigma * (1.0 + gate * (1.0 - sigma)))
        grad_both = jnp.concatenate([grad_gate, grad_act * swish], 1).astype(low)

        def scatter_group(value):
            mine, theirs = value[: 2 * rows], value[2 * rows :]
            mine = mine + flip(theirs.astype(low), 0).astype(full)
            return mine[:rows] + flip(mine[rows:].astype(low), 1).astype(full)

        result = first + scatter_group(plain(act, w_down))
        grad_second = scatter_group(outer(grad_both, w_gu))
        grad_down = inner(act, cot_all).astype(low)
        grad_gu = inner(second_all, grad_both).astype(low)

        def plus(a, b):
            return (a.astype(full) + b.astype(full)).astype(low)

        def upper_bits(value):
            for bit in range(3, seq.bit_length() - 1):
                value = plus(value, flip(value, bit))
            return value

        buf = grad_gu.reshape(4, 2, part // 2, 2 * hq)
        buf = plus(take(buf, (None, ybit)), flip(take(buf, (None, 1 - ybit)), 2))
        buf = buf.reshape(2, 2, part // 2, 2 * hq)
        buf = plus(buf[:, 0], zflip(buf[:, 1], 1))
        buf = upper_bits(plus(buf[0], zflip(buf[1], 2)))

        def spread_gu(piece, order):
            home = jnp.zeros((2, 2, 2, part // 2, hq), low)
            index = [xbit, core, ybit]
            home = put(home, piece.reshape(1, 1, 1, part // 2, hq), index)
            for step in order:
                got = flip(take(home, index), step)
                spot = {1: 0, 0: 1, 2: 2}[step]
                index[spot] = 1 - index[spot]
                home = put(home, got, index)
                index[spot] = None
            home = home.reshape(4, part, hq)
            return jnp.concatenate([home[i] for i in range(4)], 1)

        total_gu = jnp.concatenate(
            [spread_gu(buf[:, :hq], (1, 2, 0)), spread_gu(buf[:, hq:], (2, 1, 0))], 1
        ).astype(full)

        buf = grad_down.reshape(2, hq // 2, width)
        half = plus(take(buf, (ybit,)), flip(take(buf, (1 - ybit,)), 2))
        half = plus(
            half,
            chosen(
                half, [((s, s % 4 ^ m ^ 1), (s, s % 4 ^ m)) for s in range(seq) for m in (0, 2)]
            ),
        )
        half = plus(half, chosen(half, [((s, s % 4 ^ 2), (s, s % 4)) for s in range(seq)]))
        half = upper_bits(half)
        got = chosen(half, [((s, s % 4), (s ^ 2, s % 4)) for s in range(seq)])
        half = jnp.where(quarter == z, half, got)
        evens = [(s, b) for s in range(seq) for b in range(wsh) if (s ^ b) % 2 == 0]
        other = chosen(half, [((s, b), (s ^ 4, b)) for s, b in evens])
        home = put(put(jnp.zeros((2, hq // 2, width), low), half, (ybit,)), other, (1 - ybit,))
        got = chosen(home, [((s, b), (s ^ 1, b)) for s, b in evens])
        total_down = jnp.where((me ^ z) % 2 == 0, home, got).reshape(hq, width).astype(full)

        grad_gain_two = jnp.sum(grad_second * normed_two, axis=0)
        scaled_two = grad_second * gain_two
        grad_first = cot.astype(full) + by_z(
            rate_two
            * (scaled_two - normed_two * jnp.mean(scaled_two * normed_two, axis=-1, keepdims=True))
        )
        grad_branch = grad_first.astype(low)
        grad_outw = inner(zed, grad_branch)
        grad_zed = by_z(outer(grad_branch, w_out))
        grad_cpart = grad_zed * mixed
        grad_mixed = grad_zed * cpart
        term_one = keep_one * grad_mixed
        term_two = keep_two * grad_mixed
        grad_taps = [
            jnp.sum(grad_mixed * current, axis=0),
            jnp.sum(term_one * lag_one, axis=0),
            jnp.sum(term_two * lag_two, axis=0),
        ]
        grad_ext = jnp.pad(taps[0] * grad_mixed, ((2, 0), (0, 0)))
        grad_ext = grad_ext + jnp.pad(taps[1] * term_one, ((1, 1), (0, 0)))
        grad_ext = grad_ext + jnp.pad(taps[2] * term_two, ((0, 2), (0, 0)))
        returned = lax.ppermute(grad_ext[:2], "seq", [(i + 1, i) for i in range(seq - 1)])
        grad_gated = grad_ext[2:] + jnp.pad(returned, ((rows - 2, 0), (0, 0)))
        grad_proj = jnp.concatenate(
            [grad_gated * xpart, grad_cpart, grad_gated * bpart], 1
        ).astype(low)
        grad_a = inner(h, grad_proj[:, : 2 * width]).astype(low)
        grad_x = inner(h, grad_proj[:, 2 * width :])
        grad_normed = outer(grad_proj[:, : 2 * width], w_a) + outer(
            grad_proj[:, 2 * width :], w_x
        )
        grad_gain_one = jnp.sum(grad_normed * normed_z, axis=0)
        scaled_one = grad_normed * gain_one
        grad_input = grad_first + by_z(
            rate_one
            * (scaled_one - normed_z * jnp.mean(scaled_one * normed_z, axis=-1, keepdims=True))
        )
        tail = jnp.stack(
            [grad_gain_one, grad_gain_two] + [by_z(g[None])[0] for g in grad_taps], 1
        )
        tail = jnp.pad(tail, ((0, 0), (0, 128 - tail.shape[1])))
        grad_b = jnp.concatenate([grad_x, grad_outw, tail], 1).astype(low)

        def sum_conv(value, order):
            cols = value.shape[1]
            where = {2: 1, 1: 2, 0: 3}
            buf = value.reshape(4, 2, 2, 2, part // 8, cols)
            mine = {2: ybit, 1: xbit, 0: core}
            for step in (0,) + order:
                send, keep = [None] * 4, [None] * 4
                send[where[step]], keep[where[step]] = 1 - mine[step], mine[step]
                if buf.shape[where[step]] == 1:
                    raise ValueError
                got = flip(take(buf, send), step)
                buf = plus(take(buf, keep), got)
            buf = buf.reshape(2, 2, part // 8, cols)
            buf = plus(buf[:, 0], zflip(buf[:, 1], 1))
            buf = upper_bits(plus(buf[0], zflip(buf[1], 2)))
            home = jnp.zeros((2, 2, 2, part // 8, cols), low)
            index = [ybit, xbit, core]
            home = put(home, buf.reshape(1, 1, 1, part // 8, cols), index)
            for step in order[::-1] + (0,):
                got = flip(take(home, index), step)
                spot = where[step] - 1
                index[spot] = 1 - index[spot]
                home = put(home, got, index)
                index[spot] = None
            return home.reshape(part, cols).astype(full)

        total_a = sum_conv(grad_a, (1, 2))
        total_b = sum_conv(grad_b, (2, 1))
        tail = total_b[:, 2 * width :]
        return (
            result.astype(low)[None],
            grad_input.astype(low)[None],
            tail[:, 0],
            jnp.concatenate([total_a, total_b[:, :width]], 1),
            tail[:, 2:5],
            total_b[:, width : 2 * width],
            tail[:, 1],
            total_gu,
            total_down,
        )

    return local


def solution(mesh):
    in_specs = (
        P("wsh", "seq", None),
        P("wsh", "seq"),
        P("wsh"),
        P("wsh", None),
        P("wsh", None),
        P("wsh", None),
        P("wsh"),
        P("wsh", None),
        P("wsh", None),
        P("wsh", "seq", None),
    )
    out_specs = (
        P("wsh", "seq", None),
        P("wsh", "seq", None),
        P("wsh"),
        P("wsh", None),
        P("wsh", None),
        P("wsh", None),
        P("wsh"),
        P("wsh", None),
        P("wsh", None),
    )
    local = build(mesh.shape["seq"], mesh.shape["wsh"])
    return jax.shard_map(local, mesh=mesh, in_specs=in_specs, out_specs=out_specs, check_vma=False)
```

```python
import functools
import jax
import jax.numpy as jnp
from jax import lax
from jax.experimental import pallas as pl
from jax.experimental.pallas import tpu as pltpu
from jax.sharding import PartitionSpec as P

low = jnp.bfloat16
full = jnp.float32
MESH = pl.DeviceIdType.MESH
epsilon = 1e-06
MIB = 1 << 20


def mirrored(index, weight):
    return index + weight - 2 * weight * ((index // weight) % 2)


class Net:
    def __init__(self, me, z, send_sems, recv_sems, local_sems):
        self.me, self.z = me, z
        self.send_sems, self.recv_sems, self.local_sems = send_sems, recv_sems, local_sems
        self.count = self.local_count = 0

    def seat(self, name):
        me, z = self.me, self.z
        return {
            "core": {"seq": mirrored(me, 1), "wsh": z},
            "x": {"seq": mirrored(me, 2), "wsh": z},
            "y": {"seq": mirrored(me, 4), "wsh": z},
            "z1": {"seq": me, "wsh": mirrored(z, 1)},
            "z2": {"seq": me, "wsh": mirrored(z, 2)},
            "z3": {"seq": me, "wsh": 3 - z},
        }[name]

    def make(self, src, dst, seat, k=None):
        if k is None:
            k = self.count
            self.count += 1
        return pltpu.make_async_remote_copy(
            src_ref=src,
            dst_ref=dst,
            send_sem=self.send_sems.at[k],
            recv_sem=self.recv_sems.at[k],
            device_id=self.seat(seat) if isinstance(seat, str) else seat,
            device_id_type=MESH,
        )

    def send(self, src, dst, seat):
        copy = self.make(src, dst, seat)
        copy.start()
        return copy

    def move(self, src, dst):
        k = self.local_count
        self.local_count += 1
        copy = pltpu.make_async_copy(src, dst, self.local_sems.at[k])
        copy.start()
        return copy


def greet(seats):
    barrier = pltpu.get_barrier_semaphore()
    for seat in seats:
        pl.semaphore_signal(barrier, inc=1, device_id=seat, device_id_type=MESH)
    pl.semaphore_wait(barrier, len(seats))


def gather_kernel(
    seq,
    x_hbm, e_hbm, starts_ref, small_ref, win_hbm, wout_hbm, wgu_hbm, wdn_hbm,
    wc_out, wgu_out, wdn_out, e_out, h2_out, proj_out, first_out, zed_out, gext_out, small_out,
    wc, winf, woutf, wguf, wdnf, wgu_own, wdn_own, x_ref, h_ref, proj, gext, zed, first, h2, small_all,
    send_sems, recv_sems, local_sems,
):
    me, z = lax.axis_index("seq"), lax.axis_index("wsh")
    net = Net(me, z, send_sems, recv_sems, local_sems)
    core, xbit, ybit = me % 2, (me // 2) % 2, (me // 4) % 2
    quarter = me % 4
    rows, width = x_hbm.shape
    part = width // 4
    hq = wdn_hbm.shape[0]
    hidden = 4 * hq
    half = part // 2
    z1, z2, z3 = mirrored(z, 1), mirrored(z, 2), 3 - z
    after = {"seq": lax.rem(me + 1, seq), "wsh": z}
    before = {"seq": lax.rem(me + seq - 1, seq), "wsh": z}

    load_wout = net.move(wout_hbm, woutf)
    load_win = net.move(win_hbm, winf)
    load_x = net.move(x_hbm, x_ref.at[pl.ds(16, rows)])
    gate_at = pl.multiple_of(quarter * hq, 128)
    up_at = pl.multiple_of(hidden + quarter * hq, 128)
    load_gate = net.move(wgu_hbm.at[:, pl.ds(gate_at, hq)], wguf.at[:, pl.ds(0, hq)])
    load_up = net.move(wgu_hbm.at[:, pl.ds(up_at, hq)], wguf.at[:, pl.ds(hq, hq)])
    load_dn = net.move(wdn_hbm, wdnf)
    keep_e = net.move(e_hbm, e_out.at[0])

    greet([net.seat(n) for n in ("core", "x", "y", "z1", "z2", "z3")] + [before])

    small_all[z] = small_ref[...]
    smalls = [net.send(small_ref, small_all.at[z], n) for n in ("z1", "z2", "z3")]
    halo = net.send(x_hbm.at[pl.ds(rows - 16, 16)], x_ref.at[pl.ds(0, 16)], after)

    load_win.wait()
    load_wout.wait()
    piece = part // 8

    def cast_block(i, carry):
        at = pl.ds(pl.multiple_of(i * piece, piece), piece)
        wc[z, i // 2, i % 2, :, : 3 * width] = winf[at].astype(low)
        wc[z, i // 2, i % 2, :, 3 * width :] = woutf[at].astype(low)
        return carry

    lax.fori_loop(0, 8, cast_block, 0)
    spot = ybit * 2 + xbit
    spot_x = ybit * 2 + 1 - xbit
    spot_y = (1 - ybit) * 2 + xbit
    cols = [pl.ds(0, 2 * width), pl.ds(2 * width, 2 * width)]

    def own(zz):
        return wc.at[zz, spot, core]

    a1 = net.send(own(z), own(z), "z1")
    a2 = net.send(own(z), own(z), "z2")

    load_gate.wait()
    load_up.wait()
    wgu_own[...] = wguf[...].astype(low)
    keep_gu = net.move(wgu_own, wgu_out.at[z])
    load_dn.wait()
    cast_rows = hq // 4

    def cast_dn(i, carry):
        at = pl.ds(pl.multiple_of(i * cast_rows, cast_rows), cast_rows)
        wdn_own[at] = wdnf[at].astype(low)
        return carry

    lax.fori_loop(0, 4, cast_dn, 0)

    def spread(zz):
        bx = net.send(own(zz), own(zz), "x")
        by = net.send(own(zz), own(zz), "y")
        return bx, by

    def onward(zz, b):
        bx, by = b
        bx.wait_recv()
        d0 = net.send(wc.at[zz, spot_x, core, :, cols[0]], wc.at[zz, spot_x, core, :, cols[0]], "y")
        by.wait_recv()
        d1 = net.send(wc.at[zz, spot_y, core, :, cols[1]], wc.at[zz, spot_y, core, :, cols[1]], "x")
        return d0, d1

    def across(zz, d):
        d[0].wait_recv()
        d[1].wait_recv()
        return net.send(wc.at[zz, :, core], wc.at[zz, :, core], "core")

    a1.wait_recv()
    b1 = spread(z1)
    a2.wait_recv()
    a3 = net.send(own(z2), own(z2), "z1")
    b2 = spread(z2)

    def gu(zz, yy):
        return wgu_out.at[zz, pl.ds(pl.multiple_of(yy * half, half), half)]

    gu_own = wgu_own.at[pl.ds(pl.multiple_of(ybit * half, half), half)]
    f1 = net.send(gu_own, gu(z, ybit), "z1")
    f2 = net.send(gu_own, gu(z, ybit), "z2")
    d1 = onward(z1, b1)
    d2 = onward(z2, b2)
    a3.wait_recv()
    b3 = spread(z3)
    same0 = (z % 2) == (quarter % 2)
    same1 = (z // 2) == (quarter // 2)
    holder = same0 & same1
    dn_own = wdn_own.at[pl.ds(pl.multiple_of(ybit * (hq // 2), 32), hq // 2)]
    dn_spot = wdn_out.at[ybit]
    dn2 = net.make(dn_own, dn_spot, "z2")
    dn1a = net.make(dn_own, dn_spot, "z1")
    dn1b = net.make(dn_spot, dn_spot, "z1", net.count - 1)
    dny = net.make(dn_spot, dn_spot, "y")
    keep_dn = [
        pltpu.make_async_copy(
            wdn_own.at[pl.ds(i * (hq // 2), hq // 2)], wdn_out.at[i], local_sems.at[18 + i]
        )
        for i in range(2)
    ]

    @pl.when(holder)
    def _():
        dn2.start()
        dn1a.start()
        for copy in keep_dn:
            copy.start()

    ex = net.send(e_hbm, e_out.at[1], "x")
    ec = net.send(e_hbm, e_out.at[2], "core")
    c1 = across(z1, d1)
    c2 = across(z2, d2)
    d3 = onward(z3, b3)
    f1.wait_recv()
    g1 = net.send(gu(z1, ybit), gu(z1, ybit), "y")
    c3 = across(z3, d3)
    f2.wait_recv()
    f3 = net.send(gu(z2, ybit), gu(z2, ybit), "z1")
    g2 = net.send(gu(z2, ybit), gu(z2, ybit), "y")

    for s in smalls:
        s.wait_recv()
    load_x.wait()
    halo.wait_recv()

    def row_of(k):
        return jnp.concatenate([small_all[i, k : k + 1, :] for i in range(4)], 1).astype(full)

    gain_one, gain_two = row_of(0), row_of(1)

    def norm_one(i, carry):
        at = pl.ds(pl.multiple_of(i * 176, 16), 176)
        xf = x_ref[at].astype(full)
        rate = lax.rsqrt(jnp.mean(xf * xf, axis=-1, keepdims=True) + epsilon)
        h_ref[at] = (xf * rate * gain_one).astype(low)
        return carry

    lax.fori_loop(0, (rows + 16) // 176, norm_one, 0)
    for c in (c1, c2, c3):
        c.wait_recv()

    def project(i, carry):
        at = pl.ds(pl.multiple_of(i * 512, 512), 512)
        proj[:, at] = jnp.dot(
            h_ref[...], wc[:, :, :, :, at].reshape(width, 512), preferred_element_type=full
        )
        return carry

    lax.fori_loop(0, 6, project, 0)
    keep_wc = net.move(wc, wc_out)
    keep_proj = net.move(proj.at[pl.ds(16, rows)], proj_out)

    place = me * rows + lax.broadcasted_iota(jnp.int32, (rows, 1), 0)
    starts = starts_ref[...]
    keep_one = (place - 1 >= starts).astype(full)
    keep_two = (place - 2 >= starts).astype(full)
    cw = 128

    def mix(i, carry):
        at = pl.ds(pl.multiple_of(i * cw, cw), cw)
        xat = pl.ds(pl.multiple_of(2 * width + i * cw, cw), cw)
        cat = pl.ds(pl.multiple_of(width + i * cw, cw), cw)
        gext[:, at] = (proj[:, at] * proj[:, xat]).astype(low).astype(full)
        zi = i // (part // cw)
        inside = pl.ds(pl.multiple_of((i % (part // cw)) * cw, cw), cw)
        taps = small_all[zi, :, inside].astype(full)
        mixed = (
            taps[2:3] * gext[16:, at]
            + keep_one * taps[3:4] * gext[15 : rows + 15, at]
            + keep_two * taps[4:5] * gext[14 : rows + 14, at]
        )
        zed[:, at] = (proj[16:, cat] * mixed).astype(low)
        return carry

    lax.fori_loop(0, width // cw, mix, 0)
    keep_zed = net.move(zed, zed_out)
    keep_gext = net.move(gext, gext_out)

    def project_out(i, carry):
        at = pl.ds(pl.multiple_of(i * 512, 512), 512)
        wat = pl.ds(pl.multiple_of(3 * width + i * 512, 512), 512)
        first[:, at] = x_ref[16:, at].astype(full) + jnp.dot(
            zed[...], wc[:, :, :, :, wat].reshape(width, 512), preferred_element_type=full
        )
        return carry

    lax.fori_loop(0, 2, project_out, 0)
    keep_first = net.move(first, first_out)

    def norm_two(i, carry):
        at = pl.ds(pl.multiple_of(i * 128, 128), 128)
        xf = first[at]
        rate = lax.rsqrt(jnp.mean(xf * xf, axis=-1, keepdims=True) + epsilon)
        h2[at] = (xf * rate * gain_two).astype(low)
        return carry

    lax.fori_loop(0, rows // 128, norm_two, 0)
    keep_h2 = net.move(h2, h2_out.at[0])
    hx = net.send(h2, h2_out.at[1], "x")
    hc = net.send(h2, h2_out.at[2], "core")
    keep_small = net.move(small_all, small_out)

    ex.wait_recv()
    exc = net.send(e_out.at[1], e_out.at[3], "core")

    @pl.when(same0 & ~same1)
    def _():
        dn2.wait_recv()
        dn1b.start()
        dny.start()

    f3.wait_recv()
    g3 = net.send(gu(z3, ybit), gu(z3, ybit), "y")

    @pl.when(~same0)
    def _():
        dn1a.wait_recv()
        dny.start()

    hx.wait_recv()
    hxc = net.send(h2_out.at[1], h2_out.at[3], "core")
    for c in (g1, g2, g3, ec, exc, hc, hxc):
        c.wait_recv()

    @pl.when(~holder)
    def _():
        dny.wait()

    @pl.when(holder)
    def _():
        dn2.wait_send()
        dn1a.wait_send()
        for copy in keep_dn:
            copy.wait()

    @pl.when(same0 & ~same1)
    def _():
        dn1b.wait_send()

    for c in (
        *smalls, halo, a1, a2, a3, *b1, *b2, *b3, *d1, *d2, *d3, c1, c2, c3,
        f1, f2, f3, g1, g2, g3, ex, ec, exc, hx, hc, hxc,
    ):
        c.wait_send()
    for c in (keep_e, keep_gu, keep_wc, keep_proj, keep_zed, keep_gext, keep_first, keep_h2, keep_small):
        c.wait()


def gather(seq, x, e, starts, small, win, wout, wgu, wdn):
    rows, width = x.shape
    part = width // 4
    hq = wdn.shape[0]
    shape = jax.ShapeDtypeStruct
    anyspace = pl.BlockSpec(memory_space=pl.ANY)
    vmem = pl.BlockSpec(memory_space=pltpu.VMEM)
    conv = (4, 4, 2, part // 8, 4 * width)
    outs = [
        shape(conv, low),
        shape((4, part, 2 * hq), low),
        shape((2, hq // 2, width), low),
        shape((4, rows, width), low),
        shape((4, rows, width), low),
        shape((rows, 3 * width), full),
        shape((rows, width), full),
        shape((rows, width), low),
        shape((rows + 16, width), full),
        shape((4, 16, part), low),
    ]
    scratch = [
        pltpu.VMEM(conv, low),
        pltpu.VMEM((part, 3 * width), full),
        pltpu.VMEM((part, width), full),
        pltpu.VMEM((part, 2 * hq), full),
        pltpu.VMEM((hq, width), full),
        pltpu.VMEM((part, 2 * hq), low),
        pltpu.VMEM((hq, width), low),
        pltpu.VMEM((rows + 16, width), low),
        pltpu.VMEM((rows + 16, width), low),
        pltpu.VMEM((rows + 16, 3 * width), full),
        pltpu.VMEM((rows + 16, width), full),
        pltpu.VMEM((rows, width), low),
        pltpu.VMEM((rows, width), full),
        pltpu.VMEM((rows, width), low),
        pltpu.VMEM((4, 16, part), low),
        pltpu.SemaphoreType.DMA((48,)),
        pltpu.SemaphoreType.DMA((48,)),
        pltpu.SemaphoreType.DMA((20,)),
    ]
    return pl.pallas_call(
        functools.partial(gather_kernel, seq),
        out_shape=outs,
        in_specs=[anyspace, anyspace, vmem, vmem] + [anyspace] * 4,
        out_specs=[anyspace] * len(outs),
        scratch_shapes=scratch,
        compiler_params=pltpu.CompilerParams(
            collective_id=0, has_side_effects=True, vmem_limit_bytes=56 * MIB
        ),
        name="gather",
    )(x, e, starts, small, win, wout, wgu, wdn)


def inner(left, right):
    return lax.dot_general(left, right, (((0,), (0,)), ((), ())), preferred_element_type=full)


def outer(left, right):
    return lax.dot_general(left, right, (((1,), (1,)), ((), ())), preferred_element_type=full)


def plain(left, right):
    return jnp.dot(left, right, preferred_element_type=full)


def build(seq, wsh):
    def flip(value, bit):
        return lax.ppermute(value, "seq", [(i, i ^ (1 << bit)) for i in range(seq)])

    def zflip(value, mask):
        return lax.ppermute(value, "wsh", [(i, i ^ mask) for i in range(wsh)])

    def chosen(value, pairs):
        return lax.ppermute(
            value, ("seq", "wsh"), [(a * wsh + b, c * wsh + d) for (a, b), (c, d) in pairs]
        )

    def take(buf, at):
        start, size = [], []
        for dim in range(buf.ndim):
            index = at[dim] if dim < len(at) else None
            start.append(0 if index is None else index)
            size.append(buf.shape[dim] if index is None else 1)
        return lax.dynamic_slice(buf, start, size)

    def put(buf, value, at):
        start = [
            0 if dim >= len(at) or at[dim] is None else at[dim] for dim in range(buf.ndim)
        ]
        return lax.dynamic_update_slice(buf, value, start)

    def local(
        tokens,
        doc_start,
        norm1_gain,
        in_weight,
        conv_weight,
        out_weight,
        norm2_gain,
        gate_up_weight,
        down_weight,
        out_grad,
    ):
        me = lax.axis_index("seq")
        z = lax.axis_index("wsh")
        core, xbit, ybit = me % 2, (me // 2) % 2, (me // 4) % 2
        quarter = me % 4
        cot = out_grad[0]
        rows, width = cot.shape
        part = width // wsh
        hidden = down_weight.shape[0] * wsh
        hq = hidden // 4

        def by_z(value):
            return jnp.concatenate(
                [lax.dynamic_slice_in_dim(value, (z ^ j) * part, part, 1) for j in range(wsh)], 1
            )

        small = jnp.concatenate(
            [norm1_gain[None], norm2_gain[None], conv_weight.T], 0
        ).astype(low)
        small = jnp.pad(small, ((0, 16 - small.shape[0]), (0, 0)))
        w_c, w_gu, w_down, cot_all, second_all, proj, first, zed, gext, small_all = gather(
            seq, tokens[0], cot, doc_start.T, small, in_weight, out_weight, gate_up_weight, down_weight
        )
        w_c = w_c.reshape(width, 4 * width)
        w_gu = w_gu.reshape(width, 2 * hq)
        w_down = w_down.reshape(hq, width)
        cot_all = cot_all.reshape(4 * rows, width)
        second_all = second_all.reshape(4 * rows, width)
        w_a, w_x, w_out = w_c[:, : 2 * width], w_c[:, 2 * width : 3 * width], w_c[:, 3 * width :]
        vec = jnp.concatenate([small_all[i] for i in range(4)], 1).astype(full)
        gain_one, gain_two = vec[0:1], vec[1:2]
        taps = [vec[k : k + 1] for k in (2, 3, 4)]
        xf = tokens[0].astype(full)
        starts = doc_start[0]
        rate_one = lax.rsqrt(jnp.mean(xf * xf, axis=-1, keepdims=True) + epsilon)
        normed = xf * rate_one
        h = (normed * gain_one).astype(low)
        bpart, cpart, xpart = proj[:, :width], proj[:, width : 2 * width], proj[:, 2 * width :]
        place = me * rows + jnp.arange(rows, dtype=jnp.int32)
        keep_one = (place - 1 >= starts).astype(full)[:, None]
        keep_two = (place - 2 >= starts).astype(full)[:, None]
        current, lag_one, lag_two = gext[16:], gext[15 : rows + 15], gext[14 : rows + 14]
        mixed = taps[0] * current + keep_one * taps[1] * lag_one + keep_two * taps[2] * lag_two
        rate_two = lax.rsqrt(jnp.mean(first * first, axis=-1, keepdims=True) + epsilon)
        normed_two = first * rate_two

        both = plain(second_all, w_gu)
        gate, upper = both[:, :hq], both[:, hq:]
        sigma = jax.nn.sigmoid(gate)
        swish = gate * sigma
        act = (swish * upper).astype(low)
        grad_act = outer(cot_all, w_down)
        grad_gate = grad_act * upper * (sigma * (1.0 + gate * (1.0 - sigma)))
        grad_both = jnp.concatenate([grad_gate, grad_act * swish], 1).astype(low)

        def scatter_group(value):
            mine, theirs = value[: 2 * rows], value[2 * rows :]
            mine = mine + flip(theirs.astype(low), 0).astype(full)
            return mine[:rows] + flip(mine[rows:].astype(low), 1).astype(full)

        result = first + scatter_group(plain(act, w_down))
        grad_second = scatter_group(outer(grad_both, w_gu))
        grad_down = inner(act, cot_all).astype(low)
        grad_gu = inner(by_z(second_all), grad_both).astype(low)

        def plus(a, b):
            return (a.astype(full) + b.astype(full)).astype(low)

        def upper_bits(value):
            for bit in range(3, seq.bit_length() - 1):
                value = plus(value, flip(value, bit))
            return value

        buf = grad_gu.reshape(4, 2, part // 2, 2 * hq)
        buf = plus(take(buf, (None, ybit)), flip(take(buf, (None, 1 - ybit)), 2))
        buf = buf.reshape(2, 2, part // 2, 2 * hq)
        buf = plus(buf[:, 0], zflip(buf[:, 1], 1))
        buf = upper_bits(plus(buf[0], zflip(buf[1], 2)))

        def spread_gu(piece, order):
            home = jnp.zeros((2, 2, 2, part // 2, hq), low)
            index = [xbit, core, ybit]
            home = put(home, piece.reshape(1, 1, 1, part // 2, hq), index)
            for step in order:
                got = flip(take(home, index), step)
                spot = {1: 0, 0: 1, 2: 2}[step]
                index[spot] = 1 - index[spot]
                home = put(home, got, index)
                index[spot] = None
            home = home.reshape(4, part, hq)
            return jnp.concatenate([home[i] for i in range(4)], 1)

        total_gu = jnp.concatenate(
            [spread_gu(buf[:, :hq], (1, 2, 0)), spread_gu(buf[:, hq:], (2, 1, 0))], 1
        ).astype(full)

        buf = grad_down.reshape(2, hq // 2, width)
        half = plus(take(buf, (ybit,)), flip(take(buf, (1 - ybit,)), 2))
        half = plus(
            half,
            chosen(
                half, [((s, s % 4 ^ m ^ 1), (s, s % 4 ^ m)) for s in range(seq) for m in (0, 2)]
            ),
        )
        half = plus(half, chosen(half, [((s, s % 4 ^ 2), (s, s % 4)) for s in range(seq)]))
        half = upper_bits(half)
        got = chosen(half, [((s, s % 4), (s ^ 2, s % 4)) for s in range(seq)])
        half = jnp.where(quarter == z, half, got)
        evens = [(s, b) for s in range(seq) for b in range(wsh) if (s ^ b) % 2 == 0]
        other = chosen(half, [((s, b), (s ^ 4, b)) for s, b in evens])
        home = put(put(jnp.zeros((2, hq // 2, width), low), half, (ybit,)), other, (1 - ybit,))
        got = chosen(home, [((s, b), (s ^ 1, b)) for s, b in evens])
        total_down = jnp.where((me ^ z) % 2 == 0, home, got).reshape(hq, width).astype(full)

        grad_gain_two = jnp.sum(grad_second * normed_two, axis=0)
        scaled_two = grad_second * gain_two
        grad_first = cot.astype(full) + rate_two * (
            scaled_two - normed_two * jnp.mean(scaled_two * normed_two, axis=-1, keepdims=True)
        )
        grad_branch = grad_first.astype(low)
        grad_outw = inner(by_z(zed), grad_branch)
        grad_zed = outer(grad_branch, w_out)
        grad_cpart = grad_zed * mixed
        grad_mixed = grad_zed * cpart
        term_one = keep_one * grad_mixed
        term_two = keep_two * grad_mixed
        grad_taps = [
            jnp.sum(grad_mixed * current, axis=0),
            jnp.sum(term_one * lag_one, axis=0),
            jnp.sum(term_two * lag_two, axis=0),
        ]
        grad_ext = jnp.pad(taps[0] * grad_mixed, ((2, 0), (0, 0)))
        grad_ext = grad_ext + jnp.pad(taps[1] * term_one, ((1, 1), (0, 0)))
        grad_ext = grad_ext + jnp.pad(taps[2] * term_two, ((0, 2), (0, 0)))
        returned = lax.ppermute(grad_ext[:2], "seq", [(i + 1, i) for i in range(seq - 1)])
        grad_gated = grad_ext[2:] + jnp.pad(returned, ((rows - 2, 0), (0, 0)))
        grad_proj = jnp.concatenate(
            [grad_gated * xpart, grad_cpart, grad_gated * bpart], 1
        ).astype(low)
        hz = by_z(h)
        grad_a = inner(hz, grad_proj[:, : 2 * width]).astype(low)
        grad_x = inner(hz, grad_proj[:, 2 * width :])
        grad_normed = outer(grad_proj[:, : 2 * width], w_a) + outer(
            grad_proj[:, 2 * width :], w_x
        )
        grad_gain_one = jnp.sum(grad_normed * normed, axis=0)
        scaled_one = grad_normed * gain_one
        grad_input = grad_first + rate_one * (
            scaled_one - normed * jnp.mean(scaled_one * normed, axis=-1, keepdims=True)
        )
        tail = jnp.stack(
            [by_z(g[None])[0] for g in [grad_gain_one, grad_gain_two] + grad_taps], 1
        )
        tail = jnp.pad(tail, ((0, 0), (0, 128 - tail.shape[1])))
        grad_b = jnp.concatenate([grad_x, grad_outw, tail], 1).astype(low)

        def sum_conv(value, order):
            cols = value.shape[1]
            where = {2: 1, 1: 2, 0: 3}
            buf = value.reshape(4, 2, 2, 2, part // 8, cols)
            mine = {2: ybit, 1: xbit, 0: core}
            for step in (0,) + order:
                send, keep = [None] * 4, [None] * 4
                send[where[step]], keep[where[step]] = 1 - mine[step], mine[step]
                if buf.shape[where[step]] == 1:
                    raise ValueError
                got = flip(take(buf, send), step)
                buf = plus(take(buf, keep), got)
            buf = buf.reshape(2, 2, part // 8, cols)
            buf = plus(buf[:, 0], zflip(buf[:, 1], 1))
            buf = upper_bits(plus(buf[0], zflip(buf[1], 2)))
            home = jnp.zeros((2, 2, 2, part // 8, cols), low)
            index = [ybit, xbit, core]
            home = put(home, buf.reshape(1, 1, 1, part // 8, cols), index)
            for step in order[::-1] + (0,):
                got = flip(take(home, index), step)
                spot = where[step] - 1
                index[spot] = 1 - index[spot]
                home = put(home, got, index)
                index[spot] = None
            return home.reshape(part, cols).astype(full)

        total_a = sum_conv(grad_a, (1, 2))
        total_b = sum_conv(grad_b, (2, 1))
        tail = total_b[:, 2 * width :]
        return (
            result.astype(low)[None],
            grad_input.astype(low)[None],
            tail[:, 0],
            jnp.concatenate([total_a, total_b[:, :width]], 1),
            tail[:, 2:5],
            total_b[:, width : 2 * width],
            tail[:, 1],
            total_gu,
            total_down,
        )

    return local


def solution(mesh):
    in_specs = (
        P("wsh", "seq", None),
        P("wsh", "seq"),
        P("wsh"),
        P("wsh", None),
        P("wsh", None),
        P("wsh", None),
        P("wsh"),
        P("wsh", None),
        P("wsh", None),
        P("wsh", "seq", None),
    )
    out_specs = (
        P("wsh", "seq", None),
        P("wsh", "seq", None),
        P("wsh"),
        P("wsh", None),
        P("wsh", None),
        P("wsh", None),
        P("wsh"),
        P("wsh", None),
        P("wsh", None),
    )
    local = build(mesh.shape["seq"], mesh.shape["wsh"])
    return jax.shard_map(local, mesh=mesh, in_specs=in_specs, out_specs=out_specs, check_vma=False)
```

```python
import functools
import jax
import jax.numpy as jnp
from jax import lax
from jax.experimental import pallas as pl
from jax.experimental.pallas import tpu as pltpu
from jax.sharding import PartitionSpec as P

low = jnp.bfloat16
full = jnp.float32
MESH = pl.DeviceIdType.MESH
epsilon = 1e-06
MIB = 1 << 20


def mirrored(index, weight):
    return index + weight - 2 * weight * ((index // weight) % 2)


class Net:
    def __init__(self, me, z, send_sems, recv_sems, local_sems):
        self.me, self.z = me, z
        self.send_sems, self.recv_sems, self.local_sems = send_sems, recv_sems, local_sems
        self.count = self.local_count = 0

    def seat(self, name):
        me, z = self.me, self.z
        return {
            "core": {"seq": mirrored(me, 1), "wsh": z},
            "x": {"seq": mirrored(me, 2), "wsh": z},
            "y": {"seq": mirrored(me, 4), "wsh": z},
            "z1": {"seq": me, "wsh": mirrored(z, 1)},
            "z2": {"seq": me, "wsh": mirrored(z, 2)},
            "z3": {"seq": me, "wsh": 3 - z},
        }[name]

    def make(self, src, dst, seat, k=None):
        if k is None:
            k = self.count
            self.count += 1
        return pltpu.make_async_remote_copy(
            src_ref=src,
            dst_ref=dst,
            send_sem=self.send_sems.at[k],
            recv_sem=self.recv_sems.at[k],
            device_id=self.seat(seat) if isinstance(seat, str) else seat,
            device_id_type=MESH,
        )

    def send(self, src, dst, seat):
        copy = self.make(src, dst, seat)
        copy.start()
        return copy

    def move(self, src, dst):
        k = self.local_count
        self.local_count += 1
        copy = pltpu.make_async_copy(src, dst, self.local_sems.at[k])
        copy.start()
        return copy


def greet(seats):
    barrier = pltpu.get_barrier_semaphore()
    for seat in seats:
        pl.semaphore_signal(barrier, inc=1, device_id=seat, device_id_type=MESH)
    pl.semaphore_wait(barrier, len(seats))


def inner(left, right):
    return lax.dot_general(left, right, (((0,), (0,)), ((), ())), preferred_element_type=full)


def outer(left, right):
    return lax.dot_general(left, right, (((1,), (1,)), ((), ())), preferred_element_type=full)


def chunk_sizes(hq):
    chunk = hq // 3
    return chunk, 2 * chunk


def gather_kernel(
    seq,
    x_hbm, e_hbm, starts_ref, small_ref, win_hbm, wout_hbm, wgu_hbm, wdn_hbm,
    wc_out, wgu_out, wdn_out, e_out, h2_out, proj_out, first_out, zed_out, gext_out, small_out,
    wc, winf, woutf, wguf, wdnf, wgu_own, wdn_own, x_ref, h_ref, proj, gext, zed, first, h2, small_all,
    send_sems, recv_sems, local_sems,
):
    me, z = lax.axis_index("seq"), lax.axis_index("wsh")
    net = Net(me, z, send_sems, recv_sems, local_sems)
    core, xbit, ybit = me % 2, (me // 2) % 2, (me // 4) % 2
    quarter = me % 4
    rows, width = x_hbm.shape
    part = width // 4
    hq = wdn_hbm.shape[0]
    hidden = 4 * hq
    half = part // 2
    z1, z2, z3 = mirrored(z, 1), mirrored(z, 2), 3 - z
    after = {"seq": lax.rem(me + 1, seq), "wsh": z}
    before = {"seq": lax.rem(me + seq - 1, seq), "wsh": z}

    load_wout = net.move(wout_hbm, woutf)
    load_win = net.move(win_hbm, winf)
    load_x = net.move(x_hbm, x_ref.at[pl.ds(16, rows)])
    chunk, pair = chunk_sizes(hq)
    load_gu = []
    for k in range(3):
        for base, shift in ((quarter * hq, 0), (hidden + quarter * hq, chunk)):
            cut = pl.ds(pl.multiple_of(base + k * chunk, 128), chunk)
            load_gu.append(
                net.move(wgu_hbm.at[:, cut], wguf.at[:, pl.ds(k * pair + shift, chunk)])
            )
    load_dn = net.move(wdn_hbm, wdnf)
    keep_e = net.move(e_hbm, e_out.at[0])

    greet([net.seat(n) for n in ("core", "x", "y", "z1", "z2", "z3")] + [before])

    small_all[z] = small_ref[...]
    smalls = [net.send(small_ref, small_all.at[z], n) for n in ("z1", "z2", "z3")]
    halo = net.send(x_hbm.at[pl.ds(rows - 16, 16)], x_ref.at[pl.ds(0, 16)], after)

    load_win.wait()
    load_wout.wait()
    piece = part // 8

    def cast_block(i, carry):
        at = pl.ds(pl.multiple_of(i * piece, piece), piece)
        wc[z, i // 2, i % 2, :, : 3 * width] = winf[at].astype(low)
        wc[z, i // 2, i % 2, :, 3 * width :] = woutf[at].astype(low)
        return carry

    lax.fori_loop(0, 8, cast_block, 0)
    spot = ybit * 2 + xbit
    spot_x = ybit * 2 + 1 - xbit
    spot_y = (1 - ybit) * 2 + xbit
    cols = [pl.ds(0, 2 * width), pl.ds(2 * width, 2 * width)]

    def own(zz):
        return wc.at[zz, spot, core]

    a1 = net.send(own(z), own(z), "z1")
    a2 = net.send(own(z), own(z), "z2")

    for copy in load_gu:
        copy.wait()
    wgu_own[...] = wguf[...].astype(low)
    keep_gu = net.move(wgu_own, wgu_out.at[z])
    load_dn.wait()
    cast_rows = hq // 4

    def cast_dn(i, carry):
        at = pl.ds(pl.multiple_of(i * cast_rows, cast_rows), cast_rows)
        wdn_own[at] = wdnf[at].astype(low)
        return carry

    lax.fori_loop(0, 4, cast_dn, 0)

    def spread(zz):
        bx = net.send(own(zz), own(zz), "x")
        by = net.send(own(zz), own(zz), "y")
        return bx, by

    def onward(zz, b):
        bx, by = b
        bx.wait_recv()
        d0 = net.send(wc.at[zz, spot_x, core, :, cols[0]], wc.at[zz, spot_x, core, :, cols[0]], "y")
        by.wait_recv()
        d1 = net.send(wc.at[zz, spot_y, core, :, cols[1]], wc.at[zz, spot_y, core, :, cols[1]], "x")
        return d0, d1

    def across(zz, d):
        d[0].wait_recv()
        d[1].wait_recv()
        return net.send(wc.at[zz, :, core], wc.at[zz, :, core], "core")

    a1.wait_recv()
    b1 = spread(z1)
    a2.wait_recv()
    a3 = net.send(own(z2), own(z2), "z1")
    b2 = spread(z2)

    def gu(zz, yy):
        return wgu_out.at[zz, pl.ds(pl.multiple_of(yy * half, half), half)]

    gu_own = wgu_own.at[pl.ds(pl.multiple_of(ybit * half, half), half)]
    f1 = net.send(gu_own, gu(z, ybit), "z1")
    f2 = net.send(gu_own, gu(z, ybit), "z2")
    d1 = onward(z1, b1)
    d2 = onward(z2, b2)
    a3.wait_recv()
    b3 = spread(z3)
    same0 = (z % 2) == (quarter % 2)
    same1 = (z // 2) == (quarter // 2)
    holder = same0 & same1
    dn_own = wdn_own.at[pl.ds(pl.multiple_of(ybit * (hq // 2), 32), hq // 2)]
    dn_spot = wdn_out.at[ybit]
    dn2 = net.make(dn_own, dn_spot, "z2")
    dn1a = net.make(dn_own, dn_spot, "z1")
    dn1b = net.make(dn_spot, dn_spot, "z1", net.count - 1)
    dny = net.make(dn_spot, dn_spot, "y")
    keep_dn = [
        pltpu.make_async_copy(
            wdn_own.at[pl.ds(i * (hq // 2), hq // 2)], wdn_out.at[i], local_sems.at[24 + i]
        )
        for i in range(2)
    ]

    @pl.when(holder)
    def _():
        dn2.start()
        dn1a.start()
        for copy in keep_dn:
            copy.start()

    ex = net.send(e_hbm, e_out.at[1], "x")
    ec = net.send(e_hbm, e_out.at[2], "core")
    c1 = across(z1, d1)
    c2 = across(z2, d2)
    d3 = onward(z3, b3)
    f1.wait_recv()
    g1 = net.send(gu(z1, ybit), gu(z1, ybit), "y")
    c3 = across(z3, d3)
    f2.wait_recv()
    f3 = net.send(gu(z2, ybit), gu(z2, ybit), "z1")
    g2 = net.send(gu(z2, ybit), gu(z2, ybit), "y")

    for s in smalls:
        s.wait_recv()
    load_x.wait()
    halo.wait_recv()

    def row_of(k):
        return jnp.concatenate([small_all[i, k : k + 1, :] for i in range(4)], 1).astype(full)

    gain_one, gain_two = row_of(0), row_of(1)

    def norm_one(i, carry):
        at = pl.ds(pl.multiple_of(i * 176, 16), 176)
        xf = x_ref[at].astype(full)
        rate = lax.rsqrt(jnp.mean(xf * xf, axis=-1, keepdims=True) + epsilon)
        h_ref[at] = (xf * rate * gain_one).astype(low)
        return carry

    lax.fori_loop(0, (rows + 16) // 176, norm_one, 0)
    for c in (c1, c2, c3):
        c.wait_recv()

    def project(i, carry):
        at = pl.ds(pl.multiple_of(i * 512, 512), 512)
        proj[:, at] = jnp.dot(
            h_ref[...], wc[:, :, :, :, at].reshape(width, 512), preferred_element_type=full
        )
        return carry

    lax.fori_loop(0, 6, project, 0)
    keep_wc = net.move(wc, wc_out)
    keep_proj = net.move(proj.at[pl.ds(16, rows)], proj_out)

    place = me * rows + lax.broadcasted_iota(jnp.int32, (rows, 1), 0)
    starts = starts_ref[...]
    keep_one = (place - 1 >= starts).astype(full)
    keep_two = (place - 2 >= starts).astype(full)
    cw = 128

    def mix(i, carry):
        at = pl.ds(pl.multiple_of(i * cw, cw), cw)
        xat = pl.ds(pl.multiple_of(2 * width + i * cw, cw), cw)
        cat = pl.ds(pl.multiple_of(width + i * cw, cw), cw)
        gext[:, at] = (proj[:, at] * proj[:, xat]).astype(low).astype(full)
        zi = i // (part // cw)
        inside = pl.ds(pl.multiple_of((i % (part // cw)) * cw, cw), cw)
        taps = small_all[zi, :, inside].astype(full)
        mixed = (
            taps[2:3] * gext[16:, at]
            + keep_one * taps[3:4] * gext[15 : rows + 15, at]
            + keep_two * taps[4:5] * gext[14 : rows + 14, at]
        )
        zed[:, at] = (proj[16:, cat] * mixed).astype(low)
        return carry

    lax.fori_loop(0, width // cw, mix, 0)
    keep_zed = net.move(zed, zed_out)
    keep_gext = net.move(gext, gext_out)

    def project_out(i, carry):
        at = pl.ds(pl.multiple_of(i * 512, 512), 512)
        wat = pl.ds(pl.multiple_of(3 * width + i * 512, 512), 512)
        first[:, at] = x_ref[16:, at].astype(full) + jnp.dot(
            zed[...], wc[:, :, :, :, wat].reshape(width, 512), preferred_element_type=full
        )
        return carry

    lax.fori_loop(0, 2, project_out, 0)
    keep_first = net.move(first, first_out)

    def norm_two(i, carry):
        at = pl.ds(pl.multiple_of(i * 128, 128), 128)
        xf = first[at]
        rate = lax.rsqrt(jnp.mean(xf * xf, axis=-1, keepdims=True) + epsilon)
        h2[at] = (xf * rate * gain_two).astype(low)
        return carry

    lax.fori_loop(0, rows // 128, norm_two, 0)
    keep_h2 = net.move(h2, h2_out.at[0])
    hx = net.send(h2, h2_out.at[1], "x")
    hc = net.send(h2, h2_out.at[2], "core")
    keep_small = net.move(small_all, small_out)

    ex.wait_recv()
    exc = net.send(e_out.at[1], e_out.at[3], "core")

    @pl.when(same0 & ~same1)
    def _():
        dn2.wait_recv()
        dn1b.start()
        dny.start()

    f3.wait_recv()
    g3 = net.send(gu(z3, ybit), gu(z3, ybit), "y")

    @pl.when(~same0)
    def _():
        dn1a.wait_recv()
        dny.start()

    hx.wait_recv()
    hxc = net.send(h2_out.at[1], h2_out.at[3], "core")
    for c in (g1, g2, g3, ec, exc, hc, hxc):
        c.wait_recv()

    @pl.when(~holder)
    def _():
        dny.wait()

    @pl.when(holder)
    def _():
        dn2.wait_send()
        dn1a.wait_send()
        for copy in keep_dn:
            copy.wait()

    @pl.when(same0 & ~same1)
    def _():
        dn1b.wait_send()

    for c in (
        *smalls, halo, a1, a2, a3, *b1, *b2, *b3, *d1, *d2, *d3, c1, c2, c3,
        f1, f2, f3, g1, g2, g3, ex, ec, exc, hx, hc, hxc,
    ):
        c.wait_send()
    for c in (keep_e, keep_gu, keep_wc, keep_proj, keep_zed, keep_gext, keep_first, keep_h2, keep_small):
        c.wait()


def gather(seq, x, e, starts, small, win, wout, wgu, wdn):
    rows, width = x.shape
    part = width // 4
    hq = wdn.shape[0]
    shape = jax.ShapeDtypeStruct
    anyspace = pl.BlockSpec(memory_space=pl.ANY)
    vmem = pl.BlockSpec(memory_space=pltpu.VMEM)
    conv = (4, 4, 2, part // 8, 4 * width)
    outs = [
        shape(conv, low),
        shape((4, part, 2 * hq), low),
        shape((2, hq // 2, width), low),
        shape((4, rows, width), low),
        shape((4, rows, width), low),
        shape((rows, 3 * width), full),
        shape((rows, width), full),
        shape((rows, width), low),
        shape((rows + 16, width), full),
        shape((4, 16, part), low),
    ]
    scratch = [
        pltpu.VMEM(conv, low),
        pltpu.VMEM((part, 3 * width), full),
        pltpu.VMEM((part, width), full),
        pltpu.VMEM((part, 2 * hq), full),
        pltpu.VMEM((hq, width), full),
        pltpu.VMEM((part, 2 * hq), low),
        pltpu.VMEM((hq, width), low),
        pltpu.VMEM((rows + 16, width), low),
        pltpu.VMEM((rows + 16, width), low),
        pltpu.VMEM((rows + 16, 3 * width), full),
        pltpu.VMEM((rows + 16, width), full),
        pltpu.VMEM((rows, width), low),
        pltpu.VMEM((rows, width), full),
        pltpu.VMEM((rows, width), low),
        pltpu.VMEM((4, 16, part), low),
        pltpu.SemaphoreType.DMA((48,)),
        pltpu.SemaphoreType.DMA((48,)),
        pltpu.SemaphoreType.DMA((26,)),
    ]
    return pl.pallas_call(
        functools.partial(gather_kernel, seq),
        out_shape=outs,
        in_specs=[anyspace, anyspace, vmem, vmem] + [anyspace] * 4,
        out_specs=[anyspace] * len(outs),
        scratch_shapes=scratch,
        compiler_params=pltpu.CompilerParams(
            collective_id=0, has_side_effects=True, vmem_limit_bytes=56 * MIB
        ),
        name="gather",
    )(x, e, starts, small, win, wout, wgu, wdn)


def feed_kernel(
    seq,
    h2_hbm, e_hbm, wgu_hbm, wdn_hbm, first_hbm,
    result_out, dh2_out, gu0_out, gu1_out, gu2_out, dn_out, land_out,
    h2, h2t, e, wgu, wdn, a, at_ref, du, u, da, dgu, ddn, send_a, send_b, send_x, temp, acc, acc_out, result,
    gu0_y, gu2_y, dn_y, gu0_z1, gu0_z2, gu1_z1, gu1_z2, gu1_y, gu0_s, gu1_s, gu1_t, gu0_f, gu1_f,
    send_sems, recv_sems, local_sems,
):
    me, z = lax.axis_index("seq"), lax.axis_index("wsh")
    net = Net(me, z, send_sems, recv_sems, local_sems)
    ybit = (me // 4) % 2
    rows, width = first_hbm.shape
    hq = wdn.shape[0]
    chunk, pair = chunk_sizes(hq)
    part = width // 4
    half = part // 2
    z1, z2, z3 = mirrored(z, 1), mirrored(z, 2), 3 - z
    block = 4 * rows

    load_h2 = [net.move(h2_hbm.at[j], h2.at[pl.ds(j * rows, rows)]) for j in range(4)]
    load_gu = [net.move(wgu_hbm.at[i], wgu.at[pl.ds(i * part, part)]) for i in range(4)]
    load_e = [net.move(e_hbm.at[j], e.at[pl.ds(j * rows, rows)]) for j in range(4)]
    load_dn = net.move(wdn_hbm, wdn)
    load_first = net.move(first_hbm, acc_out)
    greet([net.seat(n) for n in ("core", "x", "y", "z1", "z2")])
    for c in load_h2:
        c.wait()

    def turn(j, carry):
        at = pl.ds(pl.multiple_of(j * 256, 256), 256)
        h2t[:, at] = h2[at].T
        return carry

    lax.fori_loop(0, block // 256, turn, 0)
    for c in load_gu + load_e + [load_dn]:
        c.wait()

    def forward(k):
        pcols, ccols = pl.ds(k * pair, pair), pl.ds(k * chunk, chunk)

        def one(j, carry):
            at = pl.ds(pl.multiple_of(j * rows, rows), rows)
            u[...] = jnp.dot(h2[at], wgu[:, pcols], preferred_element_type=full)
            da[...] = outer(e[at], wdn[ccols])

            def piece(r, carry):
                rr = pl.ds(pl.multiple_of(r * 64, 64), 64)
                tt = pl.ds(pl.multiple_of(j * rows + r * 64, 64), 64)
                gate, upper, back = u[rr, :chunk], u[rr, chunk:], da[rr]
                sigma = jax.nn.sigmoid(gate)
                swish = gate * sigma
                a[tt, ccols] = (swish * upper).astype(low)
                du[tt, pl.ds(k * pair, chunk)] = (
                    back * upper * (sigma * (1.0 + gate * (1.0 - sigma)))
                ).astype(low)
                du[tt, pl.ds(k * pair + chunk, chunk)] = (back * swish).astype(low)
                return carry

            lax.fori_loop(0, rows // 64, piece, 0)
            at_ref[:, at] = a[at, ccols].T
            return carry

        lax.fori_loop(0, 4, one, 0)

    def weights(k):
        def gate_up(n, carry):
            cols = pl.ds(pl.multiple_of(k * pair + n * 256, 256), 256)
            got = jnp.dot(h2t[...], du[:, cols], preferred_element_type=full).astype(low)
            dgu[:, :, :, cols] = got.reshape(4, 2, half, 256)
            return carry

        lax.fori_loop(0, pair // 256, gate_up, 0)

        def down(n, carry):
            cols = pl.ds(pl.multiple_of(n * 512, 512), 512)
            got = jnp.dot(at_ref[...], e[:, cols], preferred_element_type=full).astype(low)
            ddn[k, :, :, cols] = got.reshape(2, chunk // 2, 512)
            return carry

        lax.fori_loop(0, width // 512, down, 0)

    def cols_of(k):
        return pl.ds(k * pair, pair)

    forward(0)
    weights(0)
    y0 = net.send(dgu.at[:, 1 - ybit, :, cols_of(0)], gu0_y, "y")
    yd0 = net.send(ddn.at[0, 1 - ybit], dn_y.at[0], "y")
    forward(1)
    weights(1)
    m1 = net.send(dgu.at[z1, :, :, cols_of(1)], gu1_z1.at[0], "z1")
    m2 = net.send(dgu.at[z3, :, :, cols_of(1)], gu1_z1.at[1], "z1")
    yd1 = net.send(ddn.at[1, 1 - ybit], dn_y.at[1], "y")
    forward(2)

    def grad_rows(j, put):
        at = pl.ds(j * rows, rows)

        def one(n, carry):
            cols = pl.ds(pl.multiple_of(n * 256, 256), 256)
            put(cols, outer(du[at], wgu[cols]))
            return carry

        lax.fori_loop(0, width // 256, one, 0)

    def out_rows(j, put):
        at = pl.ds(j * rows, rows)

        def one(n, carry):
            cols = pl.ds(pl.multiple_of(n * 256, 256), 256)
            put(cols, jnp.dot(a[at], wdn[:, cols], preferred_element_type=full))
            return carry

        lax.fori_loop(0, width // 256, one, 0)

    def store(ref):
        def put(cols, value):
            ref[:, cols] = value.astype(low)

        return put

    def add(target, other):
        def put(cols, value):
            target[:, cols] = (value + other[:, cols].astype(full)).astype(target.dtype)

        return put

    def fetch(j):
        copy = net.move(land_out.at[j], temp)
        copy.wait()

    grad_rows(3, store(send_a))
    ga = net.send(send_a, land_out.at[0], "core")
    weights(2)
    y2 = net.send(dgu.at[:, 1 - ybit, :, cols_of(2)], gu2_y, "y")
    yd2 = net.send(ddn.at[2, 1 - ybit], dn_y.at[2], "y")
    ga.wait_recv()
    fetch(0)
    grad_rows(1, add(send_x, temp))
    gx = net.send(send_x, land_out.at[1], "x")

    def sum_rows(put, count, step):
        def one(i, carry):
            put(pl.ds(pl.multiple_of(i * step, step), step))
            return carry

        lax.fori_loop(0, count // step, one, 0)

    y0.wait_recv()

    def gu0_sum(i, carry):
        gu0_s[i] = (dgu[i, ybit, :, cols_of(0)].astype(full) + gu0_y[i].astype(full)).astype(low)
        return carry

    lax.fori_loop(0, 4, gu0_sum, 0)
    n1 = net.send(gu0_s.at[z1], gu0_z1.at[0], "z1")
    n2 = net.send(gu0_s.at[z3], gu0_z1.at[1], "z1")
    grad_rows(2, store(send_b))
    gb = net.send(send_b, land_out.at[2], "core")

    def keep(cols, value):
        acc[:, cols] = value

    grad_rows(0, keep)
    m1.wait_recv()
    m2.wait_recv()

    def gu1_sum(i, carry):
        gu1_t[i] = (dgu[z2, i, :, cols_of(1)].astype(full) + gu1_z1[1, i].astype(full)).astype(low)
        gu1_s[i] = (dgu[z, i, :, cols_of(1)].astype(full) + gu1_z1[0, i].astype(full)).astype(low)
        return carry

    lax.fori_loop(0, 2, gu1_sum, 0)
    m3 = net.send(gu1_t, gu1_z2, "z2")
    gb.wait_recv()
    fetch(2)

    def accumulate(target):
        def go(at):
            target[at] = target[at] + temp[at].astype(full)

        return go

    sum_rows(accumulate(acc), rows, 64)
    ga.wait_send()
    out_rows(3, store(send_a))
    oa = net.send(send_a, land_out.at[3], "core")
    n1.wait_recv()
    n2.wait_recv()
    own0 = (gu0_s[z2].astype(full) + gu0_z1[1].astype(full)).astype(low)
    gu0_f[1] = own0
    n3 = net.send(gu0_f.at[1], gu0_z2, "z2")
    gx.wait_recv()
    fetch(1)
    sum_rows(accumulate(acc), rows, 64)
    keep_dh2 = net.move(acc, dh2_out)
    oa.wait_recv()
    fetch(3)
    gx.wait_send()
    out_rows(1, add(send_x, temp))
    ox = net.send(send_x, land_out.at[4], "x")
    gb.wait_send()
    out_rows(2, store(send_b))
    ob = net.send(send_b, land_out.at[5], "core")
    load_first.wait()

    def more(cols, value):
        acc_out[:, cols] = acc_out[:, cols] + value

    out_rows(0, more)
    m3.wait_recv()

    def gu1_more(i, carry):
        gu1_s[i] = (gu1_s[i].astype(full) + gu1_z2[i].astype(full)).astype(low)
        return carry

    lax.fori_loop(0, 2, gu1_more, 0)
    m4 = net.send(gu1_s.at[1 - ybit], gu1_y, "y")
    n3.wait_recv()
    gu0_f[0] = (
        gu0_s[z].astype(full) + gu0_z1[0].astype(full) + gu0_z2[...].astype(full)
    ).astype(low)
    keep_gu0 = net.move(gu0_f.at[0], gu0_out)
    ob.wait_recv()
    fetch(5)
    sum_rows(accumulate(acc_out), rows, 64)
    ox.wait_recv()
    fetch(4)

    def finish(at):
        result[at] = (acc_out[at] + temp[at].astype(full)).astype(low)

    sum_rows(finish, rows, 64)
    keep_result = net.move(result, result_out)

    yd0.wait_recv()
    yd1.wait_recv()
    y2.wait_recv()

    def gu2_sum(i, carry):
        dgu[i, ybit, :, cols_of(2)] = (
            dgu[i, ybit, :, cols_of(2)].astype(full) + gu2_y[i].astype(full)
        ).astype(low)
        return carry

    lax.fori_loop(0, 4, gu2_sum, 0)
    keep_gu2 = net.move(dgu.at[:, ybit, :, cols_of(2)], gu2_out)
    yd2.wait_recv()

    def dn_sum(i, carry):
        ddn[i, ybit] = (ddn[i, ybit].astype(full) + dn_y[i].astype(full)).astype(low)
        return carry

    lax.fori_loop(0, 3, dn_sum, 0)
    keep_dn = net.move(ddn.at[:, ybit], dn_out)
    m4.wait_recv()
    gu1_f[...] = (gu1_s[ybit].astype(full) + gu1_y[...].astype(full)).astype(low)
    keep_gu1 = net.move(gu1_f, gu1_out)
    for c in (y0, yd0, m1, m2, yd1, y2, yd2, n1, n2, m3, oa, n3, ox, ob, m4):
        c.wait_send()
    for c in (keep_dh2, keep_gu0, keep_result, keep_gu2, keep_dn, keep_gu1):
        c.wait()


def feed(seq, h2_all, e_all, wgu, wdn, first):
    rows, width = first.shape
    part = width // 4
    half = part // 2
    hq = wdn.shape[0]
    chunk, pair = chunk_sizes(hq)
    shape = jax.ShapeDtypeStruct
    anyspace = pl.BlockSpec(memory_space=pl.ANY)
    outs = [
        shape((rows, width), low),
        shape((rows, width), full),
        shape((half, pair), low),
        shape((half, pair), low),
        shape((4, half, pair), low),
        shape((3, chunk // 2, width), low),
        shape((6, rows, width), low),
    ]
    v = pltpu.VMEM
    scratch = [
        v((4 * rows, width), low),
        v((width, 4 * rows), low),
        v((4 * rows, width), low),
        v((width, 2 * hq), low),
        v((hq, width), low),
        v((4 * rows, hq), low),
        v((chunk, 4 * rows), low),
        v((4 * rows, 2 * hq), low),
        v((rows, pair), full),
        v((rows, chunk), full),
        v((4, 2, half, 2 * hq), low),
        v((3, 2, chunk // 2, width), low),
        v((rows, width), low),
        v((rows, width), low),
        v((rows, width), low),
        v((rows, width), low),
        v((rows, width), full),
        v((rows, width), full),
        v((rows, width), low),
        v((4, half, pair), low),
        v((4, half, pair), low),
        v((3, chunk // 2, width), low),
        v((2, half, pair), low),
        v((half, pair), low),
        v((2, 2, half, pair), low),
        v((2, half, pair), low),
        v((half, pair), low),
        v((4, half, pair), low),
        v((2, half, pair), low),
        v((2, half, pair), low),
        v((2, half, pair), low),
        v((half, pair), low),
        pltpu.SemaphoreType.DMA((24,)),
        pltpu.SemaphoreType.DMA((24,)),
        pltpu.SemaphoreType.DMA((32,)),
    ]
    return pl.pallas_call(
        functools.partial(feed_kernel, seq),
        out_shape=outs,
        in_specs=[anyspace] * 5,
        out_specs=[anyspace] * len(outs),
        scratch_shapes=scratch,
        compiler_params=pltpu.CompilerParams(
            collective_id=1, has_side_effects=True, vmem_limit_bytes=63 * MIB
        ),
        name="feed",
    )(h2_all, e_all, wgu, wdn, first)


def finish_kernel(
    seq,
    starts_ref, small_all, x_hbm, e_hbm, first_hbm, dh2_hbm, proj_hbm, zed_hbm, gext_hbm, wc_hbm,
    gu0_hbm, gu1_hbm, gu2_hbm, dn_hbm,
    grad_out, gin_out, gout_out, ggu_out, gdn_out, gsmall_out, up_c, up_gu, up_dn,
    wc, first, dh2, x_ref, e_ref, proj, zed, ht, gext, dx1, dp, s1, s2, dwc,
    ret_send, ret_land, sums, sums_core, sums_plane, sums_z, small_out,
    cr, r1, r2, rz1, rz2, fin_c, fin_gu, fin_dn, g2, g2_z1, g2_z2, dnv, dn_z1, dn_z2, stage,
    send_sems, recv_sems, local_sems,
):
    me, z = lax.axis_index("seq"), lax.axis_index("wsh")
    net = Net(me, z, send_sems, recv_sems, local_sems)
    core, xbit, ybit = me % 2, (me // 2) % 2, (me // 4) % 2
    quarter = me % 4
    rows, width = first.shape
    part = width // 4
    half = part // 2
    chunk = dnv.shape[1] * 2
    pair = 2 * chunk
    hq = 3 * chunk
    hidden = 4 * hq
    z1, z2, z3 = mirrored(z, 1), mirrored(z, 2), 3 - z
    after = {"seq": lax.rem(me + 1, seq), "wsh": z}
    before = {"seq": lax.rem(me + seq - 1, seq), "wsh": z}
    cross = {"seq": mirrored(mirrored(me, 2), 4), "wsh": z}
    upper = [
        {"seq": mirrored(me, 1 << bit), "wsh": z} for bit in range(3, seq.bit_length() - 1)
    ]
    same0 = (z % 2) == (quarter % 2)
    same1 = (z // 2) == (quarter // 2)
    holder = same0 & same1
    level = core == z % 2

    load_gu2 = net.move(gu2_hbm, g2)
    load_dn = net.move(dn_hbm, dnv)
    load_gu = [
        net.move(gu0_hbm, fin_gu.at[0, xbit, core, ybit]),
        net.move(gu1_hbm, fin_gu.at[1, xbit, core, ybit]),
    ]
    load_first = net.move(first_hbm, first)
    load_dh2 = net.move(dh2_hbm, dh2)
    load_e = net.move(e_hbm, e_ref)
    load_wc = net.move(wc_hbm, wc)
    load_zed = net.move(zed_hbm, zed)
    zedt, do_ref, out_ref = ht, e_ref, zed
    load_x = net.move(x_hbm, x_ref)
    load_gext = net.move(gext_hbm, gext)
    load_proj = net.move(proj_hbm, proj)
    greet(
        [net.seat(n) for n in ("core", "x", "y", "z1", "z2", "z3")] + [after, cross] + upper
    )

    def plus_upper(ref, land, temp):
        for i, seat in enumerate(upper):
            copy = net.send(ref, land.at[i], seat)
            copy.wait()
            net.move(land.at[i], temp).wait()
            ref[...] = (ref[...].astype(full) + temp[...].astype(full)).astype(ref.dtype)

    load_gu2.wait()
    g1a = net.send(g2.at[z1], g2_z1.at[0], "z1")
    g1b = net.send(g2.at[z3], g2_z1.at[1], "z1")
    load_dn.wait()
    dn1 = net.make(dnv, dn_z1, "z1")
    dn2 = net.make(dnv, dn_z2, "z2")

    @pl.when(~same0)
    def _():
        dn1.start()

    def spread_gu(k):
        own = fin_gu.at[k, xbit, core, ybit]
        return net.send(own, own, "x"), net.send(own, own, "y")

    lo, hi = pl.ds(0, chunk), pl.ds(chunk, chunk)

    def onward_gu(k, b):
        b[0].wait_recv()
        spot = fin_gu.at[k, 1 - xbit, core, ybit, :, lo]
        first_half = net.send(spot, spot, "y")
        b[1].wait_recv()
        spot = fin_gu.at[k, xbit, core, 1 - ybit, :, hi]
        return first_half, net.send(spot, spot, "x")

    def across_gu(k, d):
        d[0].wait_recv()
        d[1].wait_recv()
        return net.send(fin_gu.at[k, :, core], fin_gu.at[k, :, core], "core")

    if not upper:
        for c in load_gu:
            c.wait()
        gu_b = [spread_gu(0), spread_gu(1)]
    else:
        gu_b = []
        for k in range(2):
            load_gu[k].wait()
            up_gu_own = fin_gu.at[k, xbit, core, ybit]
            plus_upper(up_gu_own, up_gu.at[k], dp.at[pl.ds(0, half), pl.ds(0, pair)])
            gu_b.append(spread_gu(k))

    def row_of(k):
        return jnp.concatenate([small_all[i, k : k + 1, :] for i in range(4)], 1).astype(full)

    gain_one, gain_two = row_of(0), row_of(1)
    sums[...] = jnp.zeros_like(sums)
    load_first.wait()
    load_dh2.wait()
    load_e.wait()
    tile = 32

    def folded(value):
        return jnp.sum(value.reshape(value.shape[0] // 8, 8, value.shape[1]), axis=0)

    def norm_two(i, total):
        at = pl.ds(pl.multiple_of(i * tile, tile), tile)
        xf, dh = first[at], dh2[at]
        rate = lax.rsqrt(jnp.mean(xf * xf, axis=-1, keepdims=True) + epsilon)
        normed = xf * rate
        scaled = dh * gain_two
        mean = jnp.mean(scaled * normed, axis=-1, keepdims=True)
        got = e_ref[at].astype(full) + rate * (scaled - normed * mean)
        dx1[at] = got
        do_ref[at] = got.astype(low)
        return total + folded(dh * normed)

    total = lax.fori_loop(0, rows // tile, norm_two, jnp.zeros((8, width), full))
    sums[1:2, :] = jnp.sum(total, axis=0, keepdims=True)

    load_wc.wait()
    dz = first

    def back_out(i, carry):
        cols = pl.ds(pl.multiple_of(i * part, part), part)
        dz[:, cols] = outer(do_ref[...], wc[i, :, :, :, 3 * width :].reshape(part, width))
        return carry

    lax.fori_loop(0, 4, back_out, 0)
    load_zed.wait()
    load_x.wait()

    def turn_zed(i, carry):
        cols = pl.ds(pl.multiple_of(i * 256, 256), 256)
        zedt[:, cols] = zed[cols].T
        return carry

    lax.fori_loop(0, rows // 256, turn_zed, 0)

    def weight_chunk(left, right, at):
        def one(n, carry):
            cols = pl.ds(pl.multiple_of(n * 256, 256), 256)
            into = pl.ds(pl.multiple_of(at + n * 256, 256), 256)
            got = jnp.dot(left[...], right(cols), preferred_element_type=full).astype(low)
            dwc[:, :, :, :, :, into] = got.reshape(4, 2, 2, 2, part // 8, 256)
            return carry

        lax.fori_loop(0, width // 256, one, 0)

    starts_at = [3 * width, width, 0, 2 * width]

    def cols_of(i):
        return pl.ds(starts_at[i], width)

    def to_core(i):
        return net.send(dwc.at[:, :, :, 1 - core, :, cols_of(i)], cr.at[i], "core")

    weight_chunk(zedt, lambda cols: do_ref[:, cols], 3 * width)
    sc = [to_core(0)]

    g1a.wait_recv()
    g1b.wait_recv()
    g2[z2] = (g2[z2].astype(full) + g2_z1[1].astype(full)).astype(low)
    g2s = net.send(g2.at[z2], g2_z2, "z2")

    def add_dn(i, carry):
        dnv[i] = (dnv[i].astype(full) + dn_z1[i].astype(full)).astype(low)
        return carry

    @pl.when(same0)
    def _():
        dn1.wait_recv()
        lax.fori_loop(0, 3, add_dn, 0)

    @pl.when(same0 & ~same1)
    def _():
        dn2.start()

    place = me * rows + lax.broadcasted_iota(jnp.int32, (rows, 1), 0)
    starts = starts_ref[...]
    keep_one = (place - 1 >= starts).astype(full)
    keep_two = (place - 2 >= starts).astype(full)
    load_gext.wait()
    load_proj.wait()
    s1[rows:] = jnp.zeros((s1.shape[0] - rows, 128), full)
    s2[rows:] = jnp.zeros((s2.shape[0] - rows, 128), full)
    dg = dh2
    row8 = lax.broadcasted_iota(jnp.int32, (8, 128), 0)

    def unmix(i, carry):
        at = pl.ds(pl.multiple_of(i * 128, 128), 128)
        cat = pl.ds(pl.multiple_of(width + i * 128, 128), 128)
        zi = i // (part // 128)
        inside = pl.ds(pl.multiple_of((i % (part // 128)) * 128, 128), 128)
        taps = small_all[zi, :, inside].astype(full)
        tap0, tap1, tap2 = taps[2:3], taps[3:4], taps[4:5]
        current, lag_one, lag_two = gext[16:, at], gext[15 : rows + 15, at], gext[14 : rows + 14, at]
        mixed = tap0 * current + keep_one * tap1 * lag_one + keep_two * tap2 * lag_two
        back = dz[:, at]
        dp[:, cat] = (back * mixed).astype(low)
        dm = back * proj[:, cat]
        t1, t2 = keep_one * dm, keep_two * dm
        for k, value in ((2, dm * current), (3, t1 * lag_one), (4, t2 * lag_two)):
            sums[k : k + 1, at] = jnp.sum(folded(value), axis=0, keepdims=True)
        s1[:rows] = tap1 * t1
        s2[:rows] = tap2 * t2
        dg[:, at] = tap0 * dm + s1[1 : rows + 1] + s2[2 : rows + 2]
        ret_send[:, at] = jnp.where(
            row8 == 6, s2[0:1], jnp.where(row8 == 7, s1[0:1] + s2[1:2], 0.0)
        )
        return carry

    lax.fori_loop(0, width // 128, unmix, 0)
    back = net.send(ret_send, ret_land, before)

    def norm_one(i, carry):
        at = pl.ds(pl.multiple_of(i * 128, 128), 128)
        xf = x_ref[at].astype(full)
        rate = lax.rsqrt(jnp.mean(xf * xf, axis=-1, keepdims=True) + epsilon)
        ht[:, at] = (xf * rate * gain_one).astype(low).T
        return carry

    lax.fori_loop(0, rows // 128, norm_one, 0)
    weight_chunk(ht, lambda cols: dp[:, pl.ds(pl.multiple_of(width + cols.start, 256), 256)], width)
    sc.append(to_core(1))

    orders = ["xy", "yx", "xy", "yx"]
    depth = part // 8

    def add_core(i):
        sc[i].wait_recv()

        def one(j, carry):
            zi, yi, xi = j // 4, (j // 2) % 2, j % 2
            spot = (zi, yi, xi, core, slice(None), cols_of(i))
            dwc[spot] = (dwc[spot].astype(full) + cr[i, zi, yi, xi].astype(full)).astype(low)
            return carry

        lax.fori_loop(0, 16, one, 0)
        cols = cols_of(i)
        if orders[i] == "xy":
            return net.send(dwc.at[:, :, 1 - xbit, core, :, cols], r1.at[i], "x")
        return net.send(dwc.at[:, 1 - ybit, :, core, :, cols], r1.at[i], "y")

    def add_first(i, copy):
        copy.wait_recv()

        def one(j, carry):
            zi, oi = j // 2, j % 2
            yi, xi = (oi, xbit) if orders[i] == "xy" else (ybit, oi)
            spot = (zi, yi, xi, core, slice(None), cols_of(i))
            dwc[spot] = (dwc[spot].astype(full) + r1[i, zi, oi].astype(full)).astype(low)
            return carry

        lax.fori_loop(0, 8, one, 0)
        cols = cols_of(i)
        if orders[i] == "xy":
            return net.send(dwc.at[:, 1 - ybit, xbit, core, :, cols], r2.at[i], "y")
        return net.send(dwc.at[:, ybit, 1 - xbit, core, :, cols], r2.at[i], "x")

    def add_second(i, copy):
        copy.wait_recv()

        def one(zi, carry):
            spot = (zi, ybit, xbit, core, slice(None), cols_of(i))
            dwc[spot] = (dwc[spot].astype(full) + r2[i, zi].astype(full)).astype(low)
            return carry

        lax.fori_loop(0, 4, one, 0)
        cols = cols_of(i)
        return (
            net.send(dwc.at[z1, ybit, xbit, core, :, cols], rz1.at[i, 0], "z1"),
            net.send(dwc.at[z3, ybit, xbit, core, :, cols], rz1.at[i, 1], "z1"),
        )

    def add_z1(i, copies):
        for c in copies:
            c.wait_recv()
        spot = (z2, ybit, xbit, core, slice(None), cols_of(i))
        dwc[spot] = (dwc[spot].astype(full) + rz1[i, 1].astype(full)).astype(low)
        return net.send(dwc.at[spot], rz2.at[i], "z2")

    def add_z2(i, copy):
        copy.wait_recv()
        spot = (z, ybit, xbit, core, slice(None), cols_of(i))
        own = fin_c.at[i, ybit, xbit, core]
        own[...] = (
            dwc[spot].astype(full) + rz1[i, 0].astype(full) + rz2[i].astype(full)
        ).astype(low)
        plus_upper(own, up_c.at[i], e_ref.at[pl.ds(0, part // 8)])
        return net.send(own, own, "x"), net.send(own, own, "y")

    def onward_c(i, copies):
        for c in copies:
            c.wait_recv()
        spot = fin_c.at[i, ybit, 1 - xbit, core]
        return net.send(spot, spot, "y")

    def across_c(i, copy):
        copy.wait_recv()
        return net.send(fin_c.at[i, :, :, core], fin_c.at[i, :, :, core], "core")

    a = {}
    b = {}
    a[0] = add_core(0)
    gu_d = [onward_gu(k, gu_b[k]) for k in range(2)]
    back.wait_recv()
    follows = (me < seq - 1).astype(full)
    dg[rows - 8 :] = dg[rows - 8 :] + ret_land[...] * follows

    def unproject(i, carry):
        at = pl.ds(pl.multiple_of(i * 128, 128), 128)
        xat = pl.ds(pl.multiple_of(2 * width + i * 128, 128), 128)
        dp[:, at] = (dg[:, at] * proj[:, xat]).astype(low)
        dp[:, xat] = (dg[:, at] * proj[:, at]).astype(low)
        return carry

    lax.fori_loop(0, width // 128, unproject, 0)
    weight_chunk(ht, lambda cols: dp[:, cols], 0)
    sc.append(to_core(2))
    a[1] = add_core(1)
    b[0] = add_first(0, a[0])
    weight_chunk(ht, lambda cols: dp[:, pl.ds(pl.multiple_of(2 * width + cols.start, 256), 256)], 2 * width)
    sc.append(to_core(3))
    a[2] = add_core(2)

    g2s.wait_recv()
    own = fin_gu.at[2, xbit, core, ybit]
    own[...] = (
        g2[z].astype(full) + g2_z1[0].astype(full) + g2_z2[...].astype(full)
    ).astype(low)
    plus_upper(own, up_gu.at[2], e_ref.at[pl.ds(0, half), pl.ds(0, pair)])
    gu_b.append(spread_gu(2))

    @pl.when(holder)
    def _():
        dn2.wait_recv()

        def one(i, carry):
            dnv[i] = (dnv[i].astype(full) + dn_z2[i].astype(full)).astype(low)
            return carry

        lax.fori_loop(0, 3, one, 0)
        plus_upper(dnv, up_dn, dn_z1)

        def two(i, carry):
            fin_dn[i, ybit] = dnv[i]
            return carry

        lax.fori_loop(0, 3, two, 0)

    dnx = net.make(fin_dn.at[:, ybit], fin_dn.at[:, ybit], "x")
    dny = net.make(fin_dn.at[:, ybit], fin_dn.at[:, ybit], "y")
    dnc = net.make(fin_dn, fin_dn, "core")

    @pl.when(holder)
    def _():
        dnx.start()
        dny.start()

    dh = dg

    def back_in(i, carry):
        cols = pl.ds(pl.multiple_of(i * part, part), part)
        dh[:, cols] = outer(dp[...], wc[i, :, :, :, : 3 * width].reshape(part, 3 * width))
        return carry

    lax.fori_loop(0, 4, back_in, 0)

    def norm_back(i, total):
        at = pl.ds(pl.multiple_of(i * tile, tile), tile)
        xf = x_ref[at].astype(full)
        rate = lax.rsqrt(jnp.mean(xf * xf, axis=-1, keepdims=True) + epsilon)
        normed = xf * rate
        got = dh[at]
        scaled = got * gain_one
        mean = jnp.mean(scaled * normed, axis=-1, keepdims=True)
        out_ref[at] = (dx1[at] + rate * (scaled - normed * mean)).astype(low)
        return total + folded(got * normed)

    total = lax.fori_loop(0, rows // tile, norm_back, jnp.zeros((8, width), full))
    keep_grad = net.move(out_ref, grad_out)
    sums[0:1, :] = jnp.sum(total, axis=0, keepdims=True)
    small_core = net.send(sums, sums_core, "core")
    a[3] = add_core(3)
    b[1] = add_first(1, a[1])
    c = {0: add_second(0, b[0])}
    gu_c = [across_gu(k, gu_d[k]) for k in range(2)]
    b[2] = add_first(2, a[2])
    small_core.wait()
    sums[...] = sums[...] + sums_core[...]
    small_plane = [
        net.send(sums, sums_plane.at[i], seat) for i, seat in enumerate(("x", "y", cross))
    ]
    c[1] = add_second(1, b[1])
    d = {0: add_z1(0, c[0])}
    b[3] = add_first(3, a[3])
    c[2] = add_second(2, b[2])

    @pl.when(level & ~holder)
    def _():
        dnx.wait_recv()
        dny.start()

    gu_d.append(onward_gu(2, gu_b[2]))
    d[1] = add_z1(1, c[1])
    c[3] = add_second(3, b[3])
    f = {0: add_z2(0, d[0])}
    for copy in small_plane:
        copy.wait()
    sums[...] = sums[...] + sums_plane[0] + sums_plane[1] + sums_plane[2]
    for i, seat in enumerate(upper):
        copy = net.send(sums, sums_plane.at[3 + i], seat)
        copy.wait()
        sums[...] = sums[...] + sums_plane[3 + i]
    def slab(zz):
        return sums.at[:, pl.ds(pl.multiple_of(zz * part, part), part)]

    small_z = [
        net.send(slab(zz), sums_z.at[i], seat)
        for i, (zz, seat) in enumerate(((z1, "z1"), (z2, "z2"), (z3, "z3")))
    ]
    d[2] = add_z1(2, c[2])
    f[1] = add_z2(1, d[1])

    ring = []

    def emit(value, targets):
        k = len(ring)
        if k >= 2:
            for copy in ring[k - 2]:
                copy.wait()
        room = stage.at[k % 2]
        room[: value.shape[0], : value.shape[1]] = value
        ring.append([net.move(room.at[r, cc], target) for (r, cc), target in targets])

    def emit_gu(k, got):
        got.wait_recv()
        for q in range(4):
            at = q * hq + k * chunk
            value = fin_gu[k, q // 2, q % 2].astype(full).reshape(part, pair)
            emit(
                value,
                [
                    ((pl.ds(0, part), lo), ggu_out.at[:, pl.ds(at, chunk)]),
                    ((pl.ds(0, part), hi), ggu_out.at[:, pl.ds(hidden + at, chunk)]),
                ],
            )

    def emit_c(i, got):
        got.wait_recv()
        value = fin_c[i].astype(full).reshape(part, width)
        target = gout_out if i == 0 else gin_out.at[:, cols_of(i)]
        emit(value, [((pl.ds(0, part), pl.ds(0, width)), target)])

    emit_gu(0, gu_c[0])
    emit_gu(1, gu_c[1])
    d[3] = add_z1(3, c[3])
    f[2] = add_z2(2, d[2])
    g = {0: onward_c(0, f[0])}

    @pl.when(level)
    def _():
        dny.wait_recv()
        dnc.start()

    gu_c.append(across_gu(2, gu_d[2]))
    g[1] = onward_c(1, f[1])
    f[3] = add_z2(3, d[3])
    h = {0: across_c(0, g[0])}
    g[2] = onward_c(2, f[2])
    h[1] = across_c(1, g[1])

    @pl.when(~level)
    def _():
        dnc.wait_recv()

    block = chunk // 2
    for k in range(6):
        target = gdn_out.at[pl.ds(k * block, block)]
        emit(fin_dn[k // 2, k % 2].astype(full), [((pl.ds(0, block), pl.ds(0, width)), target)])
    emit_gu(2, gu_c[2])
    g[3] = onward_c(3, f[3])
    h[2] = across_c(2, g[2])
    h[3] = across_c(3, g[3])
    for copy in small_z:
        copy.wait()
    small_out[...] = slab(z)[...] + sums_z[0] + sums_z[1] + sums_z[2]
    keep_small = net.move(small_out, gsmall_out)
    for i in range(4):
        emit_c(i, h[i])

    @pl.when(~same0)
    def _():
        dn1.wait_send()

    @pl.when(same0 & ~same1)
    def _():
        dn2.wait_send()

    @pl.when(holder)
    def _():
        dnx.wait_send()

    @pl.when(level)
    def _():
        dny.wait_send()
        dnc.wait_send()

    flat = [g1a, g1b, g2s, back]
    for group in (gu_b, gu_d):
        for pair_of in group:
            flat += list(pair_of)
    flat += gu_c + sc
    for group in (a, b, d, g, h):
        flat += list(group.values())
    for group in (c, f):
        for pair_of in group.values():
            flat += list(pair_of)
    for copy in flat:
        copy.wait_send()
    for k in range(max(0, len(ring) - 2), len(ring)):
        for copy in ring[k]:
            copy.wait()
    keep_grad.wait()
    keep_small.wait()


def finish(seq, starts, small_all, x, e, first, dh2, proj, zed, gext, wc, gu0, gu1, gu2, dn):
    rows, width = first.shape
    part = width // 4
    half, pair = gu0.shape
    chunk = pair // 2
    hq = 3 * chunk
    extra = seq.bit_length() - 4
    room = max(extra, 1)
    shape = jax.ShapeDtypeStruct
    anyspace = pl.BlockSpec(memory_space=pl.ANY)
    vmem = pl.BlockSpec(memory_space=pltpu.VMEM)
    outs = [
        shape((rows, width), low),
        shape((part, 3 * width), full),
        shape((part, width), full),
        shape((part, 8 * hq), full),
        shape((hq, width), full),
        shape((8, part), full),
    ]
    v = pltpu.VMEM
    eighth = part // 8
    outs += [
        shape((4, room, eighth, width), low),
        shape((3, room, half, pair), low),
        shape((room, 3, chunk // 2, width), low),
    ]
    scratch = [
        v((4, 4, 2, eighth, 4 * width), low),
        v((rows, width), full),
        v((rows, width), full),
        v((rows, width), low),
        v((rows, width), low),
        v((rows, 3 * width), full),
        v((rows, width), low),
        v((width, rows), low),
        v((rows + 16, width), full),
        v((rows, width), full),
        v((rows, 3 * width), low),
        v((rows + 8, 128), full),
        v((rows + 8, 128), full),
        v((4, 2, 2, 2, eighth, 4 * width), low),
        v((8, width), full),
        v((8, width), full),
        v((8, width), full),
        v((8, width), full),
        v((3 + room, 8, width), full),
        v((3, 8, part), full),
        v((8, part), full),
        v((4, 4, 2, 2, eighth, width), low),
        v((4, 4, 2, eighth, width), low),
        v((4, 4, eighth, width), low),
        v((4, 2, eighth, width), low),
        v((4, eighth, width), low),
        v((4, 2, 2, 2, eighth, width), low),
        v((3, 2, 2, 2, half, pair), low),
        v((3, 2, chunk // 2, width), low),
        v((4, half, pair), low),
        v((2, half, pair), low),
        v((half, pair), low),
        v((3, chunk // 2, width), low),
        v((3, chunk // 2, width), low),
        v((3, chunk // 2, width), low),
        v((2, part, width), full),
        pltpu.SemaphoreType.DMA((80 + 12 * extra,)),
        pltpu.SemaphoreType.DMA((80 + 12 * extra,)),
        pltpu.SemaphoreType.DMA((60 + 12 * extra,)),
    ]
    return pl.pallas_call(
        functools.partial(finish_kernel, seq),
        out_shape=outs,
        in_specs=[vmem, vmem] + [anyspace] * 12,
        out_specs=[anyspace] * len(outs),
        scratch_shapes=scratch,
        compiler_params=pltpu.CompilerParams(
            collective_id=2, has_side_effects=True, vmem_limit_bytes=63 * MIB
        ),
        name="finish",
    )(starts, small_all, x, e, first, dh2, proj, zed, gext, wc, gu0, gu1, gu2, dn)


def build(seq):
    def local(
        tokens,
        doc_start,
        norm1_gain,
        in_weight,
        conv_weight,
        out_weight,
        norm2_gain,
        gate_up_weight,
        down_weight,
        out_grad,
    ):
        x, cot = tokens[0], out_grad[0]
        starts = doc_start.T
        hq = down_weight.shape[0]
        small = jnp.concatenate(
            [norm1_gain[None], norm2_gain[None], conv_weight.T], 0
        ).astype(low)
        small = jnp.pad(small, ((0, 16 - small.shape[0]), (0, 0)))
        w_c, w_gu, w_down, cot_all, second_all, proj, first, zed, gext, small_all = gather(
            seq, x, cot, starts, small, in_weight, out_weight, gate_up_weight, down_weight
        )
        result, dh2, gu0, gu1, gu2, dn, _ = feed(
            seq, second_all, cot_all, w_gu, w_down.reshape(hq, x.shape[1]), first
        )
        grad_x, grad_in, grad_out, grad_gu, grad_down, grad_small, *_ = finish(
            seq, starts, small_all, x, cot, first, dh2, proj, zed, gext, w_c, gu0, gu1, gu2, dn
        )
        return (
            result[None],
            grad_x[None],
            grad_small[0],
            grad_in,
            grad_small[2:5].T,
            grad_out,
            grad_small[1],
            grad_gu,
            grad_down,
        )

    return local


def solution(mesh):
    in_specs = (
        P("wsh", "seq", None),
        P("wsh", "seq"),
        P("wsh"),
        P("wsh", None),
        P("wsh", None),
        P("wsh", None),
        P("wsh"),
        P("wsh", None),
        P("wsh", None),
        P("wsh", "seq", None),
    )
    out_specs = (
        P("wsh", "seq", None),
        P("wsh", "seq", None),
        P("wsh"),
        P("wsh", None),
        P("wsh", None),
        P("wsh", None),
        P("wsh"),
        P("wsh", None),
        P("wsh", None),
    )
    local = build(mesh.shape["seq"])
    return jax.shard_map(local, mesh=mesh, in_specs=in_specs, out_specs=out_specs, check_vma=False)
```

```python
import functools
import jax
import jax.numpy as jnp
from jax import lax
from jax.experimental import pallas as pl
from jax.experimental.pallas import tpu as pltpu
from jax.sharding import PartitionSpec as P

low = jnp.bfloat16
full = jnp.float32
MESH = pl.DeviceIdType.MESH
epsilon = 1e-06
MIB = 1 << 20


def mirrored(index, weight):
    return index + weight - 2 * weight * ((index // weight) % 2)


class Net:
    def __init__(self, me, z, send_sems, recv_sems, local_sems):
        self.me, self.z = me, z
        self.send_sems, self.recv_sems, self.local_sems = send_sems, recv_sems, local_sems
        self.count = self.local_count = 0

    def seat(self, name):
        me, z = self.me, self.z
        return {
            "core": {"seq": mirrored(me, 1), "wsh": z},
            "x": {"seq": mirrored(me, 2), "wsh": z},
            "y": {"seq": mirrored(me, 4), "wsh": z},
            "z1": {"seq": me, "wsh": mirrored(z, 1)},
            "z2": {"seq": me, "wsh": mirrored(z, 2)},
            "z3": {"seq": me, "wsh": 3 - z},
        }[name]

    def make(self, src, dst, seat, k=None):
        if k is None:
            k = self.count
            self.count += 1
        return pltpu.make_async_remote_copy(
            src_ref=src,
            dst_ref=dst,
            send_sem=self.send_sems.at[k],
            recv_sem=self.recv_sems.at[k],
            device_id=self.seat(seat) if isinstance(seat, str) else seat,
            device_id_type=MESH,
        )

    def send(self, src, dst, seat):
        copy = self.make(src, dst, seat)
        copy.start()
        return copy

    def move(self, src, dst):
        k = self.local_count
        self.local_count += 1
        copy = pltpu.make_async_copy(src, dst, self.local_sems.at[k])
        copy.start()
        return copy


def greet(seats):
    barrier = pltpu.get_barrier_semaphore()
    for seat in seats:
        pl.semaphore_signal(barrier, inc=1, device_id=seat, device_id_type=MESH)
    pl.semaphore_wait(barrier, len(seats))


def inner(left, right):
    return lax.dot_general(left, right, (((0,), (0,)), ((), ())), preferred_element_type=full)


def outer(left, right):
    return lax.dot_general(left, right, (((1,), (1,)), ((), ())), preferred_element_type=full)


def chunk_sizes(hq):
    chunk = hq // 3
    return chunk, 2 * chunk


def gather_kernel(
    seq,
    x_hbm, e_hbm, starts_ref, norm_one_ref, norm_two_ref, taps_ref, win_hbm, wout_hbm, wgu_hbm, wdn_hbm,
    wc_out, wgu_out, wdn_out, e_out, h2_out, proj_out, first_out, zed_out, gext_out, small_out,
    wc, ownf, winf, woutf, wguf, wdnf, wgu_own, wdn_own, x_ref, h_ref, proj, gext, zed, first, h2, small_all, small_own,
    send_sems, recv_sems, local_sems,
):
    me, z = lax.axis_index("seq"), lax.axis_index("wsh")
    net = Net(me, z, send_sems, recv_sems, local_sems)
    core, xbit, ybit = me % 2, (me // 2) % 2, (me // 4) % 2
    quarter = me % 4
    rows, width = x_hbm.shape
    part = width // 4
    hq = 6 * wdn_hbm.shape[2]
    hidden = 4 * hq
    half = part // 2
    z1, z2, z3 = mirrored(z, 1), mirrored(z, 2), 3 - z
    after = {"seq": lax.rem(me + 1, seq), "wsh": z}
    before = {"seq": lax.rem(me + seq - 1, seq), "wsh": z}

    piece = part // 8
    turn = (ybit * 2 + xbit) * 2 + core
    mine = pl.ds(pl.multiple_of(turn * piece, piece), piece)
    load_own = [
        net.move(win_hbm.at[mine], ownf.at[:, pl.ds(0, 3 * width)]),
        net.move(wout_hbm.at[mine], ownf.at[:, pl.ds(3 * width, width)]),
    ]
    load_x = net.move(x_hbm, x_ref.at[pl.ds(16, rows)])
    chunk, pair = chunk_sizes(hq)
    load_gu = []
    for k in range(3):
        for base, shift in ((quarter * hq, 0), (hidden + quarter * hq, chunk)):
            cut = pl.ds(pl.multiple_of(base + k * chunk, 128), chunk)
            load_gu.append(
                net.move(wgu_hbm.at[:, cut], wguf.at[:, pl.ds(k * pair + shift, chunk)])
            )
    load_win = net.move(win_hbm, winf)
    load_wout = net.move(wout_hbm, woutf)
    load_dn = net.move(wdn_hbm, wdnf)
    keep_e = net.move(e_hbm, e_out.at[0])
    small_own[...] = jnp.zeros_like(small_own)
    small_own[0:1] = norm_one_ref[...].astype(low).astype(full)
    small_own[1:2] = norm_two_ref[...].astype(low).astype(full)
    small_own[2:5] = taps_ref[...].astype(low).astype(full)
    small_all[z] = small_own[...].astype(low)
    for copy in load_own:
        copy.wait()
    spot = ybit * 2 + xbit
    spot_x = ybit * 2 + 1 - xbit
    spot_y = (1 - ybit) * 2 + xbit
    wc[z, spot, core] = ownf[...].astype(low)

    greet([net.seat(n) for n in ("core", "x", "y", "z1", "z2", "z3")] + [before])

    cols = [pl.ds(0, 2 * width), pl.ds(2 * width, 2 * width)]

    def own(zz):
        return wc.at[zz, spot, core]

    a1 = net.send(own(z), own(z), "z1")
    a2 = net.send(own(z), own(z), "z2")
    smalls = [net.send(small_all.at[z], small_all.at[z], n) for n in ("z1", "z2", "z3")]
    halo = net.send(x_hbm.at[pl.ds(rows - 16, 16)], x_ref.at[pl.ds(0, 16)], after)

    for copy in load_gu:
        copy.wait()
    wgu_own[...] = wguf[...].astype(low)
    keep_gu = net.move(wgu_own, wgu_out.at[z])
    load_win.wait()
    load_wout.wait()

    def cast_block(i, carry):
        @pl.when(i != turn)
        def _():
            at = pl.ds(pl.multiple_of(i * piece, piece), piece)
            wc[z, i // 2, i % 2, :, : 3 * width] = winf[at].astype(low)
            wc[z, i // 2, i % 2, :, 3 * width :] = woutf[at].astype(low)

        return carry

    lax.fori_loop(0, 8, cast_block, 0)
    load_dn.wait()

    def cast_dn(i, carry):
        wdn_own[i // 2, i % 2] = wdnf[i // 2, i % 2].astype(low)
        return carry

    lax.fori_loop(0, 6, cast_dn, 0)

    def spread(zz):
        return net.send(own(zz), own(zz), "x"), net.send(own(zz), own(zz), "y")

    def onward(zz, b):
        b[0].wait_recv()
        place = wc.at[zz, spot_x, core, :, cols[0]]
        d0 = net.send(place, place, "y")
        b[1].wait_recv()
        place = wc.at[zz, spot_y, core, :, cols[1]]
        return d0, net.send(place, place, "x")

    def across(zz, b, d):
        d[0].wait_recv()
        d[1].wait_recv()
        return net.send(wc.at[zz, :, core], wc.at[zz, :, core], "core")

    a1.wait_recv()
    b1 = spread(z1)
    a2.wait_recv()
    a3 = net.send(own(z2), own(z2), "z1")
    b2 = spread(z2)

    def gu(zz, yy, k):
        at = pl.ds(pl.multiple_of(yy * half, half), half)
        return wgu_out.at[zz, at, pl.ds(k * pair, pair)]

    f1, f2, f3, g1, g2, g3 = [], [], [], [], [], []
    for k in range(3):
        source = wgu_own.at[
            pl.ds(pl.multiple_of(ybit * half, half), half), pl.ds(k * pair, pair)
        ]
        f1.append(net.send(source, gu(z, ybit, k), "z1"))
        f2.append(net.send(source, gu(z, ybit, k), "z2"))

    def pass_gu(k):
        f1[k].wait_recv()
        g1.append(net.send(gu(z1, ybit, k), gu(z1, ybit, k), "y"))
        f2[k].wait_recv()
        f3.append(net.send(gu(z2, ybit, k), gu(z2, ybit, k), "z1"))
        g2.append(net.send(gu(z2, ybit, k), gu(z2, ybit, k), "y"))

    def pass_far(k):
        f3[k].wait_recv()
        g3.append(net.send(gu(z3, ybit, k), gu(z3, ybit, k), "y"))

    for copy in smalls:
        copy.wait_recv()
    load_x.wait()
    halo.wait_recv()

    def row_of(k):
        return jnp.concatenate([small_all[i, k : k + 1, :] for i in range(4)], 1).astype(full)

    gain_one, gain_two = row_of(0), row_of(1)

    def norm_one(i, carry):
        at = pl.ds(pl.multiple_of(i * 176, 16), 176)
        xf = x_ref[at].astype(full)
        rate = lax.rsqrt(jnp.mean(xf * xf, axis=-1, keepdims=True) + epsilon)
        h_ref[at] = (xf * rate * gain_one).astype(low)
        return carry

    lax.fori_loop(0, (rows + 16) // 176, norm_one, 0)
    d1 = onward(z1, b1)
    d2 = onward(z2, b2)
    a3.wait_recv()
    b3 = spread(z3)

    same0 = (z % 2) == (quarter % 2)
    same1 = (z // 2) == (quarter // 2)
    holder = same0 & same1
    dn2, dn1a, dn1b, dny = [], [], [], []
    for k in range(3):
        source = wdn_own.at[k, ybit]
        target = wdn_out.at[k, ybit]
        dn2.append(net.make(source, target, "z2"))
        dn1a.append(net.make(source, target, "z1"))
        dn1b.append(net.make(target, target, "z1", net.count - 1))
        dny.append(net.make(target, target, "y"))
    keep_dn = pltpu.make_async_copy(wdn_own, wdn_out, local_sems.at[24])

    def pass_dn(k):
        @pl.when(same0 & ~same1)
        def _():
            dn2[k].wait_recv()
            dn1b[k].start()
            dny[k].start()

        @pl.when(~same0)
        def _():
            dn1a[k].wait_recv()
            dny[k].start()

    c1 = across(z1, b1, d1)
    c2 = across(z2, b2, d2)
    d3 = onward(z3, b3)
    pass_gu(0)
    c3 = across(z3, b3, d3)

    @pl.when(holder)
    def _():
        for k in range(3):
            dn2[k].start()
            dn1a[k].start()
        keep_dn.start()

    for c in (c1, c2, c3):
        c.wait_recv()
    ex = net.send(e_hbm, e_out.at[1], "x")
    ec = net.send(e_hbm, e_out.at[2], "core")
    pass_gu(1)

    def project(i, carry):
        at = pl.ds(pl.multiple_of(i * 512, 512), 512)
        proj[:, at] = jnp.dot(
            h_ref[...], wc[:, :, :, :, at].reshape(width, 512), preferred_element_type=full
        )
        return carry

    lax.fori_loop(0, 6, project, 0)
    keep_wc = net.move(wc, wc_out)
    keep_proj = net.move(proj.at[pl.ds(16, rows)], proj_out)

    pass_gu(2)
    place = me * rows + lax.broadcasted_iota(jnp.int32, (rows, 1), 0)
    starts = jnp.broadcast_to(starts_ref[...], (8, rows)).T[:, 0:1]
    keep_one = (place - 1 >= starts).astype(full)
    keep_two = (place - 2 >= starts).astype(full)
    cw = 128
    def mix(i, carry):
        at = pl.ds(pl.multiple_of(i * cw, cw), cw)
        xat = pl.ds(pl.multiple_of(2 * width + i * cw, cw), cw)
        cat = pl.ds(pl.multiple_of(width + i * cw, cw), cw)
        gext[:, at] = (proj[:, at] * proj[:, xat]).astype(low).astype(full)
        zi = i // (part // cw)
        inside = pl.ds(pl.multiple_of((i % (part // cw)) * cw, cw), cw)
        taps = small_all[zi, :, inside].astype(full)
        mixed = (
            taps[2:3] * gext[16:, at]
            + keep_one * taps[3:4] * gext[15 : rows + 15, at]
            + keep_two * taps[4:5] * gext[14 : rows + 14, at]
        )
        zed[:, at] = (proj[16:, cat] * mixed).astype(low)
        return carry

    lax.fori_loop(0, width // cw, mix, 0)
    keep_zed = net.move(zed, zed_out)
    keep_gext = net.move(gext, gext_out)

    pass_far(0)
    pass_dn(0)

    def project_out(i, carry):
        at = pl.ds(pl.multiple_of(i * 512, 512), 512)
        wat = pl.ds(pl.multiple_of(3 * width + i * 512, 512), 512)
        first[:, at] = x_ref[16:, at].astype(full) + jnp.dot(
            zed[...], wc[:, :, :, :, wat].reshape(width, 512), preferred_element_type=full
        )
        return carry

    lax.fori_loop(0, 2, project_out, 0)
    keep_first = net.move(first, first_out)
    pass_far(1)

    def norm_two(i, carry):
        at = pl.ds(pl.multiple_of(i * 128, 128), 128)
        xf = first[at]
        rate = lax.rsqrt(jnp.mean(xf * xf, axis=-1, keepdims=True) + epsilon)
        h2[at] = (xf * rate * gain_two).astype(low)
        return carry

    lax.fori_loop(0, rows // 128, norm_two, 0)
    keep_h2 = net.move(h2, h2_out.at[0])
    hx = net.send(h2, h2_out.at[1], "x")
    hc = net.send(h2, h2_out.at[2], "core")
    keep_small = net.move(small_all, small_out)

    pass_far(2)
    ex.wait_recv()
    exc = net.send(e_out.at[1], e_out.at[3], "core")
    pass_dn(1)
    pass_dn(2)
    hx.wait_recv()
    hxc = net.send(h2_out.at[1], h2_out.at[3], "core")
    for c in (*g1, *g2, *g3, ec, exc, hc, hxc):
        c.wait_recv()

    @pl.when(~holder)
    def _():
        for copy in dny:
            copy.wait()

    @pl.when(holder)
    def _():
        for copy in dn2 + dn1a:
            copy.wait_send()
        keep_dn.wait()

    @pl.when(same0 & ~same1)
    def _():
        for copy in dn1b:
            copy.wait_send()

    for c in (
        *smalls, halo, a1, a2, a3, *b1, *b2, *b3, *d1, *d2, *d3, c1, c2, c3,
        *f1, *f2, *f3, *g1, *g2, *g3, ex, ec, exc, hx, hc, hxc,
    ):
        c.wait_send()
    for c in (keep_e, keep_gu, keep_wc, keep_proj, keep_zed, keep_gext, keep_first, keep_h2, keep_small):
        c.wait()


def gather(seq, x, e, starts, norm_one, norm_two, taps, win, wout, wgu, wdn):
    rows, width = x.shape
    part = width // 4
    hq = wdn.shape[0]
    thirds = (3, 2, hq // 6, width)
    wdn = wdn.reshape(thirds)
    shape = jax.ShapeDtypeStruct
    anyspace = pl.BlockSpec(memory_space=pl.ANY)
    vmem = pl.BlockSpec(memory_space=pltpu.VMEM)
    conv = (4, 4, 2, part // 8, 4 * width)
    outs = [
        shape(conv, low),
        shape((4, part, 2 * hq), low),
        shape(thirds, low),
        shape((4, rows, width), low),
        shape((4, rows, width), low),
        shape((rows, 3 * width), full),
        shape((rows, width), full),
        shape((rows, width), low),
        shape((rows + 16, width), full),
        shape((4, 16, part), low),
    ]
    scratch = [
        pltpu.VMEM(conv, low),
        pltpu.VMEM((part // 8, 4 * width), full),
        pltpu.VMEM((part, 3 * width), full),
        pltpu.VMEM((part, width), full),
        pltpu.VMEM((part, 2 * hq), full),
        pltpu.VMEM(thirds, full),
        pltpu.VMEM((part, 2 * hq), low),
        pltpu.VMEM(thirds, low),
        pltpu.VMEM((rows + 16, width), low),
        pltpu.VMEM((rows + 16, width), low),
        pltpu.VMEM((rows + 16, 3 * width), full),
        pltpu.VMEM((rows + 16, width), full),
        pltpu.VMEM((rows, width), low),
        pltpu.VMEM((rows, width), full),
        pltpu.VMEM((rows, width), low),
        pltpu.VMEM((4, 16, part), low),
        pltpu.VMEM((16, part), full),
        pltpu.SemaphoreType.DMA((64,)),
        pltpu.SemaphoreType.DMA((64,)),
        pltpu.SemaphoreType.DMA((26,)),
    ]
    return pl.pallas_call(
        functools.partial(gather_kernel, seq),
        out_shape=outs,
        in_specs=[anyspace, anyspace] + [vmem] * 4 + [anyspace] * 4,
        out_specs=[anyspace] * len(outs),
        scratch_shapes=scratch,
        compiler_params=pltpu.CompilerParams(
            collective_id=0, has_side_effects=True, vmem_limit_bytes=56 * MIB
        ),
        name="gather",
    )(x, e, starts, norm_one, norm_two, taps, win, wout, wgu, wdn)


def feed_kernel(
    seq,
    h2_hbm, e_hbm, wgu_hbm, wdn_hbm, first_hbm,
    result_out, dh2_out, gu0_out, gu1_out, gu2_out, dn_out, dn2_out, land_out,
    h2, h2t, e, wgu, wdn, a, at_ref, du, u, da, dgu, ddn, send_a, send_b, send_x, send_o, temp, acc, acc_out,
    gu0_y, gu2_y, dn_y, gu0_z1, gu0_z2, gu1_z1, gu1_z2, gu1_y, gu0_s, gu1_s, gu1_t, gu0_f, gu1_f,
    send_sems, recv_sems, local_sems,
):
    me, z = lax.axis_index("seq"), lax.axis_index("wsh")
    net = Net(me, z, send_sems, recv_sems, local_sems)
    ybit = (me // 4) % 2
    rows, width = first_hbm.shape
    hq = wdn.shape[0]
    chunk, pair = chunk_sizes(hq)
    part = width // 4
    half = part // 2
    z1, z2, z3 = mirrored(z, 1), mirrored(z, 2), 3 - z
    block = 4 * rows

    load_h2, load_e, load_gu, load_dn = [], [], [], []

    def load_block(j):
        load_h2.append(net.move(h2_hbm.at[j], h2.at[pl.ds(j * rows, rows)]))
        load_e.append(net.move(e_hbm.at[j], e.at[pl.ds(j * rows, rows)]))

    def load_chunk(k):
        pcols, ccols = pl.ds(k * pair, pair), pl.ds(k * chunk, chunk)
        for i in range(4):
            load_gu.append(net.move(wgu_hbm.at[i, :, pcols], wgu.at[pl.ds(i * part, part), pcols]))
        load_dn.append(net.move(wdn_hbm.at[ccols], wdn.at[ccols]))

    load_chunk(0)
    for j in range(4):
        load_block(j)
    load_chunk(1)
    load_chunk(2)
    load_first = net.move(first_hbm, acc_out)
    greet([net.seat(n) for n in ("core", "x", "y", "z1", "z2")])

    def turn(j, carry):
        at = pl.ds(pl.multiple_of(j * 256, 256), 256)
        h2t[:, at] = h2[at].T
        return carry

    def forward(k, slots, step):
        pcols, ccols = pl.ds(k * pair, pair), pl.ds(k * chunk, chunk)

        def one(i, carry):
            j = slots + i * step
            at = pl.ds(pl.multiple_of(j * rows, rows), rows)
            u[...] = jnp.dot(h2[at], wgu[:, pcols], preferred_element_type=full)
            da[...] = outer(e[at], wdn[ccols])

            def piece(r, carry):
                rr = pl.ds(pl.multiple_of(r * 64, 64), 64)
                tt = pl.ds(pl.multiple_of(j * rows + r * 64, 64), 64)
                gate, upper, back = u[rr, :chunk], u[rr, chunk:], da[rr]
                sigma = jax.nn.sigmoid(gate)
                swish = gate * sigma
                a[tt, ccols] = (swish * upper).astype(low)
                du[tt, pl.ds(k * pair, chunk)] = (
                    back * upper * (sigma * (1.0 + gate * (1.0 - sigma)))
                ).astype(low)
                du[tt, pl.ds(k * pair + chunk, chunk)] = (back * swish).astype(low)
                return carry

            lax.fori_loop(0, rows // 64, piece, 0)
            return carry

        lax.fori_loop(0, 4 // step, one, 0)

    def weights(k):
        def turn_a(j, carry):
            at = pl.ds(pl.multiple_of(j * rows, rows), rows)
            at_ref[:, at] = a[at, pl.ds(k * chunk, chunk)].T
            return carry

        lax.fori_loop(0, 4, turn_a, 0)

        def gate_up(n, carry):
            cols = pl.ds(pl.multiple_of(k * pair + n * 256, 256), 256)
            got = jnp.dot(h2t[...], du[:, cols], preferred_element_type=full).astype(low)
            dgu[:, :, :, cols] = got.reshape(4, 2, half, 256)
            return carry

        lax.fori_loop(0, pair // 256, gate_up, 0)

        def down(n, carry):
            cols = pl.ds(pl.multiple_of(n * 512, 512), 512)
            got = jnp.dot(at_ref[...], e[:, cols], preferred_element_type=full).astype(low)
            ddn[k, :, :, cols] = got.reshape(2, chunk // 2, 512)
            return carry

        lax.fori_loop(0, width // 512, down, 0)

    def cols_of(k):
        return pl.ds(k * pair, pair)

    for copy in load_gu[:4] + load_dn[:1]:
        copy.wait()
    for j in range(4):
        load_h2[j].wait()
        load_e[j].wait()
        forward(0, j, 4)
    lax.fori_loop(0, block // 256, turn, 0)
    weights(0)
    for copy in load_gu[4:] + load_dn[1:]:
        copy.wait()
    y0 = net.send(dgu.at[:, 1 - ybit, :, cols_of(0)], gu0_y, "y")
    yd0 = net.send(ddn.at[0, 1 - ybit], dn_y.at[0], "y")
    forward(1, 1, 2)
    forward(2, 1, 2)

    def sum_rows(put, count, step):
        def one(i, carry):
            put(pl.ds(pl.multiple_of(i * step, step), step))
            return carry

        lax.fori_loop(0, count // step, one, 0)

    def accumulate(target):
        def go(at):
            target[at] = target[at] + temp[at].astype(full)

        return go

    def keep(cols, value):
        acc[:, cols] = value

    def more(cols, value):
        acc_out[:, cols] = acc_out[:, cols] + value

    def gu0_sum(i, carry):
        gu0_s[i] = (dgu[i, ybit, :, cols_of(0)].astype(full) + gu0_y[i].astype(full)).astype(low)
        return carry

    def gu1_sum(i, carry):
        gu1_t[i] = (dgu[z2, i, :, cols_of(1)].astype(full) + gu1_z1[1, i].astype(full)).astype(low)
        gu1_s[i] = (dgu[z, i, :, cols_of(1)].astype(full) + gu1_z1[0, i].astype(full)).astype(low)
        return carry

    def gu1_more(i, carry):
        gu1_s[i] = (gu1_s[i].astype(full) + gu1_z2[i].astype(full)).astype(low)
        return carry

    def finish(at):
        send_a[at] = (acc_out[at] + temp[at].astype(full)).astype(low)

    def grad_rows(j, put):
        at = pl.ds(j * rows, rows)

        def one(n, carry):
            cols = pl.ds(pl.multiple_of(n * 256, 256), 256)
            put(cols, outer(du[at], wgu[cols]))
            return carry

        lax.fori_loop(0, width // 256, one, 0)

    def out_rows(j, put):
        at = pl.ds(j * rows, rows)

        def one(n, carry):
            cols = pl.ds(pl.multiple_of(n * 256, 256), 256)
            put(cols, jnp.dot(a[at], wdn[:, cols], preferred_element_type=full))
            return carry

        lax.fori_loop(0, width // 256, one, 0)

    def store(ref):
        def put(cols, value):
            ref[:, cols] = value.astype(low)

        return put

    def add(target, other):
        def put(cols, value):
            target[:, cols] = (value + other[:, cols].astype(full)).astype(target.dtype)

        return put

    def fetch(j):
        copy = net.move(land_out.at[j], temp)
        copy.wait()

    grad_rows(3, store(send_a))
    ga = net.send(send_a, land_out.at[0], "core")
    out_rows(3, store(send_b))
    oa = net.send(send_b, land_out.at[3], "core")
    ga.wait_recv()
    fetch(0)
    grad_rows(1, add(send_x, temp))
    gx = net.send(send_x, land_out.at[1], "x")
    oa.wait_recv()
    fetch(3)
    out_rows(1, add(send_o, temp))
    ox = net.send(send_o, land_out.at[4], "x")
    forward(1, 0, 2)
    weights(1)
    m1 = net.send(dgu.at[z1, :, :, cols_of(1)], gu1_z1.at[0], "z1")
    m2 = net.send(dgu.at[z3, :, :, cols_of(1)], gu1_z1.at[1], "z1")
    yd1 = net.send(ddn.at[1, 1 - ybit], dn_y.at[1], "y")
    forward(2, 0, 2)
    weights(2)
    y2 = net.send(dgu.at[:, 1 - ybit, :, cols_of(2)], gu2_y, "y")
    keep_dn2 = net.move(ddn.at[2], dn2_out)
    y0.wait_recv()
    lax.fori_loop(0, 4, gu0_sum, 0)
    n1 = net.send(gu0_s.at[z1], gu0_z1.at[0], "z1")
    n2 = net.send(gu0_s.at[z3], gu0_z1.at[1], "z1")
    m1.wait_recv()
    m2.wait_recv()
    lax.fori_loop(0, 2, gu1_sum, 0)
    m3 = net.send(gu1_t, gu1_z2, "z2")
    ga.wait_send()
    grad_rows(2, store(send_a))
    gb = net.send(send_a, land_out.at[2], "core")
    oa.wait_send()
    out_rows(2, store(send_b))
    ob = net.send(send_b, land_out.at[5], "core")
    grad_rows(0, keep)
    gb.wait_recv()
    fetch(2)
    sum_rows(accumulate(acc), rows, 64)
    load_first.wait()
    out_rows(0, more)
    ob.wait_recv()
    fetch(5)
    sum_rows(accumulate(acc_out), rows, 64)
    n1.wait_recv()
    n2.wait_recv()
    gu0_f[1] = (gu0_s[z2].astype(full) + gu0_z1[1].astype(full)).astype(low)
    n3 = net.send(gu0_f.at[1], gu0_z2, "z2")
    m3.wait_recv()
    lax.fori_loop(0, 2, gu1_more, 0)
    m4 = net.send(gu1_s.at[1 - ybit], gu1_y, "y")
    gx.wait_recv()
    fetch(1)
    sum_rows(accumulate(acc), rows, 64)
    keep_dh2 = net.move(acc, dh2_out)
    n3.wait_recv()
    gu0_f[0] = (
        gu0_s[z].astype(full) + gu0_z1[0].astype(full) + gu0_z2[...].astype(full)
    ).astype(low)
    keep_gu0 = net.move(gu0_f.at[0], gu0_out)
    ox.wait_recv()
    fetch(4)
    gb.wait_send()
    sum_rows(finish, rows, 64)
    keep_result = net.move(send_a, result_out)

    yd0.wait_recv()
    yd1.wait_recv()
    y2.wait_recv()

    def gu2_sum(i, carry):
        dgu[i, ybit, :, cols_of(2)] = (
            dgu[i, ybit, :, cols_of(2)].astype(full) + gu2_y[i].astype(full)
        ).astype(low)
        return carry

    lax.fori_loop(0, 4, gu2_sum, 0)
    keep_gu2 = net.move(dgu.at[:, ybit, :, cols_of(2)], gu2_out)

    def dn_sum(i, carry):
        ddn[i, ybit] = (ddn[i, ybit].astype(full) + dn_y[i].astype(full)).astype(low)
        return carry

    lax.fori_loop(0, 2, dn_sum, 0)
    keep_dn = net.move(ddn.at[pl.ds(0, 2), ybit], dn_out)
    m4.wait_recv()
    gu1_f[...] = (gu1_s[ybit].astype(full) + gu1_y[...].astype(full)).astype(low)
    keep_gu1 = net.move(gu1_f, gu1_out)
    for c in (y0, yd0, m1, m2, yd1, y2, n1, n2, m3, n3, ox, ob, m4, gx):
        c.wait_send()
    for c in (keep_dh2, keep_gu0, keep_result, keep_gu2, keep_dn, keep_dn2, keep_gu1):
        c.wait()


def feed(seq, h2_all, e_all, wgu, wdn, first):
    rows, width = first.shape
    part = width // 4
    half = part // 2
    hq = wdn.shape[0]
    chunk, pair = chunk_sizes(hq)
    shape = jax.ShapeDtypeStruct
    anyspace = pl.BlockSpec(memory_space=pl.ANY)
    outs = [
        shape((rows, width), low),
        shape((rows, width), full),
        shape((half, pair), low),
        shape((half, pair), low),
        shape((4, half, pair), low),
        shape((2, chunk // 2, width), low),
        shape((2, chunk // 2, width), low),
        shape((6, rows, width), low),
    ]
    v = pltpu.VMEM
    scratch = [
        v((4 * rows, width), low),
        v((width, 4 * rows), low),
        v((4 * rows, width), low),
        v((width, 2 * hq), low),
        v((hq, width), low),
        v((4 * rows, hq), low),
        v((chunk, 4 * rows), low),
        v((4 * rows, 2 * hq), low),
        v((rows, pair), full),
        v((rows, chunk), full),
        v((4, 2, half, 2 * hq), low),
        v((3, 2, chunk // 2, width), low),
        v((rows, width), low),
        v((rows, width), low),
        v((rows, width), low),
        v((rows, width), low),
        v((rows, width), low),
        v((rows, width), full),
        v((rows, width), full),
        v((4, half, pair), low),
        v((4, half, pair), low),
        v((2, chunk // 2, width), low),
        v((2, half, pair), low),
        v((half, pair), low),
        v((2, 2, half, pair), low),
        v((2, half, pair), low),
        v((half, pair), low),
        v((4, half, pair), low),
        v((2, half, pair), low),
        v((2, half, pair), low),
        v((2, half, pair), low),
        v((half, pair), low),
        pltpu.SemaphoreType.DMA((24,)),
        pltpu.SemaphoreType.DMA((24,)),
        pltpu.SemaphoreType.DMA((44,)),
    ]
    return pl.pallas_call(
        functools.partial(feed_kernel, seq),
        out_shape=outs,
        in_specs=[anyspace] * 5,
        out_specs=[anyspace] * len(outs),
        scratch_shapes=scratch,
        compiler_params=pltpu.CompilerParams(
            collective_id=1, has_side_effects=True, vmem_limit_bytes=63 * MIB
        ),
        name="feed",
    )(h2_all, e_all, wgu, wdn, first)


def finish_kernel(
    seq,
    starts_ref, small_all, x_hbm, e_hbm, first_hbm, dh2_hbm, proj_hbm, zed_hbm, gext_hbm, wc_hbm,
    gu0_hbm, gu1_hbm, gu2_hbm, dn_hbm, dn2_hbm,
    grad_out, gin_out, gout_out, ggu_out, gdn_out, gsmall_out, up_c, up_gu, up_dn,
    wc, first, dh2, x_ref, e_ref, proj, zed, ht, gext, dx1, dp, s1, s2, dwc,
    ret_send, ret_land, sums, sums_core, sums_plane, sums_z, small_out,
    cr, r1, r2, rz, fin_c, fin_gu, fin_dn, g2, g2_z1, g2_z2, dnv, dn_z1, dn_z2, dn_o, dn_y,
    send_sems, recv_sems, local_sems,
):
    me, z = lax.axis_index("seq"), lax.axis_index("wsh")
    net = Net(me, z, send_sems, recv_sems, local_sems)
    core, xbit, ybit = me % 2, (me // 2) % 2, (me // 4) % 2
    quarter = me % 4
    rows, width = first.shape
    part = width // 4
    half = part // 2
    chunk = dnv.shape[1] * 2
    pair = 2 * chunk
    hq = 3 * chunk
    hidden = 4 * hq
    z1, z2, z3 = mirrored(z, 1), mirrored(z, 2), 3 - z
    after = {"seq": lax.rem(me + 1, seq), "wsh": z}
    before = {"seq": lax.rem(me + seq - 1, seq), "wsh": z}
    cross = {"seq": mirrored(mirrored(me, 2), 4), "wsh": z}
    upper = [
        {"seq": mirrored(me, 1 << bit), "wsh": z} for bit in range(3, seq.bit_length() - 1)
    ]
    same0 = (z % 2) == (quarter % 2)
    same1 = (z // 2) == (quarter // 2)
    holder = same0 & same1
    level = core == z % 2

    load_gu2 = net.move(gu2_hbm, g2)
    load_dn = [
        net.move(dn2_hbm.at[ybit], dnv.at[2]),
        net.move(dn2_hbm.at[1 - ybit], dn_o),
        net.move(dn_hbm, dnv.at[pl.ds(0, 2)]),
    ]
    load_gu = [
        net.move(gu0_hbm, fin_gu.at[0, xbit, core, ybit]),
        net.move(gu1_hbm, fin_gu.at[1, xbit, core, ybit]),
    ]
    load_first = net.move(first_hbm, first)
    load_dh2 = net.move(dh2_hbm, dh2)
    load_e = net.move(e_hbm, e_ref)
    outer_cols = pl.ds(3 * width, width)
    inner_cols = pl.ds(0, 3 * width)
    load_wc = net.move(
        wc_hbm.at[:, :, :, :, outer_cols], wc.at[:, :, :, :, outer_cols]
    )
    load_zed = net.move(zed_hbm, zed)
    zedt, do_ref, out_ref = ht, e_ref, zed
    load_x = net.move(x_hbm, x_ref)
    load_gext = net.move(gext_hbm, gext)
    load_proj = net.move(proj_hbm, proj)
    load_win = net.move(
        wc_hbm.at[:, :, :, :, inner_cols], wc.at[:, :, :, :, inner_cols]
    )
    greet(
        [net.seat(n) for n in ("core", "x", "y", "z1", "z2", "z3")] + [after, cross] + upper
    )

    def plus_upper(ref, land, temp):
        for i, seat in enumerate(upper):
            copy = net.send(ref, land.at[i], seat)
            copy.wait()
            net.move(land.at[i], temp).wait()
            ref[...] = (ref[...].astype(full) + temp[...].astype(full)).astype(ref.dtype)

    load_gu2.wait()
    g1a = net.send(g2.at[z1], g2_z1.at[0], "z1")
    g1b = net.send(g2.at[z3], g2_z1.at[1], "z1")
    for copy in load_dn:
        copy.wait()
    dn0 = net.send(dn_o, dn_y, "y")
    dn1 = [net.make(dnv.at[k], dn_z1.at[k], "z1") for k in range(3)]
    dn2 = [net.make(dnv.at[k], dn_z2.at[k], "z2") for k in range(3)]
    dnx, dny, dnc = [], [], []
    for k in range(3):
        spot = fin_dn.at[k, ybit]
        dnx.append(net.make(spot, spot, "x"))
        dny.append(net.make(spot, spot, "y"))
        dnc.append(net.make(fin_dn.at[k], fin_dn.at[k], "core"))

    @pl.when(~same0)
    def _():
        for k in range(2):
            dn1[k].start()

    def dn_first():
        dn0.wait_recv()
        dnv[2] = (dnv[2].astype(full) + dn_y[...].astype(full)).astype(low)

        @pl.when(~same0)
        def _():
            dn1[2].start()

    def dn_second(k):
        @pl.when(same0)
        def _():
            dn1[k].wait_recv()
            dnv[k] = (dnv[k].astype(full) + dn_z1[k].astype(full)).astype(low)

        @pl.when(same0 & ~same1)
        def _():
            dn2[k].start()

    def dn_third(k):
        @pl.when(holder)
        def _():
            dn2[k].wait_recv()
            dnv[k] = (dnv[k].astype(full) + dn_z2[k].astype(full)).astype(low)
            plus_upper(dnv.at[k], up_dn.at[k], dn_z1.at[k])
            fin_dn[k, ybit] = dnv[k]
            dnx[k].start()
            dny[k].start()

    def dn_fourth(k):
        @pl.when(level & ~holder)
        def _():
            dnx[k].wait_recv()
            dny[k].start()

    def dn_fifth(k):
        @pl.when(level)
        def _():
            dny[k].wait_recv()
            dnc[k].start()

    def dn_last(k):
        @pl.when(~level)
        def _():
            dnc[k].wait_recv()

        for y in range(2):
            at = (2 * k + y) * (chunk // 2)
            results.append(net.move(fin_dn.at[k, y], gdn_out.at[pl.ds(at, chunk // 2)]))

    results = []

    def spread_gu(k):
        own = fin_gu.at[k, xbit, core, ybit]
        return net.send(own, own, "x"), net.send(own, own, "y")

    lo, hi = pl.ds(0, chunk), pl.ds(chunk, chunk)

    def onward_gu(k, b):
        b[0].wait_recv()
        spot = fin_gu.at[k, 1 - xbit, core, ybit, :, lo]
        first_half = net.send(spot, spot, "y")
        b[1].wait_recv()
        spot = fin_gu.at[k, xbit, core, 1 - ybit, :, hi]
        return first_half, net.send(spot, spot, "x")

    def across_gu(k, d):
        d[0].wait_recv()
        d[1].wait_recv()
        return net.send(fin_gu.at[k, :, core], fin_gu.at[k, :, core], "core")

    if not upper:
        for c in load_gu:
            c.wait()
        gu_b = [spread_gu(0), spread_gu(1)]
    else:
        gu_b = []
        for k in range(2):
            load_gu[k].wait()
            up_gu_own = fin_gu.at[k, xbit, core, ybit]
            plus_upper(up_gu_own, up_gu.at[k], dp.at[pl.ds(0, half), pl.ds(0, pair)])
            gu_b.append(spread_gu(k))

    def row_of(k):
        return jnp.concatenate([small_all[i, k : k + 1, :] for i in range(4)], 1).astype(full)

    gain_one, gain_two = row_of(0), row_of(1)
    sums[...] = jnp.zeros_like(sums)
    load_first.wait()
    load_dh2.wait()
    load_e.wait()
    tile = 32

    def folded(value):
        return jnp.sum(value.reshape(value.shape[0] // 8, 8, value.shape[1]), axis=0)

    def norm_two(i, total):
        at = pl.ds(pl.multiple_of(i * tile, tile), tile)
        xf, dh = first[at], dh2[at]
        rate = lax.rsqrt(jnp.mean(xf * xf, axis=-1, keepdims=True) + epsilon)
        normed = xf * rate
        scaled = dh * gain_two
        mean = jnp.mean(scaled * normed, axis=-1, keepdims=True)
        got = e_ref[at].astype(full) + rate * (scaled - normed * mean)
        dx1[at] = got
        do_ref[at] = got.astype(low)
        return total + folded(dh * normed)

    total = lax.fori_loop(0, rows // tile, norm_two, jnp.zeros((8, width), full))
    sums[1:2, :] = jnp.sum(total, axis=0, keepdims=True)

    load_wc.wait()
    dz = first

    def back_out(i, carry):
        cols = pl.ds(pl.multiple_of(i * part, part), part)
        dz[:, cols] = outer(do_ref[...], wc[i, :, :, :, 3 * width :].reshape(part, width))
        return carry

    lax.fori_loop(0, 4, back_out, 0)
    load_zed.wait()
    load_x.wait()

    def turn_zed(i, carry):
        cols = pl.ds(pl.multiple_of(i * 256, 256), 256)
        zedt[:, cols] = zed[cols].T
        return carry

    lax.fori_loop(0, rows // 256, turn_zed, 0)

    def weight_chunk(left, right, at):
        def one(n, carry):
            cols = pl.ds(pl.multiple_of(n * 256, 256), 256)
            into = pl.ds(pl.multiple_of(at + n * 256, 256), 256)
            got = jnp.dot(left[...], right(cols), preferred_element_type=full).astype(low)
            dwc[:, :, :, :, :, into] = got.reshape(4, 2, 2, 2, part // 8, 256)
            return carry

        lax.fori_loop(0, width // 256, one, 0)

    starts_at = [3 * width, width, 0, 2 * width]

    def cols_of(i):
        return pl.ds(starts_at[i], width)

    def to_core(i):
        return net.send(dwc.at[:, :, :, 1 - core, :, cols_of(i)], cr.at[i], "core")

    weight_chunk(zedt, lambda cols: do_ref[:, cols], 3 * width)
    sc = [to_core(0)]

    g1a.wait_recv()
    g1b.wait_recv()
    g2[z2] = (g2[z2].astype(full) + g2_z1[1].astype(full)).astype(low)
    g2s = net.send(g2.at[z2], g2_z2, "z2")

    dn_first()
    dn_second(0)
    dn_second(1)

    place = me * rows + lax.broadcasted_iota(jnp.int32, (rows, 1), 0)
    starts = jnp.broadcast_to(starts_ref[...], (8, rows)).T[:, 0:1]
    keep_one = (place - 1 >= starts).astype(full)
    keep_two = (place - 2 >= starts).astype(full)
    load_gext.wait()
    load_proj.wait()
    s1[rows:] = jnp.zeros((s1.shape[0] - rows, 128), full)
    s2[rows:] = jnp.zeros((s2.shape[0] - rows, 128), full)
    dg = dh2
    row8 = lax.broadcasted_iota(jnp.int32, (8, 128), 0)

    def unmix(i, carry):
        at = pl.ds(pl.multiple_of(i * 128, 128), 128)
        cat = pl.ds(pl.multiple_of(width + i * 128, 128), 128)
        zi = i // (part // 128)
        inside = pl.ds(pl.multiple_of((i % (part // 128)) * 128, 128), 128)
        taps = small_all[zi, :, inside].astype(full)
        tap0, tap1, tap2 = taps[2:3], taps[3:4], taps[4:5]
        current, lag_one, lag_two = gext[16:, at], gext[15 : rows + 15, at], gext[14 : rows + 14, at]
        mixed = tap0 * current + keep_one * tap1 * lag_one + keep_two * tap2 * lag_two
        back = dz[:, at]
        dp[:, cat] = (back * mixed).astype(low)
        dm = back * proj[:, cat]
        t1, t2 = keep_one * dm, keep_two * dm
        for k, value in ((2, dm * current), (3, t1 * lag_one), (4, t2 * lag_two)):
            sums[k : k + 1, at] = jnp.sum(folded(value), axis=0, keepdims=True)
        s1[:rows] = tap1 * t1
        s2[:rows] = tap2 * t2
        dg[:, at] = tap0 * dm + s1[1 : rows + 1] + s2[2 : rows + 2]
        ret_send[:, at] = jnp.where(
            row8 == 6, s2[0:1], jnp.where(row8 == 7, s1[0:1] + s2[1:2], 0.0)
        )
        return carry

    lax.fori_loop(0, width // 128, unmix, 0)
    back = net.send(ret_send, ret_land, before)

    def norm_one(i, carry):
        at = pl.ds(pl.multiple_of(i * 128, 128), 128)
        xf = x_ref[at].astype(full)
        rate = lax.rsqrt(jnp.mean(xf * xf, axis=-1, keepdims=True) + epsilon)
        ht[:, at] = (xf * rate * gain_one).astype(low).T
        return carry

    lax.fori_loop(0, rows // 128, norm_one, 0)
    weight_chunk(ht, lambda cols: dp[:, pl.ds(pl.multiple_of(width + cols.start, 256), 256)], width)
    sc.append(to_core(1))

    orders = ["xy", "yx", "xy", "all"]
    def spot_of(i, zi, yi, xi):
        return (zi, yi, xi, core, slice(None), cols_of(i))

    def add_core(i):
        sc[i].wait_recv()

        def one(j, carry):
            zi, yi, xi = j // 4, (j // 2) % 2, j % 2
            spot = spot_of(i, zi, yi, xi)
            dwc[spot] = (dwc[spot].astype(full) + cr[i, zi, yi, xi].astype(full)).astype(low)
            return carry

        lax.fori_loop(0, 16, one, 0)
        cols = cols_of(i)
        if orders[i] == "xy":
            return net.send(dwc.at[:, :, 1 - xbit, core, :, cols], r1.at[i], "x")
        if orders[i] == "yx":
            return net.send(dwc.at[:, 1 - ybit, :, core, :, cols], r1.at[i], "y")
        return [
            net.send(dwc.at[:, yi, xi, core, :, cols], land, seat)
            for yi, xi, land, seat in (
                (ybit, 1 - xbit, r1.at[i, :, 0], "x"),
                (1 - ybit, xbit, r1.at[i, :, 1], "y"),
                (1 - ybit, 1 - xbit, r2.at[i], cross),
            )
        ]

    def add_first(i, copy):
        copy.wait_recv()

        def one(j, carry):
            zi, oi = j // 2, j % 2
            yi, xi = (oi, xbit) if orders[i] == "xy" else (ybit, oi)
            spot = spot_of(i, zi, yi, xi)
            dwc[spot] = (dwc[spot].astype(full) + r1[i, zi, oi].astype(full)).astype(low)
            return carry

        lax.fori_loop(0, 8, one, 0)
        cols = cols_of(i)
        if orders[i] == "xy":
            return net.send(dwc.at[:, 1 - ybit, xbit, core, :, cols], r2.at[i], "y")
        return net.send(dwc.at[:, ybit, 1 - xbit, core, :, cols], r2.at[i], "x")

    def add_second(i, copy):
        if orders[i] == "all":
            for c in copy:
                c.wait_recv()
        else:
            copy.wait_recv()

        def one(zi, carry):
            spot = spot_of(i, zi, ybit, xbit)
            got = dwc[spot].astype(full) + r2[i, zi].astype(full)
            if orders[i] == "all":
                got = got + r1[i, zi, 0].astype(full) + r1[i, zi, 1].astype(full)
            dwc[spot] = got.astype(low)
            return carry

        lax.fori_loop(0, 4, one, 0)
        return [
            net.send(dwc.at[spot_of(i, zz, ybit, xbit)], rz.at[i, k], seat)
            for k, (zz, seat) in enumerate(((z1, "z1"), (z2, "z2"), (z3, "z3")))
        ]

    def add_z(i, copies):
        for c in copies:
            c.wait_recv()
        own = fin_c.at[i, ybit, xbit, core]
        own[...] = (
            dwc[spot_of(i, z, ybit, xbit)].astype(full)
            + rz[i, 0].astype(full)
            + rz[i, 1].astype(full)
            + rz[i, 2].astype(full)
        ).astype(low)
        plus_upper(own, up_c.at[i], e_ref.at[pl.ds(0, part // 8)])
        return [net.send(own, own, seat) for seat in ("x", "y", cross)]

    def across_c(i, copies):
        for c in copies:
            c.wait_recv()
        return net.send(fin_c.at[i, :, :, core], fin_c.at[i, :, :, core], "core")

    def last_c(i, copy):
        copy.wait_recv()
        target = gout_out if i == 0 else gin_out.at[:, :, :, :, cols_of(i)]
        results.append(net.move(fin_c.at[i], target))

    def last_gu(k, copy):
        copy.wait_recv()
        for q in range(4):
            at = q * hq + k * chunk
            spot = fin_gu.at[k, q // 2, q % 2]
            results.append(net.move(spot.at[:, :, lo], ggu_out.at[:, :, pl.ds(at, chunk)]))
            results.append(
                net.move(spot.at[:, :, hi], ggu_out.at[:, :, pl.ds(hidden + at, chunk)])
            )

    a = {}
    b = {}
    a[0] = add_core(0)
    gu_d = [onward_gu(k, gu_b[k]) for k in range(2)]
    back.wait_recv()
    follows = (me < seq - 1).astype(full)
    dg[rows - 8 :] = dg[rows - 8 :] + ret_land[...] * follows

    def unproject(i, carry):
        at = pl.ds(pl.multiple_of(i * 128, 128), 128)
        xat = pl.ds(pl.multiple_of(2 * width + i * 128, 128), 128)
        dp[:, at] = (dg[:, at] * proj[:, xat]).astype(low)
        dp[:, xat] = (dg[:, at] * proj[:, at]).astype(low)
        return carry

    lax.fori_loop(0, width // 128, unproject, 0)
    weight_chunk(ht, lambda cols: dp[:, cols], 0)
    sc.append(to_core(2))
    a[1] = add_core(1)
    weight_chunk(ht, lambda cols: dp[:, pl.ds(pl.multiple_of(2 * width + cols.start, 256), 256)], 2 * width)
    sc.append(to_core(3))
    a[2] = add_core(2)
    b[0] = add_first(0, a[0])
    a[3] = add_core(3)

    g2s.wait_recv()
    own = fin_gu.at[2, xbit, core, ybit]
    own[...] = (
        g2[z].astype(full) + g2_z1[0].astype(full) + g2_z2[...].astype(full)
    ).astype(low)
    plus_upper(own, up_gu.at[2], e_ref.at[pl.ds(0, half), pl.ds(0, pair)])
    gu_b.append(spread_gu(2))
    dn_second(2)
    dn_third(0)

    load_win.wait()
    dh = dg

    def back_in(i, carry):
        cols = pl.ds(pl.multiple_of(i * part, part), part)
        dh[:, cols] = outer(dp[...], wc[i, :, :, :, : 3 * width].reshape(part, 3 * width))
        return carry

    lax.fori_loop(0, 4, back_in, 0)
    b[1] = add_first(1, a[1])
    c = {0: add_second(0, b[0])}

    def norm_back(i, total):
        at = pl.ds(pl.multiple_of(i * tile, tile), tile)
        xf = x_ref[at].astype(full)
        rate = lax.rsqrt(jnp.mean(xf * xf, axis=-1, keepdims=True) + epsilon)
        normed = xf * rate
        got = dh[at]
        scaled = got * gain_one
        mean = jnp.mean(scaled * normed, axis=-1, keepdims=True)
        out_ref[at] = (dx1[at] + rate * (scaled - normed * mean)).astype(low)
        return total + folded(got * normed)

    total = lax.fori_loop(0, rows // tile, norm_back, jnp.zeros((8, width), full))
    keep_grad = net.move(out_ref, grad_out)
    sums[0:1, :] = jnp.sum(total, axis=0, keepdims=True)
    small_core = net.send(sums, sums_core, "core")
    dn_third(1)
    b[2] = add_first(2, a[2])
    small_core.wait()
    sums[...] = sums[...] + sums_core[...]
    small_plane = [
        net.send(sums, sums_plane.at[i], seat) for i, seat in enumerate(("x", "y", cross))
    ]
    gu_c = [across_gu(k, gu_d[k]) for k in range(2)]
    dn_third(2)
    dn_fourth(0)
    c[1] = add_second(1, b[1])
    c[3] = add_second(3, a[3])
    c[2] = add_second(2, b[2])
    dn_fourth(1)
    d = {0: add_z(0, c[0])}
    gu_d.append(onward_gu(2, gu_b[2]))
    dn_fourth(2)
    dn_fifth(0)
    for copy in small_plane:
        copy.wait()
    sums[...] = sums[...] + sums_plane[0] + sums_plane[1] + sums_plane[2]
    for i, seat in enumerate(upper):
        copy = net.send(sums, sums_plane.at[3 + i], seat)
        copy.wait()
        sums[...] = sums[...] + sums_plane[3 + i]

    def slab(zz):
        return sums.at[:, pl.ds(pl.multiple_of(zz * part, part), part)]

    small_z = [
        net.send(slab(zz), sums_z.at[i], seat)
        for i, (zz, seat) in enumerate(((z1, "z1"), (z2, "z2"), (z3, "z3")))
    ]
    d[1] = add_z(1, c[1])
    d[3] = add_z(3, c[3])
    d[2] = add_z(2, c[2])
    f = {0: across_c(0, d[0])}
    last_gu(0, gu_c[0])
    last_gu(1, gu_c[1])
    dn_fifth(1)
    dn_fifth(2)
    gu_c.append(across_gu(2, gu_d[2]))
    for i in (1, 3, 2):
        f[i] = across_c(i, d[i])
    for copy in small_z:
        copy.wait()
    small_out[...] = slab(z)[...] + sums_z[0] + sums_z[1] + sums_z[2]
    keep_small = net.move(small_out, gsmall_out)
    for k in range(3):
        dn_last(k)
    for i in (0, 1, 3, 2):
        last_c(i, f[i])
    last_gu(2, gu_c[2])

    @pl.when(~same0)
    def _():
        for copy in dn1:
            copy.wait_send()

    @pl.when(same0 & ~same1)
    def _():
        for copy in dn2:
            copy.wait_send()

    @pl.when(holder)
    def _():
        for copy in dnx:
            copy.wait_send()

    @pl.when(level)
    def _():
        for copy in dny + dnc:
            copy.wait_send()

    flat = [g1a, g1b, g2s, back, dn0] + gu_c + sc
    for group in gu_b + gu_d:
        flat += list(group)
    for group in (a, b, c, d, f):
        for copies in group.values():
            flat += copies if isinstance(copies, list) else [copies]
    for copy in flat:
        copy.wait_send()
    for copy in results:
        copy.wait()
    keep_grad.wait()
    keep_small.wait()


def finish(seq, starts, small_all, x, e, first, dh2, proj, zed, gext, wc, gu0, gu1, gu2, dn, dn2):
    rows, width = first.shape
    part = width // 4
    half, pair = gu0.shape
    chunk = pair // 2
    hq = 3 * chunk
    extra = seq.bit_length() - 4
    room = max(extra, 1)
    eighth = part // 8
    shape = jax.ShapeDtypeStruct
    anyspace = pl.BlockSpec(memory_space=pl.ANY)
    vmem = pl.BlockSpec(memory_space=pltpu.VMEM)
    outs = [
        shape((rows, width), low),
        shape((2, 2, 2, eighth, 3 * width), low),
        shape((2, 2, 2, eighth, width), low),
        shape((2, half, 8 * hq), low),
        shape((hq, width), low),
        shape((8, part), full),
    ]
    v = pltpu.VMEM
    outs += [
        shape((4, room, eighth, width), low),
        shape((3, room, half, pair), low),
        shape((3, room, chunk // 2, width), low),
    ]
    scratch = [
        v((4, 4, 2, eighth, 4 * width), low),
        v((rows, width), full),
        v((rows, width), full),
        v((rows, width), low),
        v((rows, width), low),
        v((rows, 3 * width), full),
        v((rows, width), low),
        v((width, rows), low),
        v((rows + 16, width), full),
        v((rows, width), full),
        v((rows, 3 * width), low),
        v((rows + 8, 128), full),
        v((rows + 8, 128), full),
        v((4, 2, 2, 2, eighth, 4 * width), low),
        v((8, width), full),
        v((8, width), full),
        v((8, width), full),
        v((8, width), full),
        v((3 + room, 8, width), full),
        v((3, 8, part), full),
        v((8, part), full),
        v((4, 4, 2, 2, eighth, width), low),
        v((4, 4, 2, eighth, width), low),
        v((4, 4, eighth, width), low),
        v((4, 3, eighth, width), low),
        v((4, 2, 2, 2, eighth, width), low),
        v((3, 2, 2, 2, half, pair), low),
        v((3, 2, chunk // 2, width), low),
        v((4, half, pair), low),
        v((2, half, pair), low),
        v((half, pair), low),
        v((3, chunk // 2, width), low),
        v((3, chunk // 2, width), low),
        v((3, chunk // 2, width), low),
        v((chunk // 2, width), low),
        v((chunk // 2, width), low),
        pltpu.SemaphoreType.DMA((100 + 12 * extra,)),
        pltpu.SemaphoreType.DMA((100 + 12 * extra,)),
        pltpu.SemaphoreType.DMA((60 + 12 * extra,)),
    ]
    return pl.pallas_call(
        functools.partial(finish_kernel, seq),
        out_shape=outs,
        in_specs=[vmem, vmem] + [anyspace] * 13,
        out_specs=[anyspace] * len(outs),
        scratch_shapes=scratch,
        compiler_params=pltpu.CompilerParams(
            collective_id=2, has_side_effects=True, vmem_limit_bytes=63 * MIB
        ),
        name="finish",
    )(starts, small_all, x, e, first, dh2, proj, zed, gext, wc, gu0, gu1, gu2, dn, dn2)


def cast_kernel(gu_ref, dn_ref, win_ref, wout_ref, res_ref, gx_ref, small_ref, *outs):
    ggu, gdn, gin, gout, res, gx, norm_one, norm_two, taps = outs
    ggu[...] = gu_ref[...].astype(full)
    gdn[...] = dn_ref[...].astype(full)
    gin[...] = win_ref[...].astype(full)
    gout[...] = wout_ref[...].astype(full)
    res[0] = res_ref[...]
    gx[0] = gx_ref[...]
    norm_one[...] = small_ref[0:1]
    norm_two[...] = small_ref[1:2]
    taps[...] = small_ref[2:5]


def cast(gu, dn, win, wout, result, grad_x, small):
    steps = 8
    arrays = (gu, dn, win, wout, result, grad_x)

    def cut(v, lead=False):
        rows, cols = v.shape
        if lead:
            return pl.BlockSpec((1, rows // steps, cols), lambda i: (0, i, 0))
        return pl.BlockSpec((rows // steps, cols), lambda i: (i, 0))

    def whole(shape):
        return pl.BlockSpec(shape, lambda i: (0, 0))

    part = small.shape[1]
    rows = ((1, part), (1, part), (3, part))
    moved = sum(v.size for v in arrays)
    return pl.pallas_call(
        cast_kernel,
        grid=(steps,),
        out_shape=[jax.ShapeDtypeStruct(v.shape, full) for v in arrays[:4]]
        + [jax.ShapeDtypeStruct((1, *v.shape), low) for v in arrays[4:]]
        + [jax.ShapeDtypeStruct(r, full) for r in rows],
        in_specs=[cut(v) for v in arrays] + [whole(small.shape)],
        out_specs=[cut(v) for v in arrays[:4]]
        + [cut(v, True) for v in arrays[4:]]
        + [whole(r) for r in rows],
        cost_estimate=pl.CostEstimate(flops=0, bytes_accessed=6 * moved, transcendentals=0),
        compiler_params=pltpu.CompilerParams(vmem_limit_bytes=63 * MIB),
        name="cast",
    )(*arrays, small)


def build(seq):
    def local(
        tokens,
        doc_start,
        norm1_gain,
        in_weight,
        conv_weight,
        out_weight,
        norm2_gain,
        gate_up_weight,
        down_weight,
        out_grad,
    ):
        x, cot = tokens[0], out_grad[0]
        starts = doc_start
        hq = down_weight.shape[0]
        small = (norm1_gain[None], norm2_gain[None], conv_weight.T)
        w_c, w_gu, w_down, cot_all, second_all, proj, first, zed, gext, small_all = gather(
            seq, x, cot, starts, *small, in_weight, out_weight, gate_up_weight, down_weight
        )
        result, dh2, gu0, gu1, gu2, dn, dn2, _ = feed(
            seq, second_all, cot_all, w_gu, w_down.reshape(hq, x.shape[1]), first
        )
        grad_x, grad_in, grad_out, grad_gu, grad_down, grad_small, *_ = finish(
            seq, starts, small_all, x, cot, first, dh2, proj, zed, gext, w_c, gu0, gu1, gu2, dn, dn2
        )
        grad_gu, grad_down, grad_in, grad_out, result, grad_x, norm_one, norm_two, taps = cast(
            grad_gu.reshape(gate_up_weight.shape),
            grad_down,
            grad_in.reshape(in_weight.shape),
            grad_out.reshape(out_weight.shape),
            result,
            grad_x,
            grad_small,
        )
        return (
            result,
            grad_x,
            norm_one[0],
            grad_in,
            taps.T,
            grad_out,
            norm_two[0],
            grad_gu,
            grad_down,
        )

    return local


def solution(mesh):
    in_specs = (
        P("wsh", "seq", None),
        P("wsh", "seq"),
        P("wsh"),
        P("wsh", None),
        P("wsh", None),
        P("wsh", None),
        P("wsh"),
        P("wsh", None),
        P("wsh", None),
        P("wsh", "seq", None),
    )
    out_specs = (
        P("wsh", "seq", None),
        P("wsh", "seq", None),
        P("wsh"),
        P("wsh", None),
        P("wsh", None),
        P("wsh", None),
        P("wsh"),
        P("wsh", None),
        P("wsh", None),
    )
    local = build(mesh.shape["seq"])
    return jax.shard_map(local, mesh=mesh, in_specs=in_specs, out_specs=out_specs, check_vma=False)
```

```python
import functools
import jax
import jax.numpy as jnp
from jax import lax
from jax.experimental import pallas as pl
from jax.experimental.pallas import tpu as pltpu
from jax.sharding import PartitionSpec as P

low = jnp.bfloat16
full = jnp.float32
MESH = pl.DeviceIdType.MESH
epsilon = 1e-06
MIB = 1 << 20


def mirrored(index, weight):
    return index + weight - 2 * weight * ((index // weight) % 2)


class Net:
    def __init__(self, me, z, send_sems, recv_sems, local_sems):
        self.me, self.z = me, z
        self.send_sems, self.recv_sems, self.local_sems = send_sems, recv_sems, local_sems
        self.count = self.local_count = 0

    def seat(self, name):
        me, z = self.me, self.z
        return {
            "core": {"seq": mirrored(me, 1), "wsh": z},
            "x": {"seq": mirrored(me, 2), "wsh": z},
            "y": {"seq": mirrored(me, 4), "wsh": z},
            "z1": {"seq": me, "wsh": mirrored(z, 1)},
            "z2": {"seq": me, "wsh": mirrored(z, 2)},
            "z3": {"seq": me, "wsh": 3 - z},
        }[name]

    def make(self, src, dst, seat, k=None):
        if k is None:
            k = self.count
            self.count += 1
        return pltpu.make_async_remote_copy(
            src_ref=src,
            dst_ref=dst,
            send_sem=self.send_sems.at[k],
            recv_sem=self.recv_sems.at[k],
            device_id=self.seat(seat) if isinstance(seat, str) else seat,
            device_id_type=MESH,
        )

    def send(self, src, dst, seat):
        copy = self.make(src, dst, seat)
        copy.start()
        return copy

    def move(self, src, dst):
        k = self.local_count
        self.local_count += 1
        copy = pltpu.make_async_copy(src, dst, self.local_sems.at[k])
        copy.start()
        return copy


def greet(seats):
    barrier = pltpu.get_barrier_semaphore()
    for seat in seats:
        pl.semaphore_signal(barrier, inc=1, device_id=seat, device_id_type=MESH)
    pl.semaphore_wait(barrier, len(seats))


def inner(left, right):
    return lax.dot_general(left, right, (((0,), (0,)), ((), ())), preferred_element_type=full)


def outer(left, right):
    return lax.dot_general(left, right, (((1,), (1,)), ((), ())), preferred_element_type=full)


def chunk_sizes(hq):
    chunk = hq // 3
    return chunk, 2 * chunk


def gather_kernel(
    seq,
    x_hbm, e_hbm, starts_ref, norm_one_ref, norm_two_ref, taps_ref, win_hbm, wout_hbm, wgu_hbm, wdn_hbm,
    wc_out, wgu_out, wdn_out, e_out, h2_out, proj_out, first_out, zed_out, gext_out, small_out,
    wc, ownf, winf, woutf, wguf, wdnf, wgu_own, wdn_own, x_ref, h_ref, proj, gext, zed, first, h2, small_all, small_own,
    send_sems, recv_sems, local_sems,
):
    me, z = lax.axis_index("seq"), lax.axis_index("wsh")
    net = Net(me, z, send_sems, recv_sems, local_sems)
    core, xbit, ybit = me % 2, (me // 2) % 2, (me // 4) % 2
    quarter = me % 4
    rows, width = x_hbm.shape
    part = width // 4
    hq = 6 * wdn_hbm.shape[2]
    hidden = 4 * hq
    half = part // 2
    z1, z2, z3 = mirrored(z, 1), mirrored(z, 2), 3 - z
    after = {"seq": lax.rem(me + 1, seq), "wsh": z}
    before = {"seq": lax.rem(me + seq - 1, seq), "wsh": z}

    piece = part // 8
    turn = (ybit * 2 + xbit) * 2 + core
    mine = pl.ds(pl.multiple_of(turn * piece, piece), piece)
    load_own = [
        net.move(win_hbm.at[mine], ownf.at[:, pl.ds(0, 3 * width)]),
        net.move(wout_hbm.at[mine], ownf.at[:, pl.ds(3 * width, width)]),
    ]
    load_x = net.move(x_hbm, x_ref.at[pl.ds(16, rows)])
    chunk, pair = chunk_sizes(hq)
    load_gu = []
    for k in range(3):
        for base, shift in ((quarter * hq, 0), (hidden + quarter * hq, chunk)):
            cut = pl.ds(pl.multiple_of(base + k * chunk, 128), chunk)
            load_gu.append(
                net.move(wgu_hbm.at[:, cut], wguf.at[:, pl.ds(k * pair + shift, chunk)])
            )
    load_win = net.move(win_hbm, winf)
    load_wout = net.move(wout_hbm, woutf)
    load_dn = net.move(wdn_hbm, wdnf)
    keep_e = net.move(e_hbm, e_out.at[0])
    small_own[...] = jnp.zeros_like(small_own)
    small_own[0:1] = norm_one_ref[...].astype(low).astype(full)
    small_own[1:2] = norm_two_ref[...].astype(low).astype(full)
    small_own[2:5] = taps_ref[...].astype(low).astype(full)
    small_all[z] = small_own[...].astype(low)
    for copy in load_own:
        copy.wait()
    spot = ybit * 2 + xbit
    spot_x = ybit * 2 + 1 - xbit
    spot_y = (1 - ybit) * 2 + xbit
    wc[z, spot, core] = ownf[...].astype(low)

    greet([net.seat(n) for n in ("core", "x", "y", "z1", "z2", "z3")] + [before])

    cols = [pl.ds(0, 2 * width), pl.ds(2 * width, 2 * width)]

    def own(zz):
        return wc.at[zz, spot, core]

    a1 = net.send(own(z), own(z), "z1")
    a2 = net.send(own(z), own(z), "z2")
    smalls = [net.send(small_all.at[z], small_all.at[z], n) for n in ("z1", "z2", "z3")]
    halo = net.send(x_hbm.at[pl.ds(rows - 16, 16)], x_ref.at[pl.ds(0, 16)], after)

    for copy in load_gu:
        copy.wait()
    wgu_own[...] = wguf[...].astype(low)
    keep_gu = net.move(wgu_own, wgu_out.at[z])
    load_win.wait()
    load_wout.wait()

    def cast_block(i, carry):
        @pl.when(i != turn)
        def _():
            at = pl.ds(pl.multiple_of(i * piece, piece), piece)
            wc[z, i // 2, i % 2, :, : 3 * width] = winf[at].astype(low)
            wc[z, i // 2, i % 2, :, 3 * width :] = woutf[at].astype(low)

        return carry

    lax.fori_loop(0, 8, cast_block, 0)
    load_dn.wait()

    def cast_dn(i, carry):
        wdn_own[i // 2, i % 2] = wdnf[i // 2, i % 2].astype(low)
        return carry

    lax.fori_loop(0, 6, cast_dn, 0)

    def spread(zz):
        return net.send(own(zz), own(zz), "x"), net.send(own(zz), own(zz), "y")

    def onward(zz, b):
        b[0].wait_recv()
        place = wc.at[zz, spot_x, core, :, cols[0]]
        d0 = net.send(place, place, "y")
        b[1].wait_recv()
        place = wc.at[zz, spot_y, core, :, cols[1]]
        return d0, net.send(place, place, "x")

    def across(zz, b, d):
        d[0].wait_recv()
        d[1].wait_recv()
        return net.send(wc.at[zz, :, core], wc.at[zz, :, core], "core")

    a1.wait_recv()
    b1 = spread(z1)
    a2.wait_recv()
    a3 = net.send(own(z2), own(z2), "z1")
    b2 = spread(z2)

    def gu(zz, yy, k):
        at = pl.ds(pl.multiple_of(yy * half, half), half)
        return wgu_out.at[zz, at, pl.ds(k * pair, pair)]

    f1, f2, f3, g1, g2, g3 = [], [], [], [], [], []
    for k in range(3):
        source = wgu_own.at[
            pl.ds(pl.multiple_of(ybit * half, half), half), pl.ds(k * pair, pair)
        ]
        f1.append(net.send(source, gu(z, ybit, k), "z1"))
        f2.append(net.send(source, gu(z, ybit, k), "z2"))

    same0 = (z % 2) == (quarter % 2)
    same1 = (z // 2) == (quarter // 2)
    holder = same0 & same1
    dn2, dn1a, dn1b, dny = [], [], [], []
    for k in range(3):
        source = wdn_own.at[k, ybit]
        target = wdn_out.at[k, ybit]
        dn2.append(net.make(source, target, "z2"))
        dn1a.append(net.make(source, target, "z1"))
        dn1b.append(net.make(target, target, "z1", net.count - 1))
        dny.append(net.make(target, target, "y"))
    keep_dn = pltpu.make_async_copy(wdn_own, wdn_out, local_sems.at[24])

    @pl.when(holder)
    def _():
        for k in range(3):
            dn2[k].start()
        keep_dn.start()

    def pass_gu(k):
        f1[k].wait_recv()
        g1.append(net.send(gu(z1, ybit, k), gu(z1, ybit, k), "y"))
        f2[k].wait_recv()
        f3.append(net.send(gu(z2, ybit, k), gu(z2, ybit, k), "z1"))
        g2.append(net.send(gu(z2, ybit, k), gu(z2, ybit, k), "y"))

    def pass_far(k):
        f3[k].wait_recv()
        g3.append(net.send(gu(z3, ybit, k), gu(z3, ybit, k), "y"))

    for copy in smalls:
        copy.wait_recv()
    load_x.wait()
    halo.wait_recv()

    def row_of(k):
        return jnp.concatenate([small_all[i, k : k + 1, :] for i in range(4)], 1).astype(full)

    gain_one, gain_two = row_of(0), row_of(1)

    def norm_one(i, carry):
        at = pl.ds(pl.multiple_of(i * 176, 16), 176)
        xf = x_ref[at].astype(full)
        rate = lax.rsqrt(jnp.mean(xf * xf, axis=-1, keepdims=True) + epsilon)
        h_ref[at] = (xf * rate * gain_one).astype(low)
        return carry

    lax.fori_loop(0, (rows + 16) // 176, norm_one, 0)
    d1 = onward(z1, b1)
    d2 = onward(z2, b2)
    a3.wait_recv()
    b3 = spread(z3)

    def pass_dn(k):
        @pl.when(same0 & ~same1)
        def _():
            dn2[k].wait_recv()
            dn1b[k].start()
            dny[k].start()

        @pl.when(~same0)
        def _():
            dn1a[k].wait_recv()
            dny[k].start()

    c1 = across(z1, b1, d1)
    c2 = across(z2, b2, d2)
    d3 = onward(z3, b3)
    pass_gu(0)
    c3 = across(z3, b3, d3)

    @pl.when(holder)
    def _():
        for k in range(3):
            dn1a[k].start()

    for c in (c1, c2, c3):
        c.wait_recv()
    ex = net.send(e_hbm, e_out.at[1], "x")
    ec = net.send(e_hbm, e_out.at[2], "core")
    pass_gu(1)

    def project(i, carry):
        at = pl.ds(pl.multiple_of(i * 512, 512), 512)
        proj[:, at] = jnp.dot(
            h_ref[...], wc[:, :, :, :, at].reshape(width, 512), preferred_element_type=full
        )
        return carry

    lax.fori_loop(0, 6, project, 0)
    keep_wc = net.move(wc, wc_out)
    keep_proj = net.move(proj.at[pl.ds(16, rows)], proj_out)

    pass_gu(2)
    place = me * rows + lax.broadcasted_iota(jnp.int32, (rows, 1), 0)
    starts = jnp.broadcast_to(starts_ref[...], (8, rows)).T[:, 0:1]
    keep_one = (place - 1 >= starts).astype(full)
    keep_two = (place - 2 >= starts).astype(full)
    cw = 128
    def mix(i, carry):
        at = pl.ds(pl.multiple_of(i * cw, cw), cw)
        xat = pl.ds(pl.multiple_of(2 * width + i * cw, cw), cw)
        cat = pl.ds(pl.multiple_of(width + i * cw, cw), cw)
        gext[:, at] = (proj[:, at] * proj[:, xat]).astype(low).astype(full)
        zi = i // (part // cw)
        inside = pl.ds(pl.multiple_of((i % (part // cw)) * cw, cw), cw)
        taps = small_all[zi, :, inside].astype(full)
        mixed = (
            taps[2:3] * gext[16:, at]
            + keep_one * taps[3:4] * gext[15 : rows + 15, at]
            + keep_two * taps[4:5] * gext[14 : rows + 14, at]
        )
        zed[:, at] = (proj[16:, cat] * mixed).astype(low)
        return carry

    lax.fori_loop(0, width // cw, mix, 0)
    keep_zed = net.move(zed, zed_out)
    keep_gext = net.move(gext, gext_out)

    pass_dn(0)
    pass_far(0)
    pass_dn(1)

    def project_out(i, carry):
        at = pl.ds(pl.multiple_of(i * 512, 512), 512)
        wat = pl.ds(pl.multiple_of(3 * width + i * 512, 512), 512)
        first[:, at] = x_ref[16:, at].astype(full) + jnp.dot(
            zed[...], wc[:, :, :, :, wat].reshape(width, 512), preferred_element_type=full
        )
        return carry

    lax.fori_loop(0, 2, project_out, 0)
    keep_first = net.move(first, first_out)
    pass_far(1)

    def norm_two(i, carry):
        at = pl.ds(pl.multiple_of(i * 128, 128), 128)
        xf = first[at]
        rate = lax.rsqrt(jnp.mean(xf * xf, axis=-1, keepdims=True) + epsilon)
        h2[at] = (xf * rate * gain_two).astype(low)
        return carry

    lax.fori_loop(0, rows // 128, norm_two, 0)
    keep_h2 = net.move(h2, h2_out.at[0])
    hx = net.send(h2, h2_out.at[1], "x")
    hc = net.send(h2, h2_out.at[2], "core")
    keep_small = net.move(small_all, small_out)

    pass_far(2)
    ex.wait_recv()
    exc = net.send(e_out.at[1], e_out.at[3], "core")
    pass_dn(2)
    hx.wait_recv()
    hxc = net.send(h2_out.at[1], h2_out.at[3], "core")
    for c in (*g1, *g2, *g3, ec, exc, hc, hxc):
        c.wait_recv()

    @pl.when(~holder)
    def _():
        for copy in dny:
            copy.wait()

    @pl.when(holder)
    def _():
        for copy in dn2 + dn1a:
            copy.wait_send()
        keep_dn.wait()

    @pl.when(same0 & ~same1)
    def _():
        for copy in dn1b:
            copy.wait_send()

    for c in (
        *smalls, halo, a1, a2, a3, *b1, *b2, *b3, *d1, *d2, *d3, c1, c2, c3,
        *f1, *f2, *f3, *g1, *g2, *g3, ex, ec, exc, hx, hc, hxc,
    ):
        c.wait_send()
    for c in (keep_e, keep_gu, keep_wc, keep_proj, keep_zed, keep_gext, keep_first, keep_h2, keep_small):
        c.wait()


def gather(seq, x, e, starts, norm_one, norm_two, taps, win, wout, wgu, wdn):
    rows, width = x.shape
    part = width // 4
    hq = wdn.shape[0]
    thirds = (3, 2, hq // 6, width)
    wdn = wdn.reshape(thirds)
    shape = jax.ShapeDtypeStruct
    anyspace = pl.BlockSpec(memory_space=pl.ANY)
    vmem = pl.BlockSpec(memory_space=pltpu.VMEM)
    conv = (4, 4, 2, part // 8, 4 * width)
    outs = [
        shape(conv, low),
        shape((4, part, 2 * hq), low),
        shape(thirds, low),
        shape((4, rows, width), low),
        shape((4, rows, width), low),
        shape((rows, 3 * width), full),
        shape((rows, width), full),
        shape((rows, width), low),
        shape((rows + 16, width), full),
        shape((4, 16, part), low),
    ]
    scratch = [
        pltpu.VMEM(conv, low),
        pltpu.VMEM((part // 8, 4 * width), full),
        pltpu.VMEM((part, 3 * width), full),
        pltpu.VMEM((part, width), full),
        pltpu.VMEM((part, 2 * hq), full),
        pltpu.VMEM(thirds, full),
        pltpu.VMEM((part, 2 * hq), low),
        pltpu.VMEM(thirds, low),
        pltpu.VMEM((rows + 16, width), low),
        pltpu.VMEM((rows + 16, width), low),
        pltpu.VMEM((rows + 16, 3 * width), full),
        pltpu.VMEM((rows + 16, width), full),
        pltpu.VMEM((rows, width), low),
        pltpu.VMEM((rows, width), full),
        pltpu.VMEM((rows, width), low),
        pltpu.VMEM((4, 16, part), low),
        pltpu.VMEM((16, part), full),
        pltpu.SemaphoreType.DMA((64,)),
        pltpu.SemaphoreType.DMA((64,)),
        pltpu.SemaphoreType.DMA((26,)),
    ]
    return pl.pallas_call(
        functools.partial(gather_kernel, seq),
        out_shape=outs,
        in_specs=[anyspace, anyspace] + [vmem] * 4 + [anyspace] * 4,
        out_specs=[anyspace] * len(outs),
        scratch_shapes=scratch,
        compiler_params=pltpu.CompilerParams(
            collective_id=0, has_side_effects=True, vmem_limit_bytes=56 * MIB
        ),
        name="gather",
    )(x, e, starts, norm_one, norm_two, taps, win, wout, wgu, wdn)


def feed_kernel(
    seq,
    h2_hbm, e_hbm, wgu_hbm, wdn_hbm, first_hbm,
    result_out, dh2_out, gu0_out, gu1_out, gu2_out, dn_out, dn2_out, land_out,
    h2, h2t, e, wgu, wdn, a, at_ref, du, u, da, dgu, ddn, send_a, send_b, send_x, send_o, temp, acc, acc_out,
    gu0_y, gu2_y, dn_y, gu0_z1, gu0_z2, gu1_z1, gu1_z2, gu0_s, gu1_s, gu1_t, gu0_f,
    send_sems, recv_sems, local_sems,
):
    me, z = lax.axis_index("seq"), lax.axis_index("wsh")
    net = Net(me, z, send_sems, recv_sems, local_sems)
    ybit = (me // 4) % 2
    rows, width = first_hbm.shape
    hq = wdn.shape[0]
    chunk, pair = chunk_sizes(hq)
    part = width // 4
    half = part // 2
    z1, z2, z3 = mirrored(z, 1), mirrored(z, 2), 3 - z
    block = 4 * rows

    load_h2, load_e, load_gu, load_dn = [], [], [], []

    def load_block(j):
        load_h2.append(net.move(h2_hbm.at[j], h2.at[pl.ds(j * rows, rows)]))
        load_e.append(net.move(e_hbm.at[j], e.at[pl.ds(j * rows, rows)]))

    def load_chunk(k):
        pcols, ccols = pl.ds(k * pair, pair), pl.ds(k * chunk, chunk)
        for i in range(4):
            load_gu.append(net.move(wgu_hbm.at[i, :, pcols], wgu.at[pl.ds(i * part, part), pcols]))
        load_dn.append(net.move(wdn_hbm.at[ccols], wdn.at[ccols]))

    load_chunk(0)
    for j in range(4):
        load_block(j)
    load_chunk(1)
    load_chunk(2)
    load_first = net.move(first_hbm, acc_out)
    greet([net.seat(n) for n in ("core", "x", "y", "z1", "z2")])

    def turn(j, carry):
        at = pl.ds(pl.multiple_of(j * 256, 256), 256)
        h2t[:, at] = h2[at].T
        return carry

    def forward(k, slots, step):
        pcols, ccols = pl.ds(k * pair, pair), pl.ds(k * chunk, chunk)

        def one(i, carry):
            j = slots + i * step
            at = pl.ds(pl.multiple_of(j * rows, rows), rows)
            u[...] = jnp.dot(h2[at], wgu[:, pcols], preferred_element_type=full)
            da[...] = outer(e[at], wdn[ccols])

            def piece(r, carry):
                rr = pl.ds(pl.multiple_of(r * 64, 64), 64)
                tt = pl.ds(pl.multiple_of(j * rows + r * 64, 64), 64)
                gate, upper, back = u[rr, :chunk], u[rr, chunk:], da[rr]
                sigma = jax.nn.sigmoid(gate)
                swish = gate * sigma
                a[tt, ccols] = (swish * upper).astype(low)
                du[tt, pl.ds(k * pair, chunk)] = (
                    back * upper * (sigma * (1.0 + gate * (1.0 - sigma)))
                ).astype(low)
                du[tt, pl.ds(k * pair + chunk, chunk)] = (back * swish).astype(low)
                return carry

            lax.fori_loop(0, rows // 64, piece, 0)
            return carry

        lax.fori_loop(0, 4 // step, one, 0)

    def weights(k):
        def turn_a(j, carry):
            at = pl.ds(pl.multiple_of(j * rows, rows), rows)
            at_ref[:, at] = a[at, pl.ds(k * chunk, chunk)].T
            return carry

        lax.fori_loop(0, 4, turn_a, 0)

        def gate_up(n, carry):
            cols = pl.ds(pl.multiple_of(k * pair + n * 256, 256), 256)
            got = jnp.dot(h2t[...], du[:, cols], preferred_element_type=full).astype(low)
            dgu[:, :, :, cols] = got.reshape(4, 2, half, 256)
            return carry

        lax.fori_loop(0, pair // 256, gate_up, 0)

        def down(n, carry):
            cols = pl.ds(pl.multiple_of(n * 512, 512), 512)
            got = jnp.dot(at_ref[...], e[:, cols], preferred_element_type=full).astype(low)
            ddn[k, :, :, cols] = got.reshape(2, chunk // 2, 512)
            return carry

        lax.fori_loop(0, width // 512, down, 0)

    def cols_of(k):
        return pl.ds(k * pair, pair)

    for copy in load_gu[:4] + load_dn[:1]:
        copy.wait()
    for j in range(4):
        load_h2[j].wait()
        load_e[j].wait()
        forward(0, j, 4)
    lax.fori_loop(0, block // 256, turn, 0)
    weights(0)
    for copy in load_gu[4:] + load_dn[1:]:
        copy.wait()
    y0 = net.send(dgu.at[:, 1 - ybit, :, cols_of(0)], gu0_y, "y")
    yd0 = net.send(ddn.at[0, 1 - ybit], dn_y.at[0], "y")
    forward(1, 0, 1)
    forward(2, 1, 2)

    def sum_rows(put, count, step):
        def one(i, carry):
            put(pl.ds(pl.multiple_of(i * step, step), step))
            return carry

        lax.fori_loop(0, count // step, one, 0)

    def accumulate(target):
        def go(at):
            target[at] = target[at] + temp[at].astype(full)

        return go

    def keep(cols, value):
        acc[:, cols] = value

    def more(cols, value):
        acc_out[:, cols] = acc_out[:, cols] + value

    def gu0_sum(i, carry):
        gu0_s[i] = (dgu[i, ybit, :, cols_of(0)].astype(full) + gu0_y[i].astype(full)).astype(low)
        return carry

    def gu1_sum(i, carry):
        gu1_t[i] = (dgu[z2, i, :, cols_of(1)].astype(full) + gu1_z1[1, i].astype(full)).astype(low)
        gu1_s[i] = (dgu[z, i, :, cols_of(1)].astype(full) + gu1_z1[0, i].astype(full)).astype(low)
        return carry

    def gu1_more(i, carry):
        gu1_s[i] = (gu1_s[i].astype(full) + gu1_z2[i].astype(full)).astype(low)
        return carry

    def finish(at):
        send_a[at] = (acc_out[at] + temp[at].astype(full)).astype(low)

    def grad_rows(j, put):
        at = pl.ds(j * rows, rows)

        def one(n, carry):
            cols = pl.ds(pl.multiple_of(n * 256, 256), 256)
            put(cols, outer(du[at], wgu[cols]))
            return carry

        lax.fori_loop(0, width // 256, one, 0)

    def out_rows(j, put):
        at = pl.ds(j * rows, rows)

        def one(n, carry):
            cols = pl.ds(pl.multiple_of(n * 256, 256), 256)
            put(cols, jnp.dot(a[at], wdn[:, cols], preferred_element_type=full))
            return carry

        lax.fori_loop(0, width // 256, one, 0)

    def store(ref):
        def put(cols, value):
            ref[:, cols] = value.astype(low)

        return put

    def add(target, other):
        def put(cols, value):
            target[:, cols] = (value + other[:, cols].astype(full)).astype(target.dtype)

        return put

    def fetch(j):
        copy = net.move(land_out.at[j], temp)
        copy.wait()

    grad_rows(3, store(send_a))
    ga = net.send(send_a, land_out.at[0], "core")
    out_rows(3, store(send_b))
    oa = net.send(send_b, land_out.at[3], "core")
    ga.wait_recv()
    fetch(0)
    grad_rows(1, add(send_x, temp))
    gx = net.send(send_x, land_out.at[1], "x")
    weights(1)
    m1 = net.send(dgu.at[z1, :, :, cols_of(1)], gu1_z1.at[0], "z1")
    m2 = net.send(dgu.at[z3, :, :, cols_of(1)], gu1_z1.at[1], "z1")
    yd1 = net.send(ddn.at[1, 1 - ybit], dn_y.at[1], "y")
    oa.wait_recv()
    fetch(3)
    out_rows(1, add(send_o, temp))
    ox = net.send(send_o, land_out.at[4], "x")
    forward(2, 0, 2)
    y0.wait_recv()
    lax.fori_loop(0, 4, gu0_sum, 0)
    n1 = net.send(gu0_s.at[z1], gu0_z1.at[0], "z1")
    n2 = net.send(gu0_s.at[z3], gu0_z1.at[1], "z1")
    weights(2)
    y2 = net.send(dgu.at[:, 1 - ybit, :, cols_of(2)], gu2_y, "y")
    keep_dn2 = net.move(ddn.at[2], dn2_out)
    m1.wait_recv()
    m2.wait_recv()
    lax.fori_loop(0, 2, gu1_sum, 0)
    m3 = net.send(gu1_t, gu1_z2, "z2")
    ga.wait_send()
    grad_rows(2, store(send_a))
    gb = net.send(send_a, land_out.at[2], "core")
    n1.wait_recv()
    n2.wait_recv()
    gu0_f[1] = (gu0_s[z2].astype(full) + gu0_z1[1].astype(full)).astype(low)
    n3 = net.send(gu0_f.at[1], gu0_z2, "z2")
    oa.wait_send()
    out_rows(2, store(send_b))
    ob = net.send(send_b, land_out.at[5], "core")
    grad_rows(0, keep)
    gb.wait_recv()
    fetch(2)
    sum_rows(accumulate(acc), rows, 64)
    load_first.wait()
    out_rows(0, more)
    ob.wait_recv()
    fetch(5)
    sum_rows(accumulate(acc_out), rows, 64)
    m3.wait_recv()
    lax.fori_loop(0, 2, gu1_more, 0)
    keep_gu1 = net.move(gu1_s, gu1_out)
    gx.wait_recv()
    fetch(1)
    sum_rows(accumulate(acc), rows, 64)
    keep_dh2 = net.move(acc, dh2_out)
    n3.wait_recv()
    gu0_f[0] = (
        gu0_s[z].astype(full) + gu0_z1[0].astype(full) + gu0_z2[...].astype(full)
    ).astype(low)
    keep_gu0 = net.move(gu0_f.at[0], gu0_out)
    ox.wait_recv()
    fetch(4)
    gb.wait_send()
    sum_rows(finish, rows, 64)
    keep_result = net.move(send_a, result_out)

    yd0.wait_recv()
    yd1.wait_recv()
    y2.wait_recv()

    def gu2_sum(i, carry):
        dgu[i, ybit, :, cols_of(2)] = (
            dgu[i, ybit, :, cols_of(2)].astype(full) + gu2_y[i].astype(full)
        ).astype(low)
        return carry

    lax.fori_loop(0, 4, gu2_sum, 0)
    keep_gu2 = net.move(dgu.at[:, ybit, :, cols_of(2)], gu2_out)

    def dn_sum(i, carry):
        ddn[i, ybit] = (ddn[i, ybit].astype(full) + dn_y[i].astype(full)).astype(low)
        return carry

    lax.fori_loop(0, 2, dn_sum, 0)
    keep_dn = net.move(ddn.at[pl.ds(0, 2), ybit], dn_out)
    for c in (y0, yd0, m1, m2, yd1, y2, n1, n2, m3, n3, ox, ob, gx):
        c.wait_send()
    for c in (keep_dh2, keep_gu0, keep_result, keep_gu2, keep_dn, keep_dn2, keep_gu1):
        c.wait()


def feed(seq, h2_all, e_all, wgu, wdn, first):
    rows, width = first.shape
    part = width // 4
    half = part // 2
    hq = wdn.shape[0]
    chunk, pair = chunk_sizes(hq)
    shape = jax.ShapeDtypeStruct
    anyspace = pl.BlockSpec(memory_space=pl.ANY)
    outs = [
        shape((rows, width), low),
        shape((rows, width), full),
        shape((half, pair), low),
        shape((2, half, pair), low),
        shape((4, half, pair), low),
        shape((2, chunk // 2, width), low),
        shape((2, chunk // 2, width), low),
        shape((6, rows, width), low),
    ]
    v = pltpu.VMEM
    scratch = [
        v((4 * rows, width), low),
        v((width, 4 * rows), low),
        v((4 * rows, width), low),
        v((width, 2 * hq), low),
        v((hq, width), low),
        v((4 * rows, hq), low),
        v((chunk, 4 * rows), low),
        v((4 * rows, 2 * hq), low),
        v((rows, pair), full),
        v((rows, chunk), full),
        v((4, 2, half, 2 * hq), low),
        v((3, 2, chunk // 2, width), low),
        v((rows, width), low),
        v((rows, width), low),
        v((rows, width), low),
        v((rows, width), low),
        v((rows, width), low),
        v((rows, width), full),
        v((rows, width), full),
        v((4, half, pair), low),
        v((4, half, pair), low),
        v((2, chunk // 2, width), low),
        v((2, half, pair), low),
        v((half, pair), low),
        v((2, 2, half, pair), low),
        v((2, half, pair), low),
        v((4, half, pair), low),
        v((2, half, pair), low),
        v((2, half, pair), low),
        v((2, half, pair), low),
        pltpu.SemaphoreType.DMA((24,)),
        pltpu.SemaphoreType.DMA((24,)),
        pltpu.SemaphoreType.DMA((44,)),
    ]
    return pl.pallas_call(
        functools.partial(feed_kernel, seq),
        out_shape=outs,
        in_specs=[anyspace] * 5,
        out_specs=[anyspace] * len(outs),
        scratch_shapes=scratch,
        compiler_params=pltpu.CompilerParams(
            collective_id=1, has_side_effects=True, vmem_limit_bytes=63 * MIB
        ),
        name="feed",
    )(h2_all, e_all, wgu, wdn, first)


def finish_kernel(
    seq,
    starts_ref, small_all, x_hbm, e_hbm, first_hbm, dh2_hbm, proj_hbm, zed_hbm, gext_hbm, wc_hbm,
    gu0_hbm, gu1_hbm, gu2_hbm, dn_hbm, dn2_hbm,
    grad_out, gin_out, gout_out, ggu_out, gdn_out, gsmall_out, up_c, up_gu, up_dn,
    wc, first, dh2, x_ref, e_ref, proj, zed, ht, gext, dx1, dp, s1, s2, dwc,
    ret_send, ret_land, sums, sums_core, sums_plane, sums_z, small_out,
    cr, r1, r2, rz, fin_c, fin_gu, fin_dn, g2, g2_z1, g2_z2, g1_o, g1_y, dnv, dn_z1, dn_z2, dn_o, dn_y,
    send_sems, recv_sems, local_sems,
):
    me, z = lax.axis_index("seq"), lax.axis_index("wsh")
    net = Net(me, z, send_sems, recv_sems, local_sems)
    core, xbit, ybit = me % 2, (me // 2) % 2, (me // 4) % 2
    quarter = me % 4
    rows, width = first.shape
    part = width // 4
    half = part // 2
    chunk = dnv.shape[1] * 2
    pair = 2 * chunk
    hq = 3 * chunk
    hidden = 4 * hq
    z1, z2, z3 = mirrored(z, 1), mirrored(z, 2), 3 - z
    after = {"seq": lax.rem(me + 1, seq), "wsh": z}
    before = {"seq": lax.rem(me + seq - 1, seq), "wsh": z}
    cross = {"seq": mirrored(mirrored(me, 2), 4), "wsh": z}
    upper = [
        {"seq": mirrored(me, 1 << bit), "wsh": z} for bit in range(3, seq.bit_length() - 1)
    ]
    same0 = (z % 2) == (quarter % 2)
    same1 = (z // 2) == (quarter // 2)
    holder = same0 & same1
    level = core == z % 2

    load_gu2 = net.move(gu2_hbm, g2)
    load_dn = [
        net.move(dn2_hbm.at[ybit], dnv.at[2]),
        net.move(dn2_hbm.at[1 - ybit], dn_o),
        net.move(dn_hbm, dnv.at[pl.ds(0, 2)]),
    ]
    load_gu = [
        net.move(gu0_hbm, fin_gu.at[0, xbit, core, ybit]),
        net.move(gu1_hbm.at[ybit], fin_gu.at[1, xbit, core, ybit]),
        net.move(gu1_hbm.at[1 - ybit], g1_o),
    ]
    load_first = net.move(first_hbm, first)
    load_dh2 = net.move(dh2_hbm, dh2)
    load_e = net.move(e_hbm, e_ref)
    outer_cols = pl.ds(3 * width, width)
    inner_cols = pl.ds(0, 3 * width)
    load_wc = net.move(
        wc_hbm.at[:, :, :, :, outer_cols], wc.at[:, :, :, :, outer_cols]
    )
    load_zed = net.move(zed_hbm, zed)
    zedt, do_ref, out_ref = ht, e_ref, zed
    load_x = net.move(x_hbm, x_ref)
    load_gext = net.move(gext_hbm, gext)
    load_proj = net.move(proj_hbm, proj)
    load_win = net.move(
        wc_hbm.at[:, :, :, :, inner_cols], wc.at[:, :, :, :, inner_cols]
    )
    greet(
        [net.seat(n) for n in ("core", "x", "y", "z1", "z2", "z3")] + [after, cross] + upper
    )

    def plus_upper(ref, land, temp):
        for i, seat in enumerate(upper):
            copy = net.send(ref, land.at[i], seat)
            copy.wait()
            net.move(land.at[i], temp).wait()
            ref[...] = (ref[...].astype(full) + temp[...].astype(full)).astype(ref.dtype)

    load_gu2.wait()
    g1a = net.send(g2.at[z1], g2_z1.at[0], "z1")
    g1b = net.send(g2.at[z3], g2_z1.at[1], "z1")
    for copy in load_dn:
        copy.wait()
    dn0 = net.send(dn_o, dn_y, "y")
    dn1 = [net.make(dnv.at[k], dn_z1.at[k], "z1") for k in range(3)]
    dn2 = [net.make(dnv.at[k], dn_z2.at[k], "z2") for k in range(3)]
    dnx, dny, dnc = [], [], []
    for k in range(3):
        spot = fin_dn.at[k, ybit]
        dnx.append(net.make(spot, spot, "x"))
        dny.append(net.make(spot, spot, "y"))
        dnc.append(net.make(fin_dn.at[k], fin_dn.at[k], "core"))

    @pl.when(~same0)
    def _():
        for k in range(2):
            dn1[k].start()

    def dn_first():
        dn0.wait_recv()
        dnv[2] = (dnv[2].astype(full) + dn_y[...].astype(full)).astype(low)

        @pl.when(~same0)
        def _():
            dn1[2].start()

    def dn_second(k):
        @pl.when(same0)
        def _():
            dn1[k].wait_recv()
            dnv[k] = (dnv[k].astype(full) + dn_z1[k].astype(full)).astype(low)

        @pl.when(same0 & ~same1)
        def _():
            dn2[k].start()

    def dn_third(k):
        @pl.when(holder)
        def _():
            dn2[k].wait_recv()
            dnv[k] = (dnv[k].astype(full) + dn_z2[k].astype(full)).astype(low)
            plus_upper(dnv.at[k], up_dn.at[k], dn_z1.at[k])
            fin_dn[k, ybit] = dnv[k]
            dnx[k].start()
            dny[k].start()

    def dn_fourth(k):
        @pl.when(level & ~holder)
        def _():
            dnx[k].wait_recv()
            dny[k].start()

    def dn_fifth(k):
        @pl.when(level)
        def _():
            dny[k].wait_recv()
            dnc[k].start()

    def dn_last(k):
        @pl.when(~level)
        def _():
            dnc[k].wait_recv()

        for y in range(2):
            at = (2 * k + y) * (chunk // 2)
            results.append(net.move(fin_dn.at[k, y], gdn_out.at[pl.ds(at, chunk // 2)]))

    results = []

    def spread_gu(k):
        own = fin_gu.at[k, xbit, core, ybit]
        return net.send(own, own, "x"), net.send(own, own, "y")

    lo, hi = pl.ds(0, chunk), pl.ds(chunk, chunk)

    def onward_gu(k, b):
        b[0].wait_recv()
        spot = fin_gu.at[k, 1 - xbit, core, ybit, :, lo]
        first_half = net.send(spot, spot, "y")
        b[1].wait_recv()
        spot = fin_gu.at[k, xbit, core, 1 - ybit, :, hi]
        return first_half, net.send(spot, spot, "x")

    def across_gu(k, d):
        d[0].wait_recv()
        d[1].wait_recv()
        return net.send(fin_gu.at[k, :, core], fin_gu.at[k, :, core], "core")

    for copy in load_gu:
        copy.wait()
    g1y = net.send(g1_o, g1_y, "y")
    room_gu = pl.ds(0, half), pl.ds(0, pair)
    plus_upper(fin_gu.at[0, xbit, core, ybit], up_gu.at[0], dp.at[room_gu])
    gu_b = [spread_gu(0)]

    def gu_first():
        g1y.wait_recv()
        own = fin_gu.at[1, xbit, core, ybit]
        own[...] = (own[...].astype(full) + g1_y[...].astype(full)).astype(low)
        plus_upper(own, up_gu.at[1], dp.at[room_gu])
        gu_b.append(spread_gu(1))

    def row_of(k):
        return jnp.concatenate([small_all[i, k : k + 1, :] for i in range(4)], 1).astype(full)

    gain_one, gain_two = row_of(0), row_of(1)
    sums[...] = jnp.zeros_like(sums)
    load_first.wait()
    load_dh2.wait()
    load_e.wait()
    tile = 32

    def folded(value):
        return jnp.sum(value.reshape(value.shape[0] // 8, 8, value.shape[1]), axis=0)

    def norm_two(i, total):
        at = pl.ds(pl.multiple_of(i * tile, tile), tile)
        xf, dh = first[at], dh2[at]
        rate = lax.rsqrt(jnp.mean(xf * xf, axis=-1, keepdims=True) + epsilon)
        normed = xf * rate
        scaled = dh * gain_two
        mean = jnp.mean(scaled * normed, axis=-1, keepdims=True)
        got = e_ref[at].astype(full) + rate * (scaled - normed * mean)
        dx1[at] = got
        do_ref[at] = got.astype(low)
        return total + folded(dh * normed)

    total = lax.fori_loop(0, rows // tile, norm_two, jnp.zeros((8, width), full))
    sums[1:2, :] = jnp.sum(total, axis=0, keepdims=True)

    load_wc.wait()
    dz = first

    def back_out(i, carry):
        cols = pl.ds(pl.multiple_of(i * part, part), part)
        dz[:, cols] = outer(do_ref[...], wc[i, :, :, :, 3 * width :].reshape(part, width))
        return carry

    lax.fori_loop(0, 4, back_out, 0)
    load_zed.wait()
    load_x.wait()

    def turn_zed(i, carry):
        cols = pl.ds(pl.multiple_of(i * 256, 256), 256)
        zedt[:, cols] = zed[cols].T
        return carry

    lax.fori_loop(0, rows // 256, turn_zed, 0)

    def weight_chunk(left, right, at):
        def one(n, carry):
            cols = pl.ds(pl.multiple_of(n * 256, 256), 256)
            into = pl.ds(pl.multiple_of(at + n * 256, 256), 256)
            got = jnp.dot(left[...], right(cols), preferred_element_type=full).astype(low)
            dwc[:, :, :, :, :, into] = got.reshape(4, 2, 2, 2, part // 8, 256)
            return carry

        lax.fori_loop(0, width // 256, one, 0)

    starts_at = [3 * width, width, 0, 2 * width]

    def cols_of(i):
        return pl.ds(starts_at[i], width)

    def to_core(i):
        return net.send(dwc.at[:, :, :, 1 - core, :, cols_of(i)], cr.at[i], "core")

    weight_chunk(zedt, lambda cols: do_ref[:, cols], 3 * width)
    sc = [to_core(0)]

    g1a.wait_recv()
    g1b.wait_recv()
    g2[z2] = (g2[z2].astype(full) + g2_z1[1].astype(full)).astype(low)
    g2s = net.send(g2.at[z2], g2_z2, "z2")

    gu_first()
    dn_first()
    dn_second(0)
    dn_second(1)

    place = me * rows + lax.broadcasted_iota(jnp.int32, (rows, 1), 0)
    starts = jnp.broadcast_to(starts_ref[...], (8, rows)).T[:, 0:1]
    keep_one = (place - 1 >= starts).astype(full)
    keep_two = (place - 2 >= starts).astype(full)
    load_gext.wait()
    load_proj.wait()
    s1[rows:] = jnp.zeros((s1.shape[0] - rows, 128), full)
    s2[rows:] = jnp.zeros((s2.shape[0] - rows, 128), full)
    dg = dh2
    row8 = lax.broadcasted_iota(jnp.int32, (8, 128), 0)

    def unmix(i, carry):
        at = pl.ds(pl.multiple_of(i * 128, 128), 128)
        cat = pl.ds(pl.multiple_of(width + i * 128, 128), 128)
        zi = i // (part // 128)
        inside = pl.ds(pl.multiple_of((i % (part // 128)) * 128, 128), 128)
        taps = small_all[zi, :, inside].astype(full)
        tap0, tap1, tap2 = taps[2:3], taps[3:4], taps[4:5]
        current, lag_one, lag_two = gext[16:, at], gext[15 : rows + 15, at], gext[14 : rows + 14, at]
        mixed = tap0 * current + keep_one * tap1 * lag_one + keep_two * tap2 * lag_two
        back = dz[:, at]
        dp[:, cat] = (back * mixed).astype(low)
        dm = back * proj[:, cat]
        t1, t2 = keep_one * dm, keep_two * dm
        for k, value in ((2, dm * current), (3, t1 * lag_one), (4, t2 * lag_two)):
            sums[k : k + 1, at] = jnp.sum(folded(value), axis=0, keepdims=True)
        s1[:rows] = tap1 * t1
        s2[:rows] = tap2 * t2
        dg[:, at] = tap0 * dm + s1[1 : rows + 1] + s2[2 : rows + 2]
        ret_send[:, at] = jnp.where(
            row8 == 6, s2[0:1], jnp.where(row8 == 7, s1[0:1] + s2[1:2], 0.0)
        )
        return carry

    lax.fori_loop(0, width // 128, unmix, 0)
    back = net.send(ret_send, ret_land, before)

    def norm_one(i, carry):
        at = pl.ds(pl.multiple_of(i * 128, 128), 128)
        xf = x_ref[at].astype(full)
        rate = lax.rsqrt(jnp.mean(xf * xf, axis=-1, keepdims=True) + epsilon)
        ht[:, at] = (xf * rate * gain_one).astype(low).T
        return carry

    lax.fori_loop(0, rows // 128, norm_one, 0)
    weight_chunk(ht, lambda cols: dp[:, pl.ds(pl.multiple_of(width + cols.start, 256), 256)], width)
    sc.append(to_core(1))

    orders = ["xy", "yx", "yx", "xy"]
    def spot_of(i, zi, yi, xi):
        return (zi, yi, xi, core, slice(None), cols_of(i))

    def add_core(i):
        sc[i].wait_recv()

        def one(j, carry):
            zi, yi, xi = j // 4, (j // 2) % 2, j % 2
            spot = spot_of(i, zi, yi, xi)
            dwc[spot] = (dwc[spot].astype(full) + cr[i, zi, yi, xi].astype(full)).astype(low)
            return carry

        lax.fori_loop(0, 16, one, 0)
        cols = cols_of(i)
        if orders[i] == "xy":
            return net.send(dwc.at[:, :, 1 - xbit, core, :, cols], r1.at[i], "x")
        if orders[i] == "yx":
            return net.send(dwc.at[:, 1 - ybit, :, core, :, cols], r1.at[i], "y")
        return [
            net.send(dwc.at[:, yi, xi, core, :, cols], land, seat)
            for yi, xi, land, seat in (
                (ybit, 1 - xbit, r1.at[i, :, 0], "x"),
                (1 - ybit, xbit, r1.at[i, :, 1], "y"),
                (1 - ybit, 1 - xbit, r2.at[i], cross),
            )
        ]

    def add_first(i, copy):
        copy.wait_recv()

        def one(j, carry):
            zi, oi = j // 2, j % 2
            yi, xi = (oi, xbit) if orders[i] == "xy" else (ybit, oi)
            spot = spot_of(i, zi, yi, xi)
            dwc[spot] = (dwc[spot].astype(full) + r1[i, zi, oi].astype(full)).astype(low)
            return carry

        lax.fori_loop(0, 8, one, 0)
        cols = cols_of(i)
        if orders[i] == "xy":
            return net.send(dwc.at[:, 1 - ybit, xbit, core, :, cols], r2.at[i], "y")
        return net.send(dwc.at[:, ybit, 1 - xbit, core, :, cols], r2.at[i], "x")

    def add_second(i, copy):
        if orders[i] == "all":
            for c in copy:
                c.wait_recv()
        else:
            copy.wait_recv()

        def one(zi, carry):
            spot = spot_of(i, zi, ybit, xbit)
            got = dwc[spot].astype(full) + r2[i, zi].astype(full)
            if orders[i] == "all":
                got = got + r1[i, zi, 0].astype(full) + r1[i, zi, 1].astype(full)
            dwc[spot] = got.astype(low)
            return carry

        lax.fori_loop(0, 4, one, 0)
        return [
            net.send(dwc.at[spot_of(i, zz, ybit, xbit)], rz.at[i, k], seat)
            for k, (zz, seat) in enumerate(((z1, "z1"), (z2, "z2"), (z3, "z3")))
        ]

    def add_z(i, copies):
        for c in copies:
            c.wait_recv()
        own = fin_c.at[i, ybit, xbit, core]
        own[...] = (
            dwc[spot_of(i, z, ybit, xbit)].astype(full)
            + rz[i, 0].astype(full)
            + rz[i, 1].astype(full)
            + rz[i, 2].astype(full)
        ).astype(low)
        plus_upper(own, up_c.at[i], e_ref.at[pl.ds(0, part // 8)])
        return [net.send(own, own, seat) for seat in ("x", "y", cross)]

    def across_c(i, copies):
        for c in copies:
            c.wait_recv()
        return net.send(fin_c.at[i, :, :, core], fin_c.at[i, :, :, core], "core")

    def last_c(i, copy):
        copy.wait_recv()
        target = gout_out if i == 0 else gin_out.at[:, :, :, :, cols_of(i)]
        results.append(net.move(fin_c.at[i], target))

    def last_gu(k, copy):
        copy.wait_recv()
        for q in range(4):
            at = q * hq + k * chunk
            spot = fin_gu.at[k, q // 2, q % 2]
            results.append(net.move(spot.at[:, :, lo], ggu_out.at[:, :, pl.ds(at, chunk)]))
            results.append(
                net.move(spot.at[:, :, hi], ggu_out.at[:, :, pl.ds(hidden + at, chunk)])
            )

    a = {}
    b = {}
    a[0] = add_core(0)
    gu_d = [onward_gu(k, gu_b[k]) for k in range(2)]
    back.wait_recv()
    follows = (me < seq - 1).astype(full)
    dg[rows - 8 :] = dg[rows - 8 :] + ret_land[...] * follows

    def unproject(i, carry):
        at = pl.ds(pl.multiple_of(i * 128, 128), 128)
        xat = pl.ds(pl.multiple_of(2 * width + i * 128, 128), 128)
        dp[:, at] = (dg[:, at] * proj[:, xat]).astype(low)
        dp[:, xat] = (dg[:, at] * proj[:, at]).astype(low)
        return carry

    lax.fori_loop(0, width // 128, unproject, 0)
    weight_chunk(ht, lambda cols: dp[:, cols], 0)
    sc.append(to_core(2))
    a[1] = add_core(1)
    weight_chunk(ht, lambda cols: dp[:, pl.ds(pl.multiple_of(2 * width + cols.start, 256), 256)], 2 * width)
    sc.append(to_core(3))
    a[2] = add_core(2)
    b[0] = add_first(0, a[0])
    a[3] = add_core(3)

    g2s.wait_recv()
    own = fin_gu.at[2, xbit, core, ybit]
    own[...] = (
        g2[z].astype(full) + g2_z1[0].astype(full) + g2_z2[...].astype(full)
    ).astype(low)
    plus_upper(own, up_gu.at[2], e_ref.at[pl.ds(0, half), pl.ds(0, pair)])
    gu_b.append(spread_gu(2))
    dn_second(2)
    dn_third(0)

    load_win.wait()
    dh = dg

    def back_in(i, carry):
        cols = pl.ds(pl.multiple_of(i * part, part), part)
        dh[:, cols] = outer(dp[...], wc[i, :, :, :, : 3 * width].reshape(part, 3 * width))
        return carry

    lax.fori_loop(0, 4, back_in, 0)
    def norm_back(i, total):
        at = pl.ds(pl.multiple_of(i * tile, tile), tile)
        xf = x_ref[at].astype(full)
        rate = lax.rsqrt(jnp.mean(xf * xf, axis=-1, keepdims=True) + epsilon)
        normed = xf * rate
        got = dh[at]
        scaled = got * gain_one
        mean = jnp.mean(scaled * normed, axis=-1, keepdims=True)
        out_ref[at] = (dx1[at] + rate * (scaled - normed * mean)).astype(low)
        return total + folded(got * normed)

    total = lax.fori_loop(0, rows // tile, norm_back, jnp.zeros((8, width), full))
    keep_grad = net.move(out_ref, grad_out)
    sums[0:1, :] = jnp.sum(total, axis=0, keepdims=True)
    small_core = net.send(sums, sums_core, "core")
    b[1] = add_first(1, a[1])
    c = {0: add_second(0, b[0])}
    b[2] = add_first(2, a[2])
    dn_third(1)
    small_core.wait()
    sums[...] = sums[...] + sums_core[...]
    small_plane = [
        net.send(sums, sums_plane.at[i], seat) for i, seat in enumerate(("x", "y", cross))
    ]
    gu_c = [across_gu(k, gu_d[k]) for k in range(2)]
    dn_third(2)
    dn_fourth(0)
    c[1] = add_second(1, b[1])
    b[3] = add_first(3, a[3])
    c[2] = add_second(2, b[2])
    c[3] = add_second(3, b[3])
    dn_fourth(1)
    d = {0: add_z(0, c[0])}
    gu_d.append(onward_gu(2, gu_b[2]))
    dn_fourth(2)
    dn_fifth(0)
    for copy in small_plane:
        copy.wait()
    sums[...] = sums[...] + sums_plane[0] + sums_plane[1] + sums_plane[2]
    for i, seat in enumerate(upper):
        copy = net.send(sums, sums_plane.at[3 + i], seat)
        copy.wait()
        sums[...] = sums[...] + sums_plane[3 + i]

    def slab(zz):
        return sums.at[:, pl.ds(pl.multiple_of(zz * part, part), part)]

    small_z = [
        net.send(slab(zz), sums_z.at[i], seat)
        for i, (zz, seat) in enumerate(((z1, "z1"), (z2, "z2"), (z3, "z3")))
    ]
    d[1] = add_z(1, c[1])
    d[2] = add_z(2, c[2])
    d[3] = add_z(3, c[3])
    f = {0: across_c(0, d[0])}
    last_gu(0, gu_c[0])
    last_gu(1, gu_c[1])
    dn_fifth(1)
    dn_fifth(2)
    gu_c.append(across_gu(2, gu_d[2]))
    for i in (1, 2, 3):
        f[i] = across_c(i, d[i])
    for copy in small_z:
        copy.wait()
    small_out[...] = slab(z)[...] + sums_z[0] + sums_z[1] + sums_z[2]
    keep_small = net.move(small_out, gsmall_out)
    for k in range(3):
        dn_last(k)
    for i in (0, 1, 2, 3):
        last_c(i, f[i])
    last_gu(2, gu_c[2])

    @pl.when(~same0)
    def _():
        for copy in dn1:
            copy.wait_send()

    @pl.when(same0 & ~same1)
    def _():
        for copy in dn2:
            copy.wait_send()

    @pl.when(holder)
    def _():
        for copy in dnx:
            copy.wait_send()

    @pl.when(level)
    def _():
        for copy in dny + dnc:
            copy.wait_send()

    flat = [g1a, g1b, g2s, back, dn0, g1y] + gu_c + sc
    for group in gu_b + gu_d:
        flat += list(group)
    for group in (a, b, c, d, f):
        for copies in group.values():
            flat += copies if isinstance(copies, list) else [copies]
    for copy in flat:
        copy.wait_send()
    for copy in results:
        copy.wait()
    keep_grad.wait()
    keep_small.wait()


def finish(seq, starts, small_all, x, e, first, dh2, proj, zed, gext, wc, gu0, gu1, gu2, dn, dn2):
    rows, width = first.shape
    part = width // 4
    half, pair = gu0.shape
    chunk = pair // 2
    hq = 3 * chunk
    extra = seq.bit_length() - 4
    room = max(extra, 1)
    eighth = part // 8
    shape = jax.ShapeDtypeStruct
    anyspace = pl.BlockSpec(memory_space=pl.ANY)
    vmem = pl.BlockSpec(memory_space=pltpu.VMEM)
    outs = [
        shape((rows, width), low),
        shape((2, 2, 2, eighth, 3 * width), low),
        shape((2, 2, 2, eighth, width), low),
        shape((2, half, 8 * hq), low),
        shape((hq, width), low),
        shape((8, part), full),
    ]
    v = pltpu.VMEM
    outs += [
        shape((4, room, eighth, width), low),
        shape((3, room, half, pair), low),
        shape((3, room, chunk // 2, width), low),
    ]
    scratch = [
        v((4, 4, 2, eighth, 4 * width), low),
        v((rows, width), full),
        v((rows, width), full),
        v((rows, width), low),
        v((rows, width), low),
        v((rows, 3 * width), full),
        v((rows, width), low),
        v((width, rows), low),
        v((rows + 16, width), full),
        v((rows, width), full),
        v((rows, 3 * width), low),
        v((rows + 8, 128), full),
        v((rows + 8, 128), full),
        v((4, 2, 2, 2, eighth, 4 * width), low),
        v((8, width), full),
        v((8, width), full),
        v((8, width), full),
        v((8, width), full),
        v((3 + room, 8, width), full),
        v((3, 8, part), full),
        v((8, part), full),
        v((4, 4, 2, 2, eighth, width), low),
        v((4, 4, 2, eighth, width), low),
        v((4, 4, eighth, width), low),
        v((4, 3, eighth, width), low),
        v((4, 2, 2, 2, eighth, width), low),
        v((3, 2, 2, 2, half, pair), low),
        v((3, 2, chunk // 2, width), low),
        v((4, half, pair), low),
        v((2, half, pair), low),
        v((half, pair), low),
        v((half, pair), low),
        v((half, pair), low),
        v((3, chunk // 2, width), low),
        v((3, chunk // 2, width), low),
        v((3, chunk // 2, width), low),
        v((chunk // 2, width), low),
        v((chunk // 2, width), low),
        pltpu.SemaphoreType.DMA((100 + 12 * extra,)),
        pltpu.SemaphoreType.DMA((100 + 12 * extra,)),
        pltpu.SemaphoreType.DMA((60 + 12 * extra,)),
    ]
    return pl.pallas_call(
        functools.partial(finish_kernel, seq),
        out_shape=outs,
        in_specs=[vmem, vmem] + [anyspace] * 13,
        out_specs=[anyspace] * len(outs),
        scratch_shapes=scratch,
        compiler_params=pltpu.CompilerParams(
            collective_id=2, has_side_effects=True, vmem_limit_bytes=63 * MIB
        ),
        name="finish",
    )(starts, small_all, x, e, first, dh2, proj, zed, gext, wc, gu0, gu1, gu2, dn, dn2)


def cast_kernel(gu_ref, dn_ref, win_ref, wout_ref, res_ref, gx_ref, small_ref, *outs):
    ggu, gdn, gin, gout, res, gx, norm_one, norm_two, taps = outs
    ggu[...] = gu_ref[...].astype(full)
    gdn[...] = dn_ref[...].astype(full)
    gin[...] = win_ref[...].astype(full)
    gout[...] = wout_ref[...].astype(full)
    res[0] = res_ref[...]
    gx[0] = gx_ref[...]
    norm_one[...] = small_ref[0:1]
    norm_two[...] = small_ref[1:2]
    taps[...] = small_ref[2:5]


def cast(gu, dn, win, wout, result, grad_x, small):
    steps = 8
    arrays = (gu, dn, win, wout, result, grad_x)

    def cut(v, lead=False):
        rows, cols = v.shape
        if lead:
            return pl.BlockSpec((1, rows // steps, cols), lambda i: (0, i, 0))
        return pl.BlockSpec((rows // steps, cols), lambda i: (i, 0))

    def whole(shape):
        return pl.BlockSpec(shape, lambda i: (0, 0))

    part = small.shape[1]
    rows = ((1, part), (1, part), (3, part))
    moved = sum(v.size for v in arrays)
    return pl.pallas_call(
        cast_kernel,
        grid=(steps,),
        out_shape=[jax.ShapeDtypeStruct(v.shape, full) for v in arrays[:4]]
        + [jax.ShapeDtypeStruct((1, *v.shape), low) for v in arrays[4:]]
        + [jax.ShapeDtypeStruct(r, full) for r in rows],
        in_specs=[cut(v) for v in arrays] + [whole(small.shape)],
        out_specs=[cut(v) for v in arrays[:4]]
        + [cut(v, True) for v in arrays[4:]]
        + [whole(r) for r in rows],
        cost_estimate=pl.CostEstimate(flops=0, bytes_accessed=6 * moved, transcendentals=0),
        compiler_params=pltpu.CompilerParams(vmem_limit_bytes=63 * MIB),
        name="cast",
    )(*arrays, small)


def build(seq):
    def local(
        tokens,
        doc_start,
        norm1_gain,
        in_weight,
        conv_weight,
        out_weight,
        norm2_gain,
        gate_up_weight,
        down_weight,
        out_grad,
    ):
        x, cot = tokens[0], out_grad[0]
        starts = doc_start
        hq = down_weight.shape[0]
        small = (norm1_gain[None], norm2_gain[None], conv_weight.T)
        w_c, w_gu, w_down, cot_all, second_all, proj, first, zed, gext, small_all = gather(
            seq, x, cot, starts, *small, in_weight, out_weight, gate_up_weight, down_weight
        )
        result, dh2, gu0, gu1, gu2, dn, dn2, _ = feed(
            seq, second_all, cot_all, w_gu, w_down.reshape(hq, x.shape[1]), first
        )
        grad_x, grad_in, grad_out, grad_gu, grad_down, grad_small, *_ = finish(
            seq, starts, small_all, x, cot, first, dh2, proj, zed, gext, w_c, gu0, gu1, gu2, dn, dn2
        )
        grad_gu, grad_down, grad_in, grad_out, result, grad_x, norm_one, norm_two, taps = cast(
            grad_gu.reshape(gate_up_weight.shape),
            grad_down,
            grad_in.reshape(in_weight.shape),
            grad_out.reshape(out_weight.shape),
            result,
            grad_x,
            grad_small,
        )
        return (
            result,
            grad_x,
            norm_one[0],
            grad_in,
            taps.T,
            grad_out,
            norm_two[0],
            grad_gu,
            grad_down,
        )

    return local


def solution(mesh):
    in_specs = (
        P("wsh", "seq", None),
        P("wsh", "seq"),
        P("wsh"),
        P("wsh", None),
        P("wsh", None),
        P("wsh", None),
        P("wsh"),
        P("wsh", None),
        P("wsh", None),
        P("wsh", "seq", None),
    )
    out_specs = (
        P("wsh", "seq", None),
        P("wsh", "seq", None),
        P("wsh"),
        P("wsh", None),
        P("wsh", None),
        P("wsh", None),
        P("wsh"),
        P("wsh", None),
        P("wsh", None),
    )
    local = build(mesh.shape["seq"])
    return jax.shard_map(local, mesh=mesh, in_specs=in_specs, out_specs=out_specs, check_vma=False)
```

```python
import functools
import jax
import jax.numpy as jnp
from jax import lax
from jax.experimental import pallas as pl
from jax.experimental.pallas import tpu as pltpu
from jax.sharding import PartitionSpec as P

low = jnp.bfloat16
full = jnp.float32
MESH = pl.DeviceIdType.MESH
epsilon = 1e-06
MIB = 1 << 20


def mirrored(index, weight):
    return index + weight - 2 * weight * ((index // weight) % 2)


class Net:
    def __init__(self, me, z, send_sems, recv_sems, local_sems):
        self.me, self.z = me, z
        self.send_sems, self.recv_sems, self.local_sems = send_sems, recv_sems, local_sems
        self.count = self.local_count = 0

    def seat(self, name):
        me, z = self.me, self.z
        return {
            "core": {"seq": mirrored(me, 1), "wsh": z},
            "x": {"seq": mirrored(me, 2), "wsh": z},
            "y": {"seq": mirrored(me, 4), "wsh": z},
            "z1": {"seq": me, "wsh": mirrored(z, 1)},
            "z2": {"seq": me, "wsh": mirrored(z, 2)},
            "z3": {"seq": me, "wsh": 3 - z},
        }[name]

    def make(self, src, dst, seat, k=None):
        if k is None:
            k = self.count
            self.count += 1
        return pltpu.make_async_remote_copy(
            src_ref=src,
            dst_ref=dst,
            send_sem=self.send_sems.at[k],
            recv_sem=self.recv_sems.at[k],
            device_id=self.seat(seat) if isinstance(seat, str) else seat,
            device_id_type=MESH,
        )

    def send(self, src, dst, seat):
        copy = self.make(src, dst, seat)
        copy.start()
        return copy

    def move(self, src, dst):
        k = self.local_count
        self.local_count += 1
        copy = pltpu.make_async_copy(src, dst, self.local_sems.at[k])
        copy.start()
        return copy


def greet(seats):
    barrier = pltpu.get_barrier_semaphore()
    for seat in seats:
        pl.semaphore_signal(barrier, inc=1, device_id=seat, device_id_type=MESH)
    pl.semaphore_wait(barrier, len(seats))


def inner(left, right):
    return lax.dot_general(left, right, (((0,), (0,)), ((), ())), preferred_element_type=full)


def outer(left, right):
    return lax.dot_general(left, right, (((1,), (1,)), ((), ())), preferred_element_type=full)


def chunk_sizes(hq):
    chunk = hq // 3
    return chunk, 2 * chunk


def gather_kernel(
    seq,
    x_hbm, e_hbm, starts_ref, norm_one_ref, norm_two_ref, taps_ref, win_hbm, wout_hbm, wgu_hbm, wdn_hbm,
    wc_out, wgu_out, wdn_out, e_out, h2_out, proj_out, first_out, zed_out, gext_out, small_out,
    wc, ownf, winf, woutf, wguf, wdnf, wgu_own, wdn_own, x_ref, h_ref, proj, gext, zed, first, h2, small_all, small_own,
    send_sems, recv_sems, local_sems,
):
    me, z = lax.axis_index("seq"), lax.axis_index("wsh")
    net = Net(me, z, send_sems, recv_sems, local_sems)
    core, xbit, ybit = me % 2, (me // 2) % 2, (me // 4) % 2
    quarter = me % 4
    rows, width = x_hbm.shape
    part = width // 4
    hq = 6 * wdn_hbm.shape[2]
    hidden = 4 * hq
    half = part // 2
    z1, z2, z3 = mirrored(z, 1), mirrored(z, 2), 3 - z
    after = {"seq": lax.rem(me + 1, seq), "wsh": z}
    before = {"seq": lax.rem(me + seq - 1, seq), "wsh": z}

    piece = part // 8
    turn = (ybit * 2 + xbit) * 2 + core
    mine = pl.ds(pl.multiple_of(turn * piece, piece), piece)
    load_own = [
        net.move(win_hbm.at[mine], ownf.at[:, pl.ds(0, 3 * width)]),
        net.move(wout_hbm.at[mine], ownf.at[:, pl.ds(3 * width, width)]),
    ]
    load_x = net.move(x_hbm, x_ref.at[pl.ds(16, rows)])
    chunk, pair = chunk_sizes(hq)
    load_gu = []
    for k in range(3):
        for base, shift in ((quarter * hq, 0), (hidden + quarter * hq, chunk)):
            cut = pl.ds(pl.multiple_of(base + k * chunk, 128), chunk)
            load_gu.append(
                net.move(wgu_hbm.at[:, cut], wguf.at[:, pl.ds(k * pair + shift, chunk)])
            )
    load_win = net.move(win_hbm, winf)
    load_wout = net.move(wout_hbm, woutf)
    load_dn = net.move(wdn_hbm, wdnf)
    keep_e = net.move(e_hbm, e_out.at[0])
    small_own[...] = jnp.zeros_like(small_own)
    small_own[0:1] = norm_one_ref[...].astype(low).astype(full)
    small_own[1:2] = norm_two_ref[...].astype(low).astype(full)
    small_own[2:5] = taps_ref[...].astype(low).astype(full)
    small_all[z] = small_own[...].astype(low)
    for copy in load_own:
        copy.wait()
    spot = ybit * 2 + xbit
    spot_x = ybit * 2 + 1 - xbit
    spot_y = (1 - ybit) * 2 + xbit
    wc[z, spot, core] = ownf[...].astype(low)

    greet([net.seat(n) for n in ("core", "x", "y", "z1", "z2", "z3")] + [before])

    cols = [pl.ds(0, 2 * width), pl.ds(2 * width, 2 * width)]

    def own(zz):
        return wc.at[zz, spot, core]

    a1 = net.send(own(z), own(z), "z1")
    a2 = net.send(own(z), own(z), "z2")
    smalls = [net.send(small_all.at[z], small_all.at[z], n) for n in ("z1", "z2", "z3")]
    halo = net.send(x_hbm.at[pl.ds(rows - 16, 16)], x_ref.at[pl.ds(0, 16)], after)

    for copy in load_gu:
        copy.wait()
    wgu_own[...] = wguf[...].astype(low)
    keep_gu = net.move(wgu_own, wgu_out.at[z])
    load_win.wait()
    load_wout.wait()

    def cast_block(i, carry):
        @pl.when(i != turn)
        def _():
            at = pl.ds(pl.multiple_of(i * piece, piece), piece)
            wc[z, i // 2, i % 2, :, : 3 * width] = winf[at].astype(low)
            wc[z, i // 2, i % 2, :, 3 * width :] = woutf[at].astype(low)

        return carry

    lax.fori_loop(0, 8, cast_block, 0)
    load_dn.wait()

    def cast_dn(i, carry):
        wdn_own[i // 2, i % 2] = wdnf[i // 2, i % 2].astype(low)
        return carry

    lax.fori_loop(0, 6, cast_dn, 0)

    def spread(zz):
        return net.send(own(zz), own(zz), "x"), net.send(own(zz), own(zz), "y")

    def onward(zz, b):
        b[0].wait_recv()
        place = wc.at[zz, spot_x, core, :, cols[0]]
        d0 = net.send(place, place, "y")
        b[1].wait_recv()
        place = wc.at[zz, spot_y, core, :, cols[1]]
        return d0, net.send(place, place, "x")

    def across(zz, b, d):
        d[0].wait_recv()
        d[1].wait_recv()
        return net.send(wc.at[zz, :, core], wc.at[zz, :, core], "core")

    a1.wait_recv()
    b1 = spread(z1)
    a2.wait_recv()
    a3 = net.send(own(z2), own(z2), "z1")
    b2 = spread(z2)

    def gu(zz, yy, k):
        at = pl.ds(pl.multiple_of(yy * half, half), half)
        return wgu_out.at[zz, at, pl.ds(k * pair, pair)]

    f1, f2, f3, g1, g2, g3 = [], [], [], [], [], []
    for k in range(3):
        source = wgu_own.at[
            pl.ds(pl.multiple_of(ybit * half, half), half), pl.ds(k * pair, pair)
        ]
        f1.append(net.send(source, gu(z, ybit, k), "z1"))
        f2.append(net.send(source, gu(z, ybit, k), "z2"))

    same0 = (z % 2) == (quarter % 2)
    same1 = (z // 2) == (quarter // 2)
    holder = same0 & same1
    dn2, dn1a, dn1b, dny = [], [], [], []
    for k in range(3):
        source = wdn_own.at[k, ybit]
        target = wdn_out.at[k, ybit]
        dn2.append(net.make(source, target, "z2"))
        dn1a.append(net.make(source, target, "z1"))
        dn1b.append(net.make(target, target, "z1", net.count - 1))
        dny.append(net.make(target, target, "y"))
    keep_dn = pltpu.make_async_copy(wdn_own, wdn_out, local_sems.at[24])

    @pl.when(holder)
    def _():
        for k in range(3):
            dn2[k].start()
        keep_dn.start()

    def pass_gu(k):
        f1[k].wait_recv()
        g1.append(net.send(gu(z1, ybit, k), gu(z1, ybit, k), "y"))
        f2[k].wait_recv()
        f3.append(net.send(gu(z2, ybit, k), gu(z2, ybit, k), "z1"))
        g2.append(net.send(gu(z2, ybit, k), gu(z2, ybit, k), "y"))

    def pass_far(k):
        f3[k].wait_recv()
        g3.append(net.send(gu(z3, ybit, k), gu(z3, ybit, k), "y"))

    for copy in smalls:
        copy.wait_recv()
    load_x.wait()
    halo.wait_recv()

    def row_of(k):
        return jnp.concatenate([small_all[i, k : k + 1, :] for i in range(4)], 1).astype(full)

    gain_one, gain_two = row_of(0), row_of(1)

    def norm_one(i, carry):
        at = pl.ds(pl.multiple_of(i * 176, 16), 176)
        xf = x_ref[at].astype(full)
        rate = lax.rsqrt(jnp.mean(xf * xf, axis=-1, keepdims=True) + epsilon)
        h_ref[at] = (xf * rate * gain_one).astype(low)
        return carry

    lax.fori_loop(0, (rows + 16) // 176, norm_one, 0)
    d1 = onward(z1, b1)
    d2 = onward(z2, b2)
    a3.wait_recv()
    b3 = spread(z3)

    def pass_dn(k):
        @pl.when(same0 & ~same1)
        def _():
            dn2[k].wait_recv()
            dn1b[k].start()
            dny[k].start()

        @pl.when(~same0)
        def _():
            dn1a[k].wait_recv()
            dny[k].start()

    c1 = across(z1, b1, d1)
    c2 = across(z2, b2, d2)
    d3 = onward(z3, b3)
    pass_gu(0)
    c3 = across(z3, b3, d3)

    @pl.when(holder)
    def _():
        for k in range(3):
            dn1a[k].start()

    for c in (c1, c2, c3):
        c.wait_recv()
    ex = net.send(e_hbm, e_out.at[1], "x")
    ec = net.send(e_hbm, e_out.at[2], "core")
    pass_gu(1)

    def project(i, carry):
        at = pl.ds(pl.multiple_of(i * 512, 512), 512)
        proj[:, at] = jnp.dot(
            h_ref[...], wc[:, :, :, :, at].reshape(width, 512), preferred_element_type=full
        )
        return carry

    lax.fori_loop(0, 6, project, 0)
    keep_wc = net.move(wc, wc_out)
    keep_proj = net.move(proj.at[pl.ds(16, rows)], proj_out)

    pass_gu(2)
    place = me * rows + lax.broadcasted_iota(jnp.int32, (rows, 1), 0)
    starts = jnp.broadcast_to(starts_ref[...], (8, rows)).T[:, 0:1]
    keep_one = (place - 1 >= starts).astype(full)
    keep_two = (place - 2 >= starts).astype(full)
    cw = 128
    def mix(i, carry):
        at = pl.ds(pl.multiple_of(i * cw, cw), cw)
        xat = pl.ds(pl.multiple_of(2 * width + i * cw, cw), cw)
        cat = pl.ds(pl.multiple_of(width + i * cw, cw), cw)
        gext[:, at] = (proj[:, at] * proj[:, xat]).astype(low).astype(full)
        zi = i // (part // cw)
        inside = pl.ds(pl.multiple_of((i % (part // cw)) * cw, cw), cw)
        taps = small_all[zi, :, inside].astype(full)
        mixed = (
            taps[2:3] * gext[16:, at]
            + keep_one * taps[3:4] * gext[15 : rows + 15, at]
            + keep_two * taps[4:5] * gext[14 : rows + 14, at]
        )
        zed[:, at] = (proj[16:, cat] * mixed).astype(low)
        return carry

    lax.fori_loop(0, width // cw, mix, 0)
    keep_zed = net.move(zed, zed_out)
    keep_gext = net.move(gext, gext_out)

    pass_dn(0)
    pass_far(0)
    pass_dn(1)

    def project_out(i, carry):
        at = pl.ds(pl.multiple_of(i * 512, 512), 512)
        wat = pl.ds(pl.multiple_of(3 * width + i * 512, 512), 512)
        first[:, at] = x_ref[16:, at].astype(full) + jnp.dot(
            zed[...], wc[:, :, :, :, wat].reshape(width, 512), preferred_element_type=full
        )
        return carry

    lax.fori_loop(0, 2, project_out, 0)
    keep_first = net.move(first, first_out)
    pass_far(1)

    def norm_two(i, carry):
        at = pl.ds(pl.multiple_of(i * 128, 128), 128)
        xf = first[at]
        rate = lax.rsqrt(jnp.mean(xf * xf, axis=-1, keepdims=True) + epsilon)
        h2[at] = (xf * rate * gain_two).astype(low)
        return carry

    lax.fori_loop(0, rows // 128, norm_two, 0)
    keep_h2 = net.move(h2, h2_out.at[0])
    hx = net.send(h2, h2_out.at[1], "x")
    hc = net.send(h2, h2_out.at[2], "core")
    keep_small = net.move(small_all, small_out)

    pass_far(2)
    ex.wait_recv()
    exc = net.send(e_out.at[1], e_out.at[3], "core")
    pass_dn(2)
    hx.wait_recv()
    hxc = net.send(h2_out.at[1], h2_out.at[3], "core")
    for c in (*g1, *g2, *g3, ec, exc, hc, hxc):
        c.wait_recv()

    @pl.when(~holder)
    def _():
        for copy in dny:
            copy.wait()

    @pl.when(holder)
    def _():
        for copy in dn2 + dn1a:
            copy.wait_send()
        keep_dn.wait()

    @pl.when(same0 & ~same1)
    def _():
        for copy in dn1b:
            copy.wait_send()

    for c in (
        *smalls, halo, a1, a2, a3, *b1, *b2, *b3, *d1, *d2, *d3, c1, c2, c3,
        *f1, *f2, *f3, *g1, *g2, *g3, ex, ec, exc, hx, hc, hxc,
    ):
        c.wait_send()
    for c in (keep_e, keep_gu, keep_wc, keep_proj, keep_zed, keep_gext, keep_first, keep_h2, keep_small):
        c.wait()


def gather(seq, x, e, starts, norm_one, norm_two, taps, win, wout, wgu, wdn):
    rows, width = x.shape
    part = width // 4
    hq = wdn.shape[0]
    thirds = (3, 2, hq // 6, width)
    wdn = wdn.reshape(thirds)
    shape = jax.ShapeDtypeStruct
    anyspace = pl.BlockSpec(memory_space=pl.ANY)
    vmem = pl.BlockSpec(memory_space=pltpu.VMEM)
    conv = (4, 4, 2, part // 8, 4 * width)
    outs = [
        shape(conv, low),
        shape((4, part, 2 * hq), low),
        shape(thirds, low),
        shape((4, rows, width), low),
        shape((4, rows, width), low),
        shape((rows, 3 * width), full),
        shape((rows, width), full),
        shape((rows, width), low),
        shape((rows + 16, width), full),
        shape((4, 16, part), low),
    ]
    scratch = [
        pltpu.VMEM(conv, low),
        pltpu.VMEM((part // 8, 4 * width), full),
        pltpu.VMEM((part, 3 * width), full),
        pltpu.VMEM((part, width), full),
        pltpu.VMEM((part, 2 * hq), full),
        pltpu.VMEM(thirds, full),
        pltpu.VMEM((part, 2 * hq), low),
        pltpu.VMEM(thirds, low),
        pltpu.VMEM((rows + 16, width), low),
        pltpu.VMEM((rows + 16, width), low),
        pltpu.VMEM((rows + 16, 3 * width), full),
        pltpu.VMEM((rows + 16, width), full),
        pltpu.VMEM((rows, width), low),
        pltpu.VMEM((rows, width), full),
        pltpu.VMEM((rows, width), low),
        pltpu.VMEM((4, 16, part), low),
        pltpu.VMEM((16, part), full),
        pltpu.SemaphoreType.DMA((64,)),
        pltpu.SemaphoreType.DMA((64,)),
        pltpu.SemaphoreType.DMA((26,)),
    ]
    return pl.pallas_call(
        functools.partial(gather_kernel, seq),
        out_shape=outs,
        in_specs=[anyspace, anyspace] + [vmem] * 4 + [anyspace] * 4,
        out_specs=[anyspace] * len(outs),
        scratch_shapes=scratch,
        compiler_params=pltpu.CompilerParams(
            collective_id=0, has_side_effects=True, vmem_limit_bytes=56 * MIB
        ),
        name="gather",
    )(x, e, starts, norm_one, norm_two, taps, win, wout, wgu, wdn)


def feed_kernel(
    seq,
    h2_hbm, e_hbm, wgu_hbm, wdn_hbm, first_hbm,
    result_out, dh2_out, gu0_out, gu1_out, gu2_out, dn_out, dn2_out, land_out,
    h2, h2t, e, wgu, wdn, a, at_ref, du, u, da, dgu, ddn, send_a, send_b, send_x, send_o, temp, acc, acc_out,
    gu0_y, gu2_y, dn_y, gu0_z1, gu0_z2, gu1_z1, gu1_z2, gu0_s, gu1_s, gu1_t, gu0_f,
    send_sems, recv_sems, local_sems,
):
    me, z = lax.axis_index("seq"), lax.axis_index("wsh")
    net = Net(me, z, send_sems, recv_sems, local_sems)
    ybit = (me // 4) % 2
    rows, width = first_hbm.shape
    hq = wdn.shape[0]
    chunk, pair = chunk_sizes(hq)
    part = width // 4
    half = part // 2
    z1, z2, z3 = mirrored(z, 1), mirrored(z, 2), 3 - z
    block = 4 * rows

    load_h2, load_e, load_gu, load_dn = [], [], [], []

    def load_block(j):
        load_h2.append(net.move(h2_hbm.at[j], h2.at[pl.ds(j * rows, rows)]))
        load_e.append(net.move(e_hbm.at[j], e.at[pl.ds(j * rows, rows)]))

    def load_chunk(k):
        pcols, ccols = pl.ds(k * pair, pair), pl.ds(k * chunk, chunk)
        for i in range(4):
            load_gu.append(net.move(wgu_hbm.at[i, :, pcols], wgu.at[pl.ds(i * part, part), pcols]))
        load_dn.append(net.move(wdn_hbm.at[ccols], wdn.at[ccols]))

    load_chunk(0)
    for j in range(4):
        load_block(j)
    load_chunk(1)
    load_chunk(2)
    load_first = net.move(first_hbm, acc_out)
    greet([net.seat(n) for n in ("core", "x", "y", "z1", "z2")])

    def turn(j, carry):
        at = pl.ds(pl.multiple_of(j * 256, 256), 256)
        h2t[:, at] = h2[at].T
        return carry

    def forward(k, slots, step):
        pcols, ccols = pl.ds(k * pair, pair), pl.ds(k * chunk, chunk)

        def one(i, carry):
            j = slots + i * step
            at = pl.ds(pl.multiple_of(j * rows, rows), rows)
            u[...] = jnp.dot(h2[at], wgu[:, pcols], preferred_element_type=full)
            da[...] = outer(e[at], wdn[ccols])

            def piece(r, carry):
                rr = pl.ds(pl.multiple_of(r * 64, 64), 64)
                tt = pl.ds(pl.multiple_of(j * rows + r * 64, 64), 64)
                gate, upper, back = u[rr, :chunk], u[rr, chunk:], da[rr]
                sigma = jax.nn.sigmoid(gate)
                swish = gate * sigma
                a[tt, ccols] = (swish * upper).astype(low)
                du[tt, pl.ds(k * pair, chunk)] = (
                    back * upper * (sigma * (1.0 + gate * (1.0 - sigma)))
                ).astype(low)
                du[tt, pl.ds(k * pair + chunk, chunk)] = (back * swish).astype(low)
                return carry

            lax.fori_loop(0, rows // 64, piece, 0)
            return carry

        lax.fori_loop(0, 4 // step, one, 0)

    def weights(k):
        def turn_a(j, carry):
            at = pl.ds(pl.multiple_of(j * rows, rows), rows)
            at_ref[:, at] = a[at, pl.ds(k * chunk, chunk)].T
            return carry

        lax.fori_loop(0, 4, turn_a, 0)

        def gate_up(n, carry):
            cols = pl.ds(pl.multiple_of(k * pair + n * 256, 256), 256)
            got = jnp.dot(h2t[...], du[:, cols], preferred_element_type=full).astype(low)
            dgu[:, :, :, cols] = got.reshape(4, 2, half, 256)
            return carry

        lax.fori_loop(0, pair // 256, gate_up, 0)

        def down(n, carry):
            cols = pl.ds(pl.multiple_of(n * 512, 512), 512)
            got = jnp.dot(at_ref[...], e[:, cols], preferred_element_type=full).astype(low)
            ddn[k, :, :, cols] = got.reshape(2, chunk // 2, 512)
            return carry

        lax.fori_loop(0, width // 512, down, 0)

    def cols_of(k):
        return pl.ds(k * pair, pair)

    for copy in load_gu[:4] + load_dn[:1]:
        copy.wait()
    for j in range(4):
        load_h2[j].wait()
        load_e[j].wait()
        forward(0, j, 4)
    lax.fori_loop(0, block // 256, turn, 0)
    weights(0)
    for copy in load_gu[4:] + load_dn[1:]:
        copy.wait()
    y0 = net.send(dgu.at[:, 1 - ybit, :, cols_of(0)], gu0_y, "y")
    yd0 = net.send(ddn.at[0, 1 - ybit], dn_y.at[0], "y")
    forward(1, 0, 1)
    forward(2, 1, 2)

    def sum_rows(put, count, step):
        def one(i, carry):
            put(pl.ds(pl.multiple_of(i * step, step), step))
            return carry

        lax.fori_loop(0, count // step, one, 0)

    def accumulate(target):
        def go(at):
            target[at] = target[at] + temp[at].astype(full)

        return go

    def keep(cols, value):
        acc[:, cols] = value

    def more(cols, value):
        acc_out[:, cols] = acc_out[:, cols] + value

    def gu0_sum(i, carry):
        gu0_s[i] = (dgu[i, ybit, :, cols_of(0)].astype(full) + gu0_y[i].astype(full)).astype(low)
        return carry

    def gu1_sum(i, carry):
        gu1_t[i] = (dgu[z2, i, :, cols_of(1)].astype(full) + gu1_z1[1, i].astype(full)).astype(low)
        gu1_s[i] = (dgu[z, i, :, cols_of(1)].astype(full) + gu1_z1[0, i].astype(full)).astype(low)
        return carry

    def gu1_more(i, carry):
        gu1_s[i] = (gu1_s[i].astype(full) + gu1_z2[i].astype(full)).astype(low)
        return carry

    def finish(at):
        send_a[at] = (acc_out[at] + temp[at].astype(full)).astype(low)

    def grad_rows(j, put):
        at = pl.ds(j * rows, rows)

        def one(n, carry):
            cols = pl.ds(pl.multiple_of(n * 256, 256), 256)
            put(cols, outer(du[at], wgu[cols]))
            return carry

        lax.fori_loop(0, width // 256, one, 0)

    def out_rows(j, put):
        at = pl.ds(j * rows, rows)

        def one(n, carry):
            cols = pl.ds(pl.multiple_of(n * 256, 256), 256)
            put(cols, jnp.dot(a[at], wdn[:, cols], preferred_element_type=full))
            return carry

        lax.fori_loop(0, width // 256, one, 0)

    def store(ref):
        def put(cols, value):
            ref[:, cols] = value.astype(low)

        return put

    def add(target, other):
        def put(cols, value):
            target[:, cols] = (value + other[:, cols].astype(full)).astype(target.dtype)

        return put

    def fetch(j):
        copy = net.move(land_out.at[j], temp)
        copy.wait()

    grad_rows(3, store(send_a))
    ga = net.send(send_a, land_out.at[0], "core")
    out_rows(3, store(send_b))
    oa = net.send(send_b, land_out.at[3], "core")
    ga.wait_recv()
    fetch(0)
    grad_rows(1, add(send_x, temp))
    gx = net.send(send_x, land_out.at[1], "x")
    weights(1)
    m1 = net.send(dgu.at[z1, :, :, cols_of(1)], gu1_z1.at[0], "z1")
    m2 = net.send(dgu.at[z3, :, :, cols_of(1)], gu1_z1.at[1], "z1")
    yd1 = net.send(ddn.at[1, 1 - ybit], dn_y.at[1], "y")
    oa.wait_recv()
    fetch(3)
    out_rows(1, add(send_o, temp))
    ox = net.send(send_o, land_out.at[4], "x")
    forward(2, 0, 2)
    y0.wait_recv()
    lax.fori_loop(0, 4, gu0_sum, 0)
    n1 = net.send(gu0_s.at[z1], gu0_z1.at[0], "z1")
    n2 = net.send(gu0_s.at[z3], gu0_z1.at[1], "z1")
    weights(2)
    y2 = net.send(dgu.at[:, 1 - ybit, :, cols_of(2)], gu2_y, "y")
    keep_dn2 = net.move(ddn.at[2], dn2_out)
    m1.wait_recv()
    m2.wait_recv()
    lax.fori_loop(0, 2, gu1_sum, 0)
    m3 = net.send(gu1_t, gu1_z2, "z2")
    ga.wait_send()
    grad_rows(2, store(send_a))
    gb = net.send(send_a, land_out.at[2], "core")
    n1.wait_recv()
    n2.wait_recv()
    gu0_f[1] = (gu0_s[z2].astype(full) + gu0_z1[1].astype(full)).astype(low)
    n3 = net.send(gu0_f.at[1], gu0_z2, "z2")
    oa.wait_send()
    out_rows(2, store(send_b))
    ob = net.send(send_b, land_out.at[5], "core")
    grad_rows(0, keep)
    gb.wait_recv()
    fetch(2)
    sum_rows(accumulate(acc), rows, 64)
    load_first.wait()
    out_rows(0, more)
    ob.wait_recv()
    fetch(5)
    sum_rows(accumulate(acc_out), rows, 64)
    m3.wait_recv()
    lax.fori_loop(0, 2, gu1_more, 0)
    keep_gu1 = net.move(gu1_s, gu1_out)
    gx.wait_recv()
    fetch(1)
    sum_rows(accumulate(acc), rows, 64)
    keep_dh2 = net.move(acc, dh2_out)
    n3.wait_recv()
    gu0_f[0] = (
        gu0_s[z].astype(full) + gu0_z1[0].astype(full) + gu0_z2[...].astype(full)
    ).astype(low)
    keep_gu0 = net.move(gu0_f.at[0], gu0_out)
    ox.wait_recv()
    fetch(4)
    gb.wait_send()
    sum_rows(finish, rows, 64)
    keep_result = net.move(send_a, result_out)

    yd0.wait_recv()
    yd1.wait_recv()
    y2.wait_recv()

    def gu2_sum(i, carry):
        dgu[i, ybit, :, cols_of(2)] = (
            dgu[i, ybit, :, cols_of(2)].astype(full) + gu2_y[i].astype(full)
        ).astype(low)
        return carry

    lax.fori_loop(0, 4, gu2_sum, 0)
    keep_gu2 = net.move(dgu.at[:, ybit, :, cols_of(2)], gu2_out)

    def dn_sum(i, carry):
        ddn[i, ybit] = (ddn[i, ybit].astype(full) + dn_y[i].astype(full)).astype(low)
        return carry

    lax.fori_loop(0, 2, dn_sum, 0)
    keep_dn = net.move(ddn.at[pl.ds(0, 2), ybit], dn_out)
    for c in (y0, yd0, m1, m2, yd1, y2, n1, n2, m3, n3, ox, ob, gx):
        c.wait_send()
    for c in (keep_dh2, keep_gu0, keep_result, keep_gu2, keep_dn, keep_dn2, keep_gu1):
        c.wait()


def feed(seq, h2_all, e_all, wgu, wdn, first):
    rows, width = first.shape
    part = width // 4
    half = part // 2
    hq = wdn.shape[0]
    chunk, pair = chunk_sizes(hq)
    shape = jax.ShapeDtypeStruct
    anyspace = pl.BlockSpec(memory_space=pl.ANY)
    outs = [
        shape((rows, width), low),
        shape((rows, width), full),
        shape((half, pair), low),
        shape((2, half, pair), low),
        shape((4, half, pair), low),
        shape((2, chunk // 2, width), low),
        shape((2, chunk // 2, width), low),
        shape((6, rows, width), low),
    ]
    v = pltpu.VMEM
    scratch = [
        v((4 * rows, width), low),
        v((width, 4 * rows), low),
        v((4 * rows, width), low),
        v((width, 2 * hq), low),
        v((hq, width), low),
        v((4 * rows, hq), low),
        v((chunk, 4 * rows), low),
        v((4 * rows, 2 * hq), low),
        v((rows, pair), full),
        v((rows, chunk), full),
        v((4, 2, half, 2 * hq), low),
        v((3, 2, chunk // 2, width), low),
        v((rows, width), low),
        v((rows, width), low),
        v((rows, width), low),
        v((rows, width), low),
        v((rows, width), low),
        v((rows, width), full),
        v((rows, width), full),
        v((4, half, pair), low),
        v((4, half, pair), low),
        v((2, chunk // 2, width), low),
        v((2, half, pair), low),
        v((half, pair), low),
        v((2, 2, half, pair), low),
        v((2, half, pair), low),
        v((4, half, pair), low),
        v((2, half, pair), low),
        v((2, half, pair), low),
        v((2, half, pair), low),
        pltpu.SemaphoreType.DMA((24,)),
        pltpu.SemaphoreType.DMA((24,)),
        pltpu.SemaphoreType.DMA((44,)),
    ]
    return pl.pallas_call(
        functools.partial(feed_kernel, seq),
        out_shape=outs,
        in_specs=[anyspace] * 5,
        out_specs=[anyspace] * len(outs),
        scratch_shapes=scratch,
        compiler_params=pltpu.CompilerParams(
            collective_id=1, has_side_effects=True, vmem_limit_bytes=63 * MIB
        ),
        name="feed",
    )(h2_all, e_all, wgu, wdn, first)


def finish_kernel(
    seq,
    starts_ref, small_all, x_hbm, e_hbm, first_hbm, dh2_hbm, proj_hbm, zed_hbm, gext_hbm, wc_hbm,
    gu0_hbm, gu1_hbm, gu2_hbm, dn_hbm, dn2_hbm,
    grad_out, gin_out, gout_out, ggu_out, gdn_out, gsmall_out, up_c, up_gu, up_dn,
    wc, first, dh2, x_ref, e_ref, proj, zed, ht, gext, dx1, dp, s1, s2, dwc,
    ret_send, ret_land, sums, sums_core, sums_plane, sums_z, small_out,
    cr, r1, r2, rz, fin_c, fin_gu, fin_dn, g2, g2_z1, g2_z2, g1_o, g1_y, dnv, dn_z1, dn_z2, dn_o, dn_y,
    send_sems, recv_sems, local_sems,
):
    me, z = lax.axis_index("seq"), lax.axis_index("wsh")
    net = Net(me, z, send_sems, recv_sems, local_sems)
    core, xbit, ybit = me % 2, (me // 2) % 2, (me // 4) % 2
    quarter = me % 4
    rows, width = first.shape
    part = width // 4
    half = part // 2
    chunk = dnv.shape[1] * 2
    pair = 2 * chunk
    hq = 3 * chunk
    hidden = 4 * hq
    z1, z2, z3 = mirrored(z, 1), mirrored(z, 2), 3 - z
    after = {"seq": lax.rem(me + 1, seq), "wsh": z}
    before = {"seq": lax.rem(me + seq - 1, seq), "wsh": z}
    cross = {"seq": mirrored(mirrored(me, 2), 4), "wsh": z}
    upper = [
        {"seq": mirrored(me, 1 << bit), "wsh": z} for bit in range(3, seq.bit_length() - 1)
    ]
    same0 = (z % 2) == (quarter % 2)
    same1 = (z // 2) == (quarter // 2)
    holder = same0 & same1
    level = core == z % 2

    load_gu2 = net.move(gu2_hbm, g2)
    load_dn = [
        net.move(dn2_hbm.at[ybit], dnv.at[2]),
        net.move(dn2_hbm.at[1 - ybit], dn_o),
        net.move(dn_hbm, dnv.at[pl.ds(0, 2)]),
    ]
    load_gu = [
        net.move(gu0_hbm, fin_gu.at[0, xbit, core, ybit]),
        net.move(gu1_hbm.at[ybit], fin_gu.at[1, xbit, core, ybit]),
        net.move(gu1_hbm.at[1 - ybit], g1_o),
    ]
    load_first = net.move(first_hbm, first)
    load_dh2 = net.move(dh2_hbm, dh2)
    load_e = net.move(e_hbm, e_ref)
    outer_cols = pl.ds(3 * width, width)
    inner_cols = pl.ds(0, 3 * width)
    load_wc = net.move(
        wc_hbm.at[:, :, :, :, outer_cols], wc.at[:, :, :, :, outer_cols]
    )
    load_zed = net.move(zed_hbm, zed)
    zedt, do_ref, out_ref = ht, e_ref, zed
    load_x = net.move(x_hbm, x_ref)
    load_gext = net.move(gext_hbm, gext)
    load_proj = net.move(proj_hbm, proj)
    load_win = net.move(
        wc_hbm.at[:, :, :, :, inner_cols], wc.at[:, :, :, :, inner_cols]
    )
    greet(
        [net.seat(n) for n in ("core", "x", "y", "z1", "z2", "z3")] + [after, cross] + upper
    )

    def plus_upper(ref, land, temp):
        for i, seat in enumerate(upper):
            copy = net.send(ref, land.at[i], seat)
            copy.wait()
            net.move(land.at[i], temp).wait()
            ref[...] = (ref[...].astype(full) + temp[...].astype(full)).astype(ref.dtype)

    load_gu2.wait()
    g1a = net.send(g2.at[z1], g2_z1.at[0], "z1")
    g1b = net.send(g2.at[z3], g2_z1.at[1], "z1")
    for copy in load_dn:
        copy.wait()
    dn0 = net.send(dn_o, dn_y, "y")
    dn1 = [net.make(dnv.at[k], dn_z1.at[k], "z1") for k in range(3)]
    dn2 = [net.make(dnv.at[k], dn_z2.at[k], "z2") for k in range(3)]
    dnx, dny, dnc = [], [], []
    for k in range(3):
        spot = fin_dn.at[k, ybit]
        dnx.append(net.make(spot, spot, "x"))
        dny.append(net.make(spot, spot, "y"))
        dnc.append(net.make(fin_dn.at[k], fin_dn.at[k], "core"))

    @pl.when(~same0)
    def _():
        for k in range(2):
            dn1[k].start()

    def dn_first():
        dn0.wait_recv()
        dnv[2] = (dnv[2].astype(full) + dn_y[...].astype(full)).astype(low)

        @pl.when(~same0)
        def _():
            dn1[2].start()

    def dn_second(k):
        @pl.when(same0)
        def _():
            dn1[k].wait_recv()
            dnv[k] = (dnv[k].astype(full) + dn_z1[k].astype(full)).astype(low)

        @pl.when(same0 & ~same1)
        def _():
            dn2[k].start()

    def dn_third(k):
        @pl.when(holder)
        def _():
            dn2[k].wait_recv()
            dnv[k] = (dnv[k].astype(full) + dn_z2[k].astype(full)).astype(low)
            plus_upper(dnv.at[k], up_dn.at[k], dn_z1.at[k])
            fin_dn[k, ybit] = dnv[k]
            dnx[k].start()
            dny[k].start()

    def dn_fourth(k):
        @pl.when(level & ~holder)
        def _():
            dnx[k].wait_recv()
            dny[k].start()

    def dn_fifth(k):
        @pl.when(level)
        def _():
            dny[k].wait_recv()
            dnc[k].start()

    def dn_last(k):
        @pl.when(~level)
        def _():
            dnc[k].wait_recv()

        for y in range(2):
            at = (2 * k + y) * (chunk // 2)
            results.append(net.move(fin_dn.at[k, y], gdn_out.at[pl.ds(at, chunk // 2)]))

    results = []

    def spread_gu(k):
        own = fin_gu.at[k, xbit, core, ybit]
        return net.send(own, own, "x"), net.send(own, own, "y")

    lo, hi = pl.ds(0, chunk), pl.ds(chunk, chunk)

    def onward_gu(k, b):
        b[0].wait_recv()
        spot = fin_gu.at[k, 1 - xbit, core, ybit, :, lo]
        first_half = net.send(spot, spot, "y")
        b[1].wait_recv()
        spot = fin_gu.at[k, xbit, core, 1 - ybit, :, hi]
        return first_half, net.send(spot, spot, "x")

    def across_gu(k, d):
        d[0].wait_recv()
        d[1].wait_recv()
        return net.send(fin_gu.at[k, :, core], fin_gu.at[k, :, core], "core")

    for copy in load_gu:
        copy.wait()
    g1y = net.send(g1_o, g1_y, "y")
    room_gu = pl.ds(0, half), pl.ds(0, pair)
    plus_upper(fin_gu.at[0, xbit, core, ybit], up_gu.at[0], dp.at[room_gu])
    gu_b = [spread_gu(0)]

    def gu_first():
        g1y.wait_recv()
        own = fin_gu.at[1, xbit, core, ybit]
        own[...] = (own[...].astype(full) + g1_y[...].astype(full)).astype(low)
        plus_upper(own, up_gu.at[1], dp.at[room_gu])
        gu_b.append(spread_gu(1))

    def row_of(k):
        return jnp.concatenate([small_all[i, k : k + 1, :] for i in range(4)], 1).astype(full)

    gain_one, gain_two = row_of(0), row_of(1)
    sums[...] = jnp.zeros_like(sums)
    load_first.wait()
    load_dh2.wait()
    load_e.wait()
    tile = 32

    def folded(value):
        return jnp.sum(value.reshape(value.shape[0] // 8, 8, value.shape[1]), axis=0)

    def norm_two(i, total):
        at = pl.ds(pl.multiple_of(i * tile, tile), tile)
        xf, dh = first[at], dh2[at]
        rate = lax.rsqrt(jnp.mean(xf * xf, axis=-1, keepdims=True) + epsilon)
        normed = xf * rate
        scaled = dh * gain_two
        mean = jnp.mean(scaled * normed, axis=-1, keepdims=True)
        got = e_ref[at].astype(full) + rate * (scaled - normed * mean)
        dx1[at] = got
        do_ref[at] = got.astype(low)
        return total + folded(dh * normed)

    total = lax.fori_loop(0, rows // tile, norm_two, jnp.zeros((8, width), full))
    sums[1:2, :] = jnp.sum(total, axis=0, keepdims=True)

    load_wc.wait()
    dz = first

    def back_out(i, carry):
        cols = pl.ds(pl.multiple_of(i * part, part), part)
        dz[:, cols] = outer(do_ref[...], wc[i, :, :, :, 3 * width :].reshape(part, width))
        return carry

    lax.fori_loop(0, 4, back_out, 0)
    load_zed.wait()
    load_x.wait()

    def turn_zed(i, carry):
        cols = pl.ds(pl.multiple_of(i * 256, 256), 256)
        zedt[:, cols] = zed[cols].T
        return carry

    lax.fori_loop(0, rows // 256, turn_zed, 0)

    def weight_chunk(left, right, at):
        def one(n, carry):
            cols = pl.ds(pl.multiple_of(n * 256, 256), 256)
            into = pl.ds(pl.multiple_of(at + n * 256, 256), 256)
            got = jnp.dot(left[...], right(cols), preferred_element_type=full).astype(low)
            dwc[:, :, :, :, :, into] = got.reshape(4, 2, 2, 2, part // 8, 256)
            return carry

        lax.fori_loop(0, width // 256, one, 0)

    starts_at = [3 * width, width, 0, 2 * width]

    def cols_of(i):
        return pl.ds(starts_at[i], width)

    def to_core(i):
        return net.send(dwc.at[:, :, :, 1 - core, :, cols_of(i)], cr.at[i], "core")

    weight_chunk(zedt, lambda cols: do_ref[:, cols], 3 * width)
    sc = [to_core(0)]

    g1a.wait_recv()
    g1b.wait_recv()
    g2[z2] = (g2[z2].astype(full) + g2_z1[1].astype(full)).astype(low)
    g2s = net.send(g2.at[z2], g2_z2, "z2")

    gu_first()
    dn_first()
    dn_second(0)
    dn_second(1)

    place = me * rows + lax.broadcasted_iota(jnp.int32, (rows, 1), 0)
    starts = jnp.broadcast_to(starts_ref[...], (8, rows)).T[:, 0:1]
    keep_one = (place - 1 >= starts).astype(full)
    keep_two = (place - 2 >= starts).astype(full)
    load_gext.wait()
    load_proj.wait()
    s1[rows:] = jnp.zeros((s1.shape[0] - rows, 128), full)
    s2[rows:] = jnp.zeros((s2.shape[0] - rows, 128), full)
    dg = dh2
    row8 = lax.broadcasted_iota(jnp.int32, (8, 128), 0)

    def unmix(i, carry):
        at = pl.ds(pl.multiple_of(i * 128, 128), 128)
        cat = pl.ds(pl.multiple_of(width + i * 128, 128), 128)
        zi = i // (part // 128)
        inside = pl.ds(pl.multiple_of((i % (part // 128)) * 128, 128), 128)
        taps = small_all[zi, :, inside].astype(full)
        tap0, tap1, tap2 = taps[2:3], taps[3:4], taps[4:5]
        current, lag_one, lag_two = gext[16:, at], gext[15 : rows + 15, at], gext[14 : rows + 14, at]
        mixed = tap0 * current + keep_one * tap1 * lag_one + keep_two * tap2 * lag_two
        back = dz[:, at]
        dp[:, cat] = (back * mixed).astype(low)
        dm = back * proj[:, cat]
        t1, t2 = keep_one * dm, keep_two * dm
        for k, value in ((2, dm * current), (3, t1 * lag_one), (4, t2 * lag_two)):
            sums[k : k + 1, at] = jnp.sum(folded(value), axis=0, keepdims=True)
        s1[:rows] = tap1 * t1
        s2[:rows] = tap2 * t2
        dg[:, at] = tap0 * dm + s1[1 : rows + 1] + s2[2 : rows + 2]
        ret_send[:, at] = jnp.where(
            row8 == 6, s2[0:1], jnp.where(row8 == 7, s1[0:1] + s2[1:2], 0.0)
        )
        return carry

    lax.fori_loop(0, width // 128, unmix, 0)
    back = net.send(ret_send, ret_land, before)

    def norm_one(i, carry):
        at = pl.ds(pl.multiple_of(i * 128, 128), 128)
        xf = x_ref[at].astype(full)
        rate = lax.rsqrt(jnp.mean(xf * xf, axis=-1, keepdims=True) + epsilon)
        ht[:, at] = (xf * rate * gain_one).astype(low).T
        return carry

    lax.fori_loop(0, rows // 128, norm_one, 0)
    weight_chunk(ht, lambda cols: dp[:, pl.ds(pl.multiple_of(width + cols.start, 256), 256)], width)
    sc.append(to_core(1))

    orders = ["z", "xy", "yx", "xy"]
    def spot_of(i, zi, yi, xi):
        return (zi, yi, xi, core, slice(None), cols_of(i))

    def add_core(i):
        sc[i].wait_recv()

        def one(j, carry):
            zi, yi, xi = j // 4, (j // 2) % 2, j % 2
            spot = spot_of(i, zi, yi, xi)
            dwc[spot] = (dwc[spot].astype(full) + cr[i, zi, yi, xi].astype(full)).astype(low)
            return carry

        lax.fori_loop(0, 16, one, 0)
        cols = cols_of(i)
        if orders[i] == "xy":
            return net.send(dwc.at[:, :, 1 - xbit, core, :, cols], r1.at[i], "x")
        if orders[i] == "yx":
            return net.send(dwc.at[:, 1 - ybit, :, core, :, cols], r1.at[i], "y")
        if orders[i] == "z":
            return [
                net.send(dwc.at[zz, :, :, core, :, cols], r1.at[i, pl.ds(2 * k, 2)], "z1")
                for k, zz in enumerate((z1, z3))
            ]
        return [
            net.send(dwc.at[:, yi, xi, core, :, cols], land, seat)
            for yi, xi, land, seat in (
                (ybit, 1 - xbit, r1.at[i, :, 0], "x"),
                (1 - ybit, xbit, r1.at[i, :, 1], "y"),
                (1 - ybit, 1 - xbit, r2.at[i], cross),
            )
        ]

    def add_first(i, copy):
        if orders[i] == "z":
            for c in copy:
                c.wait_recv()

            def pair_of(j, carry):
                yi, xi = j // 2, j % 2
                for k, zz in enumerate((z2, z)):
                    spot = spot_of(i, zz, yi, xi)
                    land = r1[i, 2 - 2 * k + yi, xi]
                    dwc[spot] = (dwc[spot].astype(full) + land.astype(full)).astype(low)
                return carry

            lax.fori_loop(0, 4, pair_of, 0)
            return [
                net.send(
                    dwc.at[z2, yi, :, core, :, cols_of(i)], r2.at[i, pl.ds(2 * yi, 2)], "z2"
                )
                for yi in range(2)
            ]
        copy.wait_recv()

        def one(j, carry):
            zi, oi = j // 2, j % 2
            yi, xi = (oi, xbit) if orders[i] == "xy" else (ybit, oi)
            spot = spot_of(i, zi, yi, xi)
            dwc[spot] = (dwc[spot].astype(full) + r1[i, zi, oi].astype(full)).astype(low)
            return carry

        lax.fori_loop(0, 8, one, 0)
        cols = cols_of(i)
        if orders[i] == "xy":
            return net.send(dwc.at[:, 1 - ybit, xbit, core, :, cols], r2.at[i], "y")
        return net.send(dwc.at[:, ybit, 1 - xbit, core, :, cols], r2.at[i], "x")

    def add_second(i, copy):
        if orders[i] == "z":
            for c in copy:
                c.wait_recv()

            def one_of(j, carry):
                spot = spot_of(i, z, j // 2, j % 2)
                dwc[spot] = (dwc[spot].astype(full) + r2[i, j].astype(full)).astype(low)
                return carry

            lax.fori_loop(0, 4, one_of, 0)
            return [
                net.send(dwc.at[spot_of(i, z, yi, xi)], rz.at[i, k], seat)
                for k, (yi, xi, seat) in enumerate(
                    ((ybit, 1 - xbit, "x"), (1 - ybit, xbit, "y"), (1 - ybit, 1 - xbit, cross))
                )
            ]
        if orders[i] == "all":
            for c in copy:
                c.wait_recv()
        else:
            copy.wait_recv()

        def one(zi, carry):
            spot = spot_of(i, zi, ybit, xbit)
            got = dwc[spot].astype(full) + r2[i, zi].astype(full)
            if orders[i] == "all":
                got = got + r1[i, zi, 0].astype(full) + r1[i, zi, 1].astype(full)
            dwc[spot] = got.astype(low)
            return carry

        lax.fori_loop(0, 4, one, 0)
        return [
            net.send(dwc.at[spot_of(i, zz, ybit, xbit)], rz.at[i, k], seat)
            for k, (zz, seat) in enumerate(((z1, "z1"), (z2, "z2"), (z3, "z3")))
        ]

    def add_z(i, copies):
        for c in copies:
            c.wait_recv()
        own = fin_c.at[i, ybit, xbit, core]
        own[...] = (
            dwc[spot_of(i, z, ybit, xbit)].astype(full)
            + rz[i, 0].astype(full)
            + rz[i, 1].astype(full)
            + rz[i, 2].astype(full)
        ).astype(low)
        plus_upper(own, up_c.at[i], e_ref.at[pl.ds(0, part // 8)])
        return [net.send(own, own, seat) for seat in ("x", "y", cross)]

    def across_c(i, copies):
        for c in copies:
            c.wait_recv()
        return net.send(fin_c.at[i, :, :, core], fin_c.at[i, :, :, core], "core")

    def last_c(i, copy):
        copy.wait_recv()
        target = gout_out if i == 0 else gin_out.at[:, :, :, :, cols_of(i)]
        results.append(net.move(fin_c.at[i], target))

    def last_gu(k, copy):
        copy.wait_recv()
        for q in range(4):
            at = q * hq + k * chunk
            spot = fin_gu.at[k, q // 2, q % 2]
            results.append(net.move(spot.at[:, :, lo], ggu_out.at[:, :, pl.ds(at, chunk)]))
            results.append(
                net.move(spot.at[:, :, hi], ggu_out.at[:, :, pl.ds(hidden + at, chunk)])
            )

    a = {}
    b = {}
    a[0] = add_core(0)
    gu_d = [onward_gu(k, gu_b[k]) for k in range(2)]
    back.wait_recv()
    follows = (me < seq - 1).astype(full)
    dg[rows - 8 :] = dg[rows - 8 :] + ret_land[...] * follows

    def unproject(i, carry):
        at = pl.ds(pl.multiple_of(i * 128, 128), 128)
        xat = pl.ds(pl.multiple_of(2 * width + i * 128, 128), 128)
        dp[:, at] = (dg[:, at] * proj[:, xat]).astype(low)
        dp[:, xat] = (dg[:, at] * proj[:, at]).astype(low)
        return carry

    lax.fori_loop(0, width // 128, unproject, 0)
    weight_chunk(ht, lambda cols: dp[:, cols], 0)
    sc.append(to_core(2))
    a[1] = add_core(1)
    weight_chunk(ht, lambda cols: dp[:, pl.ds(pl.multiple_of(2 * width + cols.start, 256), 256)], 2 * width)
    sc.append(to_core(3))
    a[2] = add_core(2)
    b[0] = add_first(0, a[0])
    a[3] = add_core(3)

    g2s.wait_recv()
    own = fin_gu.at[2, xbit, core, ybit]
    own[...] = (
        g2[z].astype(full) + g2_z1[0].astype(full) + g2_z2[...].astype(full)
    ).astype(low)
    plus_upper(own, up_gu.at[2], e_ref.at[pl.ds(0, half), pl.ds(0, pair)])
    gu_b.append(spread_gu(2))
    dn_second(2)
    dn_third(0)

    load_win.wait()
    dh = dg

    def back_in(i, carry):
        cols = pl.ds(pl.multiple_of(i * part, part), part)
        dh[:, cols] = outer(dp[...], wc[i, :, :, :, : 3 * width].reshape(part, 3 * width))
        return carry

    lax.fori_loop(0, 4, back_in, 0)
    def norm_back(i, total):
        at = pl.ds(pl.multiple_of(i * tile, tile), tile)
        xf = x_ref[at].astype(full)
        rate = lax.rsqrt(jnp.mean(xf * xf, axis=-1, keepdims=True) + epsilon)
        normed = xf * rate
        got = dh[at]
        scaled = got * gain_one
        mean = jnp.mean(scaled * normed, axis=-1, keepdims=True)
        out_ref[at] = (dx1[at] + rate * (scaled - normed * mean)).astype(low)
        return total + folded(got * normed)

    total = lax.fori_loop(0, rows // tile, norm_back, jnp.zeros((8, width), full))
    keep_grad = net.move(out_ref, grad_out)
    sums[0:1, :] = jnp.sum(total, axis=0, keepdims=True)
    small_core = net.send(sums, sums_core, "core")
    b[1] = add_first(1, a[1])
    c = {0: add_second(0, b[0])}
    b[2] = add_first(2, a[2])
    dn_third(1)
    small_core.wait()
    sums[...] = sums[...] + sums_core[...]
    small_plane = [
        net.send(sums, sums_plane.at[i], seat) for i, seat in enumerate(("x", "y", cross))
    ]
    gu_c = [across_gu(k, gu_d[k]) for k in range(2)]
    dn_third(2)
    dn_fourth(0)
    c[1] = add_second(1, b[1])
    b[3] = add_first(3, a[3])
    c[2] = add_second(2, b[2])
    c[3] = add_second(3, b[3])
    dn_fourth(1)
    d = {0: add_z(0, c[0])}
    gu_d.append(onward_gu(2, gu_b[2]))
    dn_fourth(2)
    dn_fifth(0)
    for copy in small_plane:
        copy.wait()
    sums[...] = sums[...] + sums_plane[0] + sums_plane[1] + sums_plane[2]
    for i, seat in enumerate(upper):
        copy = net.send(sums, sums_plane.at[3 + i], seat)
        copy.wait()
        sums[...] = sums[...] + sums_plane[3 + i]

    def slab(zz):
        return sums.at[:, pl.ds(pl.multiple_of(zz * part, part), part)]

    small_z = [
        net.send(slab(zz), sums_z.at[i], seat)
        for i, (zz, seat) in enumerate(((z1, "z1"), (z2, "z2"), (z3, "z3")))
    ]
    d[1] = add_z(1, c[1])
    d[2] = add_z(2, c[2])
    d[3] = add_z(3, c[3])
    f = {0: across_c(0, d[0])}
    last_gu(0, gu_c[0])
    last_gu(1, gu_c[1])
    dn_fifth(1)
    dn_fifth(2)
    gu_c.append(across_gu(2, gu_d[2]))
    for i in (1, 2, 3):
        f[i] = across_c(i, d[i])
    for copy in small_z:
        copy.wait()
    small_out[...] = slab(z)[...] + sums_z[0] + sums_z[1] + sums_z[2]
    keep_small = net.move(small_out, gsmall_out)
    for k in range(3):
        dn_last(k)
    for i in (0, 1, 2, 3):
        last_c(i, f[i])
    last_gu(2, gu_c[2])

    @pl.when(~same0)
    def _():
        for copy in dn1:
            copy.wait_send()

    @pl.when(same0 & ~same1)
    def _():
        for copy in dn2:
            copy.wait_send()

    @pl.when(holder)
    def _():
        for copy in dnx:
            copy.wait_send()

    @pl.when(level)
    def _():
        for copy in dny + dnc:
            copy.wait_send()

    flat = [g1a, g1b, g2s, back, dn0, g1y] + gu_c + sc
    for group in gu_b + gu_d:
        flat += list(group)
    for group in (a, b, c, d, f):
        for copies in group.values():
            flat += copies if isinstance(copies, list) else [copies]
    for copy in flat:
        copy.wait_send()
    for copy in results:
        copy.wait()
    keep_grad.wait()
    keep_small.wait()


def finish(seq, starts, small_all, x, e, first, dh2, proj, zed, gext, wc, gu0, gu1, gu2, dn, dn2):
    rows, width = first.shape
    part = width // 4
    half, pair = gu0.shape
    chunk = pair // 2
    hq = 3 * chunk
    extra = seq.bit_length() - 4
    room = max(extra, 1)
    eighth = part // 8
    shape = jax.ShapeDtypeStruct
    anyspace = pl.BlockSpec(memory_space=pl.ANY)
    vmem = pl.BlockSpec(memory_space=pltpu.VMEM)
    outs = [
        shape((rows, width), low),
        shape((2, 2, 2, eighth, 3 * width), low),
        shape((2, 2, 2, eighth, width), low),
        shape((2, half, 8 * hq), low),
        shape((hq, width), low),
        shape((8, part), full),
    ]
    v = pltpu.VMEM
    outs += [
        shape((4, room, eighth, width), low),
        shape((3, room, half, pair), low),
        shape((3, room, chunk // 2, width), low),
    ]
    scratch = [
        v((4, 4, 2, eighth, 4 * width), low),
        v((rows, width), full),
        v((rows, width), full),
        v((rows, width), low),
        v((rows, width), low),
        v((rows, 3 * width), full),
        v((rows, width), low),
        v((width, rows), low),
        v((rows + 16, width), full),
        v((rows, width), full),
        v((rows, 3 * width), low),
        v((rows + 8, 128), full),
        v((rows + 8, 128), full),
        v((4, 2, 2, 2, eighth, 4 * width), low),
        v((8, width), full),
        v((8, width), full),
        v((8, width), full),
        v((8, width), full),
        v((3 + room, 8, width), full),
        v((3, 8, part), full),
        v((8, part), full),
        v((4, 4, 2, 2, eighth, width), low),
        v((4, 4, 2, eighth, width), low),
        v((4, 4, eighth, width), low),
        v((4, 3, eighth, width), low),
        v((4, 2, 2, 2, eighth, width), low),
        v((3, 2, 2, 2, half, pair), low),
        v((3, 2, chunk // 2, width), low),
        v((4, half, pair), low),
        v((2, half, pair), low),
        v((half, pair), low),
        v((half, pair), low),
        v((half, pair), low),
        v((3, chunk // 2, width), low),
        v((3, chunk // 2, width), low),
        v((3, chunk // 2, width), low),
        v((chunk // 2, width), low),
        v((chunk // 2, width), low),
        pltpu.SemaphoreType.DMA((100 + 12 * extra,)),
        pltpu.SemaphoreType.DMA((100 + 12 * extra,)),
        pltpu.SemaphoreType.DMA((60 + 12 * extra,)),
    ]
    return pl.pallas_call(
        functools.partial(finish_kernel, seq),
        out_shape=outs,
        in_specs=[vmem, vmem] + [anyspace] * 13,
        out_specs=[anyspace] * len(outs),
        scratch_shapes=scratch,
        compiler_params=pltpu.CompilerParams(
            collective_id=2, has_side_effects=True, vmem_limit_bytes=63 * MIB
        ),
        name="finish",
    )(starts, small_all, x, e, first, dh2, proj, zed, gext, wc, gu0, gu1, gu2, dn, dn2)


def cast_kernel(gu_ref, dn_ref, win_ref, wout_ref, res_ref, gx_ref, small_ref, *outs):
    ggu, gdn, gin, gout, res, gx, norm_one, norm_two, taps = outs
    ggu[...] = gu_ref[...].astype(full)
    gdn[...] = dn_ref[...].astype(full)
    gin[...] = win_ref[...].astype(full)
    gout[...] = wout_ref[...].astype(full)
    res[0] = res_ref[...]
    gx[0] = gx_ref[...]
    norm_one[...] = small_ref[0:1]
    norm_two[...] = small_ref[1:2]
    taps[...] = small_ref[2:5]


def cast(gu, dn, win, wout, result, grad_x, small):
    steps = 4
    arrays = (gu, dn, win, wout, result, grad_x)

    def cut(v, lead=False):
        rows, cols = v.shape
        if lead:
            return pl.BlockSpec((1, rows // steps, cols), lambda i: (0, i, 0))
        return pl.BlockSpec((rows // steps, cols), lambda i: (i, 0))

    def whole(shape):
        return pl.BlockSpec(shape, lambda i: (0, 0))

    part = small.shape[1]
    rows = ((1, part), (1, part), (3, part))
    moved = sum(v.size for v in arrays)
    return pl.pallas_call(
        cast_kernel,
        grid=(steps,),
        out_shape=[jax.ShapeDtypeStruct(v.shape, full) for v in arrays[:4]]
        + [jax.ShapeDtypeStruct((1, *v.shape), low) for v in arrays[4:]]
        + [jax.ShapeDtypeStruct(r, full) for r in rows],
        in_specs=[cut(v) for v in arrays] + [whole(small.shape)],
        out_specs=[cut(v) for v in arrays[:4]]
        + [cut(v, True) for v in arrays[4:]]
        + [whole(r) for r in rows],
        cost_estimate=pl.CostEstimate(flops=0, bytes_accessed=6 * moved, transcendentals=0),
        compiler_params=pltpu.CompilerParams(vmem_limit_bytes=63 * MIB),
        name="cast",
    )(*arrays, small)


def build(seq):
    def local(
        tokens,
        doc_start,
        norm1_gain,
        in_weight,
        conv_weight,
        out_weight,
        norm2_gain,
        gate_up_weight,
        down_weight,
        out_grad,
    ):
        x, cot = tokens[0], out_grad[0]
        starts = doc_start
        hq = down_weight.shape[0]
        small = (norm1_gain[None], norm2_gain[None], conv_weight.T)
        w_c, w_gu, w_down, cot_all, second_all, proj, first, zed, gext, small_all = gather(
            seq, x, cot, starts, *small, in_weight, out_weight, gate_up_weight, down_weight
        )
        result, dh2, gu0, gu1, gu2, dn, dn2, _ = feed(
            seq, second_all, cot_all, w_gu, w_down.reshape(hq, x.shape[1]), first
        )
        grad_x, grad_in, grad_out, grad_gu, grad_down, grad_small, *_ = finish(
            seq, starts, small_all, x, cot, first, dh2, proj, zed, gext, w_c, gu0, gu1, gu2, dn, dn2
        )
        grad_gu, grad_down, grad_in, grad_out, result, grad_x, norm_one, norm_two, taps = cast(
            grad_gu.reshape(gate_up_weight.shape),
            grad_down,
            grad_in.reshape(in_weight.shape),
            grad_out.reshape(out_weight.shape),
            result,
            grad_x,
            grad_small,
        )
        return (
            result,
            grad_x,
            norm_one[0],
            grad_in,
            taps.T,
            grad_out,
            norm_two[0],
            grad_gu,
            grad_down,
        )

    return local


def solution(mesh):
    in_specs = (
        P("wsh", "seq", None),
        P("wsh", "seq"),
        P("wsh"),
        P("wsh", None),
        P("wsh", None),
        P("wsh", None),
        P("wsh"),
        P("wsh", None),
        P("wsh", None),
        P("wsh", "seq", None),
    )
    out_specs = (
        P("wsh", "seq", None),
        P("wsh", "seq", None),
        P("wsh"),
        P("wsh", None),
        P("wsh", None),
        P("wsh", None),
        P("wsh"),
        P("wsh", None),
        P("wsh", None),
    )
    local = build(mesh.shape["seq"])
    return jax.shard_map(local, mesh=mesh, in_specs=in_specs, out_specs=out_specs, check_vma=False)
```

```python
import functools
import jax
import jax.numpy as jnp
from jax import lax
from jax.experimental import pallas as pl
from jax.experimental.pallas import tpu as pltpu
from jax.sharding import PartitionSpec as P

low = jnp.bfloat16
full = jnp.float32
MESH = pl.DeviceIdType.MESH
epsilon = 1e-06
MIB = 1 << 20


def mirrored(index, weight):
    return index + weight - 2 * weight * ((index // weight) % 2)


class Net:
    def __init__(self, me, z, send_sems, recv_sems, local_sems):
        self.me, self.z = me, z
        self.send_sems, self.recv_sems, self.local_sems = send_sems, recv_sems, local_sems
        self.count = self.local_count = 0

    def seat(self, name):
        me, z = self.me, self.z
        return {
            "core": {"seq": mirrored(me, 1), "wsh": z},
            "x": {"seq": mirrored(me, 2), "wsh": z},
            "y": {"seq": mirrored(me, 4), "wsh": z},
            "z1": {"seq": me, "wsh": mirrored(z, 1)},
            "z2": {"seq": me, "wsh": mirrored(z, 2)},
            "z3": {"seq": me, "wsh": 3 - z},
        }[name]

    def make(self, src, dst, seat, k=None):
        if k is None:
            k = self.count
            self.count += 1
        return pltpu.make_async_remote_copy(
            src_ref=src,
            dst_ref=dst,
            send_sem=self.send_sems.at[k],
            recv_sem=self.recv_sems.at[k],
            device_id=self.seat(seat) if isinstance(seat, str) else seat,
            device_id_type=MESH,
        )

    def send(self, src, dst, seat):
        copy = self.make(src, dst, seat)
        copy.start()
        return copy

    def move(self, src, dst):
        k = self.local_count
        self.local_count += 1
        copy = pltpu.make_async_copy(src, dst, self.local_sems.at[k])
        copy.start()
        return copy


def greet(seats):
    barrier = pltpu.get_barrier_semaphore()
    for seat in seats:
        pl.semaphore_signal(barrier, inc=1, device_id=seat, device_id_type=MESH)
    pl.semaphore_wait(barrier, len(seats))


def inner(left, right):
    return lax.dot_general(left, right, (((0,), (0,)), ((), ())), preferred_element_type=full)


def outer(left, right):
    return lax.dot_general(left, right, (((1,), (1,)), ((), ())), preferred_element_type=full)


def chunk_sizes(hq):
    chunk = hq // 3
    return chunk, 2 * chunk


def gather_kernel(
    seq,
    x_hbm, e_hbm, starts_ref, norm_one_ref, norm_two_ref, taps_ref, win_hbm, wout_hbm, wgu_hbm, wdn_hbm,
    wc_out, wgu_out, wdn_out, e_out, h2_out, proj_out, first_out, zed_out, gext_out, small_out,
    wc, ownf, winf, woutf, wguf, wdnf, wgu_own, wdn_own, x_ref, h_ref, proj, gext, zed, first, h2, small_all, small_own,
    send_sems, recv_sems, local_sems,
):
    me, z = lax.axis_index("seq"), lax.axis_index("wsh")
    net = Net(me, z, send_sems, recv_sems, local_sems)
    core, xbit, ybit = me % 2, (me // 2) % 2, (me // 4) % 2
    quarter = me % 4
    rows, width = x_hbm.shape
    part = width // 4
    hq = 6 * wdn_hbm.shape[2]
    hidden = 4 * hq
    half = part // 2
    z1, z2, z3 = mirrored(z, 1), mirrored(z, 2), 3 - z
    after = {"seq": lax.rem(me + 1, seq), "wsh": z}
    before = {"seq": lax.rem(me + seq - 1, seq), "wsh": z}

    piece = part // 8
    turn = (ybit * 2 + xbit) * 2 + core
    mine = pl.ds(pl.multiple_of(turn * piece, piece), piece)
    load_own = [
        net.move(win_hbm.at[mine], ownf.at[:, pl.ds(0, 3 * width)]),
        net.move(wout_hbm.at[mine], ownf.at[:, pl.ds(3 * width, width)]),
    ]
    load_x = net.move(x_hbm, x_ref.at[pl.ds(16, rows)])
    chunk, pair = chunk_sizes(hq)
    load_gu = []
    for k in range(3):
        for base, shift in ((quarter * hq, 0), (hidden + quarter * hq, chunk)):
            cut = pl.ds(pl.multiple_of(base + k * chunk, 128), chunk)
            load_gu.append(
                net.move(wgu_hbm.at[:, cut], wguf.at[:, pl.ds(k * pair + shift, chunk)])
            )
    load_win = net.move(win_hbm, winf)
    load_wout = net.move(wout_hbm, woutf)
    load_dn = net.move(wdn_hbm, wdnf)
    keep_e = net.move(e_hbm, e_out.at[0])
    small_own[...] = jnp.zeros_like(small_own)
    small_own[0:1] = norm_one_ref[...].astype(low).astype(full)
    small_own[1:2] = norm_two_ref[...].astype(low).astype(full)
    small_own[2:5] = taps_ref[...].astype(low).astype(full)
    small_all[z] = small_own[...].astype(low)
    for copy in load_own:
        copy.wait()
    spot = ybit * 2 + xbit
    spot_x = ybit * 2 + 1 - xbit
    spot_y = (1 - ybit) * 2 + xbit
    wc[z, spot, core] = ownf[...].astype(low)

    greet([net.seat(n) for n in ("core", "x", "y", "z1", "z2", "z3")] + [before])

    cols = [pl.ds(0, 2 * width), pl.ds(2 * width, 2 * width)]

    def own(zz):
        return wc.at[zz, spot, core]

    a1 = net.send(own(z), own(z), "z1")
    a2 = net.send(own(z), own(z), "z2")
    smalls = [net.send(small_all.at[z], small_all.at[z], n) for n in ("z1", "z2", "z3")]
    halo = net.send(x_hbm.at[pl.ds(rows - 16, 16)], x_ref.at[pl.ds(0, 16)], after)

    for copy in load_gu:
        copy.wait()
    wgu_own[...] = wguf[...].astype(low)
    keep_gu = net.move(wgu_own, wgu_out.at[z])
    load_win.wait()
    load_wout.wait()

    def cast_block(i, carry):
        @pl.when(i != turn)
        def _():
            at = pl.ds(pl.multiple_of(i * piece, piece), piece)
            wc[z, i // 2, i % 2, :, : 3 * width] = winf[at].astype(low)
            wc[z, i // 2, i % 2, :, 3 * width :] = woutf[at].astype(low)

        return carry

    lax.fori_loop(0, 8, cast_block, 0)
    load_dn.wait()

    def cast_dn(i, carry):
        wdn_own[i // 2, i % 2] = wdnf[i // 2, i % 2].astype(low)
        return carry

    lax.fori_loop(0, 6, cast_dn, 0)

    def spread(zz):
        return net.send(own(zz), own(zz), "x"), net.send(own(zz), own(zz), "y")

    def onward(zz, b):
        b[0].wait_recv()
        place = wc.at[zz, spot_x, core, :, cols[0]]
        d0 = net.send(place, place, "y")
        b[1].wait_recv()
        place = wc.at[zz, spot_y, core, :, cols[1]]
        return d0, net.send(place, place, "x")

    def across(zz, b, d):
        d[0].wait_recv()
        d[1].wait_recv()
        return net.send(wc.at[zz, :, core], wc.at[zz, :, core], "core")

    a1.wait_recv()
    b1 = spread(z1)
    a2.wait_recv()
    a3 = net.send(own(z2), own(z2), "z1")
    b2 = spread(z2)

    def gu(zz, yy, k):
        at = pl.ds(pl.multiple_of(yy * half, half), half)
        return wgu_out.at[zz, at, pl.ds(k * pair, pair)]

    f1, f2, f3, g1, g2, g3 = [], [], [], [], [], []
    for k in range(3):
        source = wgu_own.at[
            pl.ds(pl.multiple_of(ybit * half, half), half), pl.ds(k * pair, pair)
        ]
        f1.append(net.send(source, gu(z, ybit, k), "z1"))
        f2.append(net.send(source, gu(z, ybit, k), "z2"))

    same0 = (z % 2) == (quarter % 2)
    same1 = (z // 2) == (quarter // 2)
    holder = same0 & same1
    dn2, dn1a, dn1b, dny = [], [], [], []
    for k in range(3):
        source = wdn_own.at[k, ybit]
        target = wdn_out.at[k, ybit]
        dn2.append(net.make(source, target, "z2"))
        dn1a.append(net.make(source, target, "z1"))
        dn1b.append(net.make(target, target, "z1", net.count - 1))
        dny.append(net.make(target, target, "y"))
    keep_dn = pltpu.make_async_copy(wdn_own, wdn_out, local_sems.at[24])

    @pl.when(holder)
    def _():
        for k in range(3):
            dn2[k].start()
        keep_dn.start()

    def pass_gu(k):
        f1[k].wait_recv()
        g1.append(net.send(gu(z1, ybit, k), gu(z1, ybit, k), "y"))
        f2[k].wait_recv()
        f3.append(net.send(gu(z2, ybit, k), gu(z2, ybit, k), "z1"))
        g2.append(net.send(gu(z2, ybit, k), gu(z2, ybit, k), "y"))

    def pass_far(k):
        f3[k].wait_recv()
        g3.append(net.send(gu(z3, ybit, k), gu(z3, ybit, k), "y"))

    for copy in smalls:
        copy.wait_recv()
    load_x.wait()
    halo.wait_recv()

    def row_of(k):
        return jnp.concatenate([small_all[i, k : k + 1, :] for i in range(4)], 1).astype(full)

    gain_one, gain_two = row_of(0), row_of(1)

    def norm_one(i, carry):
        at = pl.ds(pl.multiple_of(i * 176, 16), 176)
        xf = x_ref[at].astype(full)
        rate = lax.rsqrt(jnp.mean(xf * xf, axis=-1, keepdims=True) + epsilon)
        h_ref[at] = (xf * rate * gain_one).astype(low)
        return carry

    lax.fori_loop(0, (rows + 16) // 176, norm_one, 0)
    d1 = onward(z1, b1)
    d2 = onward(z2, b2)
    a3.wait_recv()
    b3 = spread(z3)

    def pass_dn(k):
        @pl.when(same0 & ~same1)
        def _():
            dn2[k].wait_recv()
            dn1b[k].start()
            dny[k].start()

        @pl.when(~same0)
        def _():
            dn1a[k].wait_recv()
            dny[k].start()

    c1 = across(z1, b1, d1)
    c2 = across(z2, b2, d2)
    d3 = onward(z3, b3)
    pass_gu(0)
    c3 = across(z3, b3, d3)

    @pl.when(holder)
    def _():
        for k in range(3):
            dn1a[k].start()

    for c in (c1, c2, c3):
        c.wait_recv()
    ex = net.send(e_hbm, e_out.at[1], "x")
    ec = net.send(e_hbm, e_out.at[2], "core")
    pass_gu(1)

    def project(i, carry):
        at = pl.ds(pl.multiple_of(i * 512, 512), 512)
        proj[:, at] = jnp.dot(
            h_ref[...], wc[:, :, :, :, at].reshape(width, 512), preferred_element_type=full
        )
        return carry

    lax.fori_loop(0, 6, project, 0)
    keep_wc = net.move(wc, wc_out)
    keep_proj = net.move(proj.at[pl.ds(16, rows)], proj_out)

    pass_gu(2)
    place = me * rows + lax.broadcasted_iota(jnp.int32, (rows, 1), 0)
    starts = jnp.broadcast_to(starts_ref[...], (8, rows)).T[:, 0:1]
    keep_one = (place - 1 >= starts).astype(full)
    keep_two = (place - 2 >= starts).astype(full)
    cw = 128
    def mix(i, carry):
        at = pl.ds(pl.multiple_of(i * cw, cw), cw)
        xat = pl.ds(pl.multiple_of(2 * width + i * cw, cw), cw)
        cat = pl.ds(pl.multiple_of(width + i * cw, cw), cw)
        gext[:, at] = (proj[:, at] * proj[:, xat]).astype(low).astype(full)
        zi = i // (part // cw)
        inside = pl.ds(pl.multiple_of((i % (part // cw)) * cw, cw), cw)
        taps = small_all[zi, :, inside].astype(full)
        mixed = (
            taps[2:3] * gext[16:, at]
            + keep_one * taps[3:4] * gext[15 : rows + 15, at]
            + keep_two * taps[4:5] * gext[14 : rows + 14, at]
        )
        zed[:, at] = (proj[16:, cat] * mixed).astype(low)
        return carry

    lax.fori_loop(0, width // cw, mix, 0)
    keep_zed = net.move(zed, zed_out)
    keep_gext = net.move(gext, gext_out)

    pass_dn(0)
    pass_far(0)
    pass_dn(1)

    def project_out(i, carry):
        at = pl.ds(pl.multiple_of(i * 512, 512), 512)
        wat = pl.ds(pl.multiple_of(3 * width + i * 512, 512), 512)
        first[:, at] = x_ref[16:, at].astype(full) + jnp.dot(
            zed[...], wc[:, :, :, :, wat].reshape(width, 512), preferred_element_type=full
        )
        return carry

    lax.fori_loop(0, 2, project_out, 0)
    keep_first = net.move(first, first_out)
    pass_far(1)

    def norm_two(i, carry):
        at = pl.ds(pl.multiple_of(i * 128, 128), 128)
        xf = first[at]
        rate = lax.rsqrt(jnp.mean(xf * xf, axis=-1, keepdims=True) + epsilon)
        h2[at] = (xf * rate * gain_two).astype(low)
        return carry

    lax.fori_loop(0, rows // 128, norm_two, 0)
    keep_h2 = net.move(h2, h2_out.at[0])
    hx = net.send(h2, h2_out.at[1], "x")
    hc = net.send(h2, h2_out.at[2], "core")
    keep_small = net.move(small_all, small_out)

    pass_far(2)
    ex.wait_recv()
    exc = net.send(e_out.at[1], e_out.at[3], "core")
    pass_dn(2)
    hx.wait_recv()
    hxc = net.send(h2_out.at[1], h2_out.at[3], "core")
    for c in (*g1, *g2, *g3, ec, exc, hc, hxc):
        c.wait_recv()

    @pl.when(~holder)
    def _():
        for copy in dny:
            copy.wait()

    @pl.when(holder)
    def _():
        for copy in dn2 + dn1a:
            copy.wait_send()
        keep_dn.wait()

    @pl.when(same0 & ~same1)
    def _():
        for copy in dn1b:
            copy.wait_send()

    for c in (
        *smalls, halo, a1, a2, a3, *b1, *b2, *b3, *d1, *d2, *d3, c1, c2, c3,
        *f1, *f2, *f3, *g1, *g2, *g3, ex, ec, exc, hx, hc, hxc,
    ):
        c.wait_send()
    for c in (keep_e, keep_gu, keep_wc, keep_proj, keep_zed, keep_gext, keep_first, keep_h2, keep_small):
        c.wait()


def gather(seq, x, e, starts, norm_one, norm_two, taps, win, wout, wgu, wdn):
    rows, width = x.shape
    part = width // 4
    hq = wdn.shape[0]
    thirds = (3, 2, hq // 6, width)
    wdn = wdn.reshape(thirds)
    shape = jax.ShapeDtypeStruct
    anyspace = pl.BlockSpec(memory_space=pl.ANY)
    vmem = pl.BlockSpec(memory_space=pltpu.VMEM)
    conv = (4, 4, 2, part // 8, 4 * width)
    outs = [
        shape(conv, low),
        shape((4, part, 2 * hq), low),
        shape(thirds, low),
        shape((4, rows, width), low),
        shape((4, rows, width), low),
        shape((rows, 3 * width), full),
        shape((rows, width), full),
        shape((rows, width), low),
        shape((rows + 16, width), full),
        shape((4, 16, part), low),
    ]
    scratch = [
        pltpu.VMEM(conv, low),
        pltpu.VMEM((part // 8, 4 * width), full),
        pltpu.VMEM((part, 3 * width), full),
        pltpu.VMEM((part, width), full),
        pltpu.VMEM((part, 2 * hq), full),
        pltpu.VMEM(thirds, full),
        pltpu.VMEM((part, 2 * hq), low),
        pltpu.VMEM(thirds, low),
        pltpu.VMEM((rows + 16, width), low),
        pltpu.VMEM((rows + 16, width), low),
        pltpu.VMEM((rows + 16, 3 * width), full),
        pltpu.VMEM((rows + 16, width), full),
        pltpu.VMEM((rows, width), low),
        pltpu.VMEM((rows, width), full),
        pltpu.VMEM((rows, width), low),
        pltpu.VMEM((4, 16, part), low),
        pltpu.VMEM((16, part), full),
        pltpu.SemaphoreType.DMA((64,)),
        pltpu.SemaphoreType.DMA((64,)),
        pltpu.SemaphoreType.DMA((26,)),
    ]
    return pl.pallas_call(
        functools.partial(gather_kernel, seq),
        out_shape=outs,
        in_specs=[anyspace, anyspace] + [vmem] * 4 + [anyspace] * 4,
        out_specs=[anyspace] * len(outs),
        scratch_shapes=scratch,
        compiler_params=pltpu.CompilerParams(
            collective_id=0, has_side_effects=True, vmem_limit_bytes=56 * MIB
        ),
        name="gather",
    )(x, e, starts, norm_one, norm_two, taps, win, wout, wgu, wdn)


def feed_kernel(
    seq,
    h2_hbm, e_hbm, wgu_hbm, wdn_hbm, first_hbm,
    result_out, dh2_out, gu0_out, gu1_out, gu2_out, dn_out, dn2_out, land_out,
    h2, h2t, e, wgu, wdn, a, at_ref, du, u, da, dgu, ddn, send_a, send_b, send_x, send_o, temp, acc, acc_out,
    gu0_y, gu2_y, dn_y, gu0_z1, gu0_z2, gu1_z1, gu1_z2, gu0_s, gu1_s, gu1_t, gu0_f,
    send_sems, recv_sems, local_sems,
):
    me, z = lax.axis_index("seq"), lax.axis_index("wsh")
    net = Net(me, z, send_sems, recv_sems, local_sems)
    ybit = (me // 4) % 2
    rows, width = first_hbm.shape
    hq = wdn.shape[0]
    chunk, pair = chunk_sizes(hq)
    part = width // 4
    half = part // 2
    z1, z2, z3 = mirrored(z, 1), mirrored(z, 2), 3 - z
    block = 4 * rows

    load_h2, load_e, load_gu, load_dn = [], [], [], []

    def load_block(j):
        load_h2.append(net.move(h2_hbm.at[j], h2.at[pl.ds(j * rows, rows)]))
        load_e.append(net.move(e_hbm.at[j], e.at[pl.ds(j * rows, rows)]))

    def load_chunk(k):
        pcols, ccols = pl.ds(k * pair, pair), pl.ds(k * chunk, chunk)
        for i in range(4):
            load_gu.append(net.move(wgu_hbm.at[i, :, pcols], wgu.at[pl.ds(i * part, part), pcols]))
        load_dn.append(net.move(wdn_hbm.at[ccols], wdn.at[ccols]))

    load_chunk(0)
    for j in range(4):
        load_block(j)
    load_chunk(1)
    load_chunk(2)
    load_first = net.move(first_hbm, acc_out)
    greet([net.seat(n) for n in ("core", "x", "y", "z1", "z2")])

    def turn(j, carry):
        at = pl.ds(pl.multiple_of(j * 256, 256), 256)
        h2t[:, at] = h2[at].T
        return carry

    def forward(k, slots, step):
        pcols, ccols = pl.ds(k * pair, pair), pl.ds(k * chunk, chunk)

        def one(i, carry):
            j = slots + i * step
            at = pl.ds(pl.multiple_of(j * rows, rows), rows)
            u[...] = jnp.dot(h2[at], wgu[:, pcols], preferred_element_type=full)
            da[...] = outer(e[at], wdn[ccols])

            def piece(r, carry):
                rr = pl.ds(pl.multiple_of(r * 64, 64), 64)
                tt = pl.ds(pl.multiple_of(j * rows + r * 64, 64), 64)
                gate, upper, back = u[rr, :chunk], u[rr, chunk:], da[rr]
                sigma = jax.nn.sigmoid(gate)
                swish = gate * sigma
                a[tt, ccols] = (swish * upper).astype(low)
                du[tt, pl.ds(k * pair, chunk)] = (
                    back * upper * (sigma * (1.0 + gate * (1.0 - sigma)))
                ).astype(low)
                du[tt, pl.ds(k * pair + chunk, chunk)] = (back * swish).astype(low)
                return carry

            lax.fori_loop(0, rows // 64, piece, 0)
            return carry

        lax.fori_loop(0, 4 // step, one, 0)

    def weights(k):
        def turn_a(j, carry):
            at = pl.ds(pl.multiple_of(j * rows, rows), rows)
            at_ref[:, at] = a[at, pl.ds(k * chunk, chunk)].T
            return carry

        lax.fori_loop(0, 4, turn_a, 0)

        def gate_up(n, carry):
            cols = pl.ds(pl.multiple_of(k * pair + n * 256, 256), 256)
            got = jnp.dot(h2t[...], du[:, cols], preferred_element_type=full).astype(low)
            dgu[:, :, :, cols] = got.reshape(4, 2, half, 256)
            return carry

        lax.fori_loop(0, pair // 256, gate_up, 0)

        def down(n, carry):
            cols = pl.ds(pl.multiple_of(n * 512, 512), 512)
            got = jnp.dot(at_ref[...], e[:, cols], preferred_element_type=full).astype(low)
            ddn[k, :, :, cols] = got.reshape(2, chunk // 2, 512)
            return carry

        lax.fori_loop(0, width // 512, down, 0)

    def cols_of(k):
        return pl.ds(k * pair, pair)

    for copy in load_gu[:4] + load_dn[:1]:
        copy.wait()
    for j in range(4):
        load_h2[j].wait()
        load_e[j].wait()
        forward(0, j, 4)
    lax.fori_loop(0, block // 256, turn, 0)
    weights(0)
    for copy in load_gu[4:] + load_dn[1:]:
        copy.wait()
    y0 = net.send(dgu.at[:, 1 - ybit, :, cols_of(0)], gu0_y, "y")
    yd0 = net.send(ddn.at[0, 1 - ybit], dn_y.at[0], "y")
    forward(1, 0, 1)
    forward(2, 1, 2)

    def sum_rows(put, count, step):
        def one(i, carry):
            put(pl.ds(pl.multiple_of(i * step, step), step))
            return carry

        lax.fori_loop(0, count // step, one, 0)

    def accumulate(target):
        def go(at):
            target[at] = target[at] + temp[at].astype(full)

        return go

    def keep(cols, value):
        acc[:, cols] = value

    def more(cols, value):
        acc_out[:, cols] = acc_out[:, cols] + value

    def gu0_sum(i, carry):
        gu0_s[i] = (dgu[i, ybit, :, cols_of(0)].astype(full) + gu0_y[i].astype(full)).astype(low)
        return carry

    def gu1_sum(i, carry):
        gu1_t[i] = (dgu[z2, i, :, cols_of(1)].astype(full) + gu1_z1[1, i].astype(full)).astype(low)
        gu1_s[i] = (dgu[z, i, :, cols_of(1)].astype(full) + gu1_z1[0, i].astype(full)).astype(low)
        return carry

    def gu1_more(i, carry):
        gu1_s[i] = (gu1_s[i].astype(full) + gu1_z2[i].astype(full)).astype(low)
        return carry

    def finish(at):
        send_a[at] = (acc_out[at] + temp[at].astype(full)).astype(low)

    def grad_rows(j, put):
        at = pl.ds(j * rows, rows)

        def one(n, carry):
            cols = pl.ds(pl.multiple_of(n * 256, 256), 256)
            put(cols, outer(du[at], wgu[cols]))
            return carry

        lax.fori_loop(0, width // 256, one, 0)

    def out_rows(j, put):
        at = pl.ds(j * rows, rows)

        def one(n, carry):
            cols = pl.ds(pl.multiple_of(n * 256, 256), 256)
            put(cols, jnp.dot(a[at], wdn[:, cols], preferred_element_type=full))
            return carry

        lax.fori_loop(0, width // 256, one, 0)

    def store(ref):
        def put(cols, value):
            ref[:, cols] = value.astype(low)

        return put

    def add(target, other):
        def put(cols, value):
            target[:, cols] = (value + other[:, cols].astype(full)).astype(target.dtype)

        return put

    def fetch(j):
        copy = net.move(land_out.at[j], temp)
        copy.wait()

    grad_rows(3, store(send_a))
    ga = net.send(send_a, land_out.at[0], "core")
    out_rows(3, store(send_b))
    oa = net.send(send_b, land_out.at[3], "core")
    ga.wait_recv()
    fetch(0)
    grad_rows(1, add(send_x, temp))
    gx = net.send(send_x, land_out.at[1], "x")
    weights(1)
    m1 = net.send(dgu.at[z1, :, :, cols_of(1)], gu1_z1.at[0], "z1")
    m2 = net.send(dgu.at[z3, :, :, cols_of(1)], gu1_z1.at[1], "z1")
    yd1 = net.send(ddn.at[1, 1 - ybit], dn_y.at[1], "y")
    oa.wait_recv()
    fetch(3)
    out_rows(1, add(send_o, temp))
    ox = net.send(send_o, land_out.at[4], "x")
    y0.wait_recv()
    lax.fori_loop(0, 4, gu0_sum, 0)
    n1 = net.send(gu0_s.at[z1], gu0_z1.at[0], "z1")
    n2 = net.send(gu0_s.at[z3], gu0_z1.at[1], "z1")
    forward(2, 0, 2)
    weights(2)
    y2 = net.send(dgu.at[:, 1 - ybit, :, cols_of(2)], gu2_y, "y")
    keep_dn2 = net.move(ddn.at[2], dn2_out)
    m1.wait_recv()
    m2.wait_recv()
    lax.fori_loop(0, 2, gu1_sum, 0)
    m3 = net.send(gu1_t, gu1_z2, "z2")
    ga.wait_send()
    grad_rows(2, store(send_a))
    gb = net.send(send_a, land_out.at[2], "core")
    n1.wait_recv()
    n2.wait_recv()
    gu0_f[1] = (gu0_s[z2].astype(full) + gu0_z1[1].astype(full)).astype(low)
    n3 = net.send(gu0_f.at[1], gu0_z2, "z2")
    oa.wait_send()
    out_rows(2, store(send_b))
    ob = net.send(send_b, land_out.at[5], "core")
    grad_rows(0, keep)
    gb.wait_recv()
    fetch(2)
    sum_rows(accumulate(acc), rows, 64)
    load_first.wait()
    out_rows(0, more)
    ob.wait_recv()
    fetch(5)
    sum_rows(accumulate(acc_out), rows, 64)
    m3.wait_recv()
    lax.fori_loop(0, 2, gu1_more, 0)
    keep_gu1 = net.move(gu1_s, gu1_out)
    gx.wait_recv()
    fetch(1)
    sum_rows(accumulate(acc), rows, 64)
    keep_dh2 = net.move(acc, dh2_out)
    n3.wait_recv()
    gu0_f[0] = (
        gu0_s[z].astype(full) + gu0_z1[0].astype(full) + gu0_z2[...].astype(full)
    ).astype(low)
    keep_gu0 = net.move(gu0_f.at[0], gu0_out)
    ox.wait_recv()
    fetch(4)
    gb.wait_send()
    sum_rows(finish, rows, 64)
    keep_result = net.move(send_a, result_out)

    yd0.wait_recv()
    yd1.wait_recv()
    y2.wait_recv()

    def gu2_sum(i, carry):
        dgu[i, ybit, :, cols_of(2)] = (
            dgu[i, ybit, :, cols_of(2)].astype(full) + gu2_y[i].astype(full)
        ).astype(low)
        return carry

    lax.fori_loop(0, 4, gu2_sum, 0)
    keep_gu2 = net.move(dgu.at[:, ybit, :, cols_of(2)], gu2_out)

    def dn_sum(i, carry):
        ddn[i, ybit] = (ddn[i, ybit].astype(full) + dn_y[i].astype(full)).astype(low)
        return carry

    lax.fori_loop(0, 2, dn_sum, 0)
    keep_dn = net.move(ddn.at[pl.ds(0, 2), ybit], dn_out)
    for c in (y0, yd0, m1, m2, yd1, y2, n1, n2, m3, n3, ox, ob, gx):
        c.wait_send()
    for c in (keep_dh2, keep_gu0, keep_result, keep_gu2, keep_dn, keep_dn2, keep_gu1):
        c.wait()


def feed(seq, h2_all, e_all, wgu, wdn, first):
    rows, width = first.shape
    part = width // 4
    half = part // 2
    hq = wdn.shape[0]
    chunk, pair = chunk_sizes(hq)
    shape = jax.ShapeDtypeStruct
    anyspace = pl.BlockSpec(memory_space=pl.ANY)
    outs = [
        shape((rows, width), low),
        shape((rows, width), full),
        shape((half, pair), low),
        shape((2, half, pair), low),
        shape((4, half, pair), low),
        shape((2, chunk // 2, width), low),
        shape((2, chunk // 2, width), low),
        shape((6, rows, width), low),
    ]
    v = pltpu.VMEM
    scratch = [
        v((4 * rows, width), low),
        v((width, 4 * rows), low),
        v((4 * rows, width), low),
        v((width, 2 * hq), low),
        v((hq, width), low),
        v((4 * rows, hq), low),
        v((chunk, 4 * rows), low),
        v((4 * rows, 2 * hq), low),
        v((rows, pair), full),
        v((rows, chunk), full),
        v((4, 2, half, 2 * hq), low),
        v((3, 2, chunk // 2, width), low),
        v((rows, width), low),
        v((rows, width), low),
        v((rows, width), low),
        v((rows, width), low),
        v((rows, width), low),
        v((rows, width), full),
        v((rows, width), full),
        v((4, half, pair), low),
        v((4, half, pair), low),
        v((2, chunk // 2, width), low),
        v((2, half, pair), low),
        v((half, pair), low),
        v((2, 2, half, pair), low),
        v((2, half, pair), low),
        v((4, half, pair), low),
        v((2, half, pair), low),
        v((2, half, pair), low),
        v((2, half, pair), low),
        pltpu.SemaphoreType.DMA((24,)),
        pltpu.SemaphoreType.DMA((24,)),
        pltpu.SemaphoreType.DMA((44,)),
    ]
    return pl.pallas_call(
        functools.partial(feed_kernel, seq),
        out_shape=outs,
        in_specs=[anyspace] * 5,
        out_specs=[anyspace] * len(outs),
        scratch_shapes=scratch,
        compiler_params=pltpu.CompilerParams(
            collective_id=1, has_side_effects=True, vmem_limit_bytes=63 * MIB
        ),
        name="feed",
    )(h2_all, e_all, wgu, wdn, first)


def finish_kernel(
    seq,
    starts_ref, small_all, x_hbm, e_hbm, first_hbm, dh2_hbm, proj_hbm, zed_hbm, gext_hbm, wc_hbm,
    gu0_hbm, gu1_hbm, gu2_hbm, dn_hbm, dn2_hbm,
    grad_out, gin_out, gout_out, ggu_out, gdn_out, gsmall_out, up_c, up_gu, up_dn,
    wc, first, dh2, x_ref, e_ref, proj, zed, ht, gext, dx1, dp, s1, s2, dwc,
    ret_send, ret_land, sums, sums_core, sums_plane, sums_z, small_out,
    cr, r1, r2, rz, fin_c, fin_gu, fin_dn, g2, g2_z1, g2_z2, g1_o, g1_y, dnv, dn_z1, dn_z2, dn_o, dn_y,
    send_sems, recv_sems, local_sems,
):
    me, z = lax.axis_index("seq"), lax.axis_index("wsh")
    net = Net(me, z, send_sems, recv_sems, local_sems)
    core, xbit, ybit = me % 2, (me // 2) % 2, (me // 4) % 2
    quarter = me % 4
    rows, width = first.shape
    part = width // 4
    half = part // 2
    chunk = dnv.shape[1] * 2
    pair = 2 * chunk
    hq = 3 * chunk
    hidden = 4 * hq
    z1, z2, z3 = mirrored(z, 1), mirrored(z, 2), 3 - z
    after = {"seq": lax.rem(me + 1, seq), "wsh": z}
    before = {"seq": lax.rem(me + seq - 1, seq), "wsh": z}
    cross = {"seq": mirrored(mirrored(me, 2), 4), "wsh": z}
    upper = [
        {"seq": mirrored(me, 1 << bit), "wsh": z} for bit in range(3, seq.bit_length() - 1)
    ]
    same0 = (z % 2) == (quarter % 2)
    same1 = (z // 2) == (quarter // 2)
    holder = same0 & same1
    level = core == z % 2

    load_gu2 = net.move(gu2_hbm, g2)
    load_dn = [
        net.move(dn2_hbm.at[ybit], dnv.at[2]),
        net.move(dn2_hbm.at[1 - ybit], dn_o),
        net.move(dn_hbm, dnv.at[pl.ds(0, 2)]),
    ]
    load_gu = [
        net.move(gu0_hbm, fin_gu.at[0, xbit, core, ybit]),
        net.move(gu1_hbm.at[ybit], fin_gu.at[1, xbit, core, ybit]),
        net.move(gu1_hbm.at[1 - ybit], g1_o),
    ]
    load_first = net.move(first_hbm, first)
    load_dh2 = net.move(dh2_hbm, dh2)
    load_e = net.move(e_hbm, e_ref)
    outer_cols = pl.ds(3 * width, width)
    inner_cols = pl.ds(0, 3 * width)
    load_wc = net.move(
        wc_hbm.at[:, :, :, :, outer_cols], wc.at[:, :, :, :, outer_cols]
    )
    load_zed = net.move(zed_hbm, zed)
    zedt, do_ref, out_ref = ht, e_ref, zed
    load_x = net.move(x_hbm, x_ref)
    load_gext = net.move(gext_hbm, gext)
    load_proj = net.move(proj_hbm, proj)
    load_win = net.move(
        wc_hbm.at[:, :, :, :, inner_cols], wc.at[:, :, :, :, inner_cols]
    )
    greet(
        [net.seat(n) for n in ("core", "x", "y", "z1", "z2", "z3")] + [after, cross] + upper
    )

    def plus_upper(ref, land, temp):
        for i, seat in enumerate(upper):
            copy = net.send(ref, land.at[i], seat)
            copy.wait()
            net.move(land.at[i], temp).wait()
            ref[...] = (ref[...].astype(full) + temp[...].astype(full)).astype(ref.dtype)

    load_gu2.wait()
    g1a = net.send(g2.at[z1], g2_z1.at[0], "z1")
    g1b = net.send(g2.at[z3], g2_z1.at[1], "z1")
    for copy in load_dn:
        copy.wait()
    dn0 = net.send(dn_o, dn_y, "y")
    dn1 = [net.make(dnv.at[k], dn_z1.at[k], "z1") for k in range(3)]
    dn2 = [net.make(dnv.at[k], dn_z2.at[k], "z2") for k in range(3)]
    dnx, dny, dnc = [], [], []
    for k in range(3):
        spot = fin_dn.at[k, ybit]
        dnx.append(net.make(spot, spot, "x"))
        dny.append(net.make(spot, spot, "y"))
        dnc.append(net.make(fin_dn.at[k], fin_dn.at[k], "core"))

    @pl.when(~same0)
    def _():
        for k in range(2):
            dn1[k].start()

    def dn_first():
        dn0.wait_recv()
        dnv[2] = (dnv[2].astype(full) + dn_y[...].astype(full)).astype(low)

        @pl.when(~same0)
        def _():
            dn1[2].start()

    def dn_second(k):
        @pl.when(same0)
        def _():
            dn1[k].wait_recv()
            dnv[k] = (dnv[k].astype(full) + dn_z1[k].astype(full)).astype(low)

        @pl.when(same0 & ~same1)
        def _():
            dn2[k].start()

    def dn_third(k):
        @pl.when(holder)
        def _():
            dn2[k].wait_recv()
            dnv[k] = (dnv[k].astype(full) + dn_z2[k].astype(full)).astype(low)
            plus_upper(dnv.at[k], up_dn.at[k], dn_z1.at[k])
            fin_dn[k, ybit] = dnv[k]
            dnx[k].start()
            dny[k].start()

    def dn_fourth(k):
        @pl.when(level & ~holder)
        def _():
            dnx[k].wait_recv()
            dny[k].start()

    def dn_fifth(k):
        @pl.when(level)
        def _():
            dny[k].wait_recv()
            dnc[k].start()

    def dn_last(k):
        @pl.when(~level)
        def _():
            dnc[k].wait_recv()

        for y in range(2):
            at = (2 * k + y) * (chunk // 2)
            results.append(net.move(fin_dn.at[k, y], gdn_out.at[pl.ds(at, chunk // 2)]))

    results = []

    def spread_gu(k):
        own = fin_gu.at[k, xbit, core, ybit]
        return net.send(own, own, "x"), net.send(own, own, "y")

    lo, hi = pl.ds(0, chunk), pl.ds(chunk, chunk)

    def onward_gu(k, b):
        b[0].wait_recv()
        spot = fin_gu.at[k, 1 - xbit, core, ybit, :, lo]
        first_half = net.send(spot, spot, "y")
        b[1].wait_recv()
        spot = fin_gu.at[k, xbit, core, 1 - ybit, :, hi]
        return first_half, net.send(spot, spot, "x")

    def across_gu(k, d):
        d[0].wait_recv()
        d[1].wait_recv()
        return net.send(fin_gu.at[k, :, core], fin_gu.at[k, :, core], "core")

    for copy in load_gu:
        copy.wait()
    g1y = net.send(g1_o, g1_y, "y")
    room_gu = pl.ds(0, half), pl.ds(0, pair)
    plus_upper(fin_gu.at[0, xbit, core, ybit], up_gu.at[0], dp.at[room_gu])
    gu_b = [spread_gu(0)]

    def gu_first():
        g1y.wait_recv()
        own = fin_gu.at[1, xbit, core, ybit]
        own[...] = (own[...].astype(full) + g1_y[...].astype(full)).astype(low)
        plus_upper(own, up_gu.at[1], dp.at[room_gu])
        gu_b.append(spread_gu(1))

    def row_of(k):
        return jnp.concatenate([small_all[i, k : k + 1, :] for i in range(4)], 1).astype(full)

    gain_one, gain_two = row_of(0), row_of(1)
    sums[...] = jnp.zeros_like(sums)
    load_first.wait()
    load_dh2.wait()
    load_e.wait()
    tile = 32

    def folded(value):
        return jnp.sum(value.reshape(value.shape[0] // 8, 8, value.shape[1]), axis=0)

    def norm_two(i, total):
        at = pl.ds(pl.multiple_of(i * tile, tile), tile)
        xf, dh = first[at], dh2[at]
        rate = lax.rsqrt(jnp.mean(xf * xf, axis=-1, keepdims=True) + epsilon)
        normed = xf * rate
        scaled = dh * gain_two
        mean = jnp.mean(scaled * normed, axis=-1, keepdims=True)
        got = e_ref[at].astype(full) + rate * (scaled - normed * mean)
        dx1[at] = got
        do_ref[at] = got.astype(low)
        return total + folded(dh * normed)

    total = lax.fori_loop(0, rows // tile, norm_two, jnp.zeros((8, width), full))
    sums[1:2, :] = jnp.sum(total, axis=0, keepdims=True)

    load_wc.wait()
    dz = first

    def back_out(i, carry):
        cols = pl.ds(pl.multiple_of(i * part, part), part)
        dz[:, cols] = outer(do_ref[...], wc[i, :, :, :, 3 * width :].reshape(part, width))
        return carry

    lax.fori_loop(0, 4, back_out, 0)
    load_zed.wait()
    load_x.wait()

    def turn_zed(i, carry):
        cols = pl.ds(pl.multiple_of(i * 256, 256), 256)
        zedt[:, cols] = zed[cols].T
        return carry

    lax.fori_loop(0, rows // 256, turn_zed, 0)

    def weight_chunk(left, right, at):
        def one(n, carry):
            cols = pl.ds(pl.multiple_of(n * 256, 256), 256)
            into = pl.ds(pl.multiple_of(at + n * 256, 256), 256)
            got = jnp.dot(left[...], right(cols), preferred_element_type=full).astype(low)
            dwc[:, :, :, :, :, into] = got.reshape(4, 2, 2, 2, part // 8, 256)
            return carry

        lax.fori_loop(0, width // 256, one, 0)

    starts_at = [3 * width, width, 0, 2 * width]

    def cols_of(i):
        return pl.ds(starts_at[i], width)

    def to_core(i):
        return net.send(dwc.at[:, :, :, 1 - core, :, cols_of(i)], cr.at[i], "core")

    weight_chunk(zedt, lambda cols: do_ref[:, cols], 3 * width)
    sc = [to_core(0)]

    g1a.wait_recv()
    g1b.wait_recv()
    g2[z2] = (g2[z2].astype(full) + g2_z1[1].astype(full)).astype(low)
    g2s = net.send(g2.at[z2], g2_z2, "z2")

    gu_first()
    dn_first()
    dn_second(0)
    dn_second(1)

    place = me * rows + lax.broadcasted_iota(jnp.int32, (rows, 1), 0)
    starts = jnp.broadcast_to(starts_ref[...], (8, rows)).T[:, 0:1]
    keep_one = (place - 1 >= starts).astype(full)
    keep_two = (place - 2 >= starts).astype(full)
    load_gext.wait()
    load_proj.wait()
    s1[rows:] = jnp.zeros((s1.shape[0] - rows, 128), full)
    s2[rows:] = jnp.zeros((s2.shape[0] - rows, 128), full)
    dg = dh2
    row8 = lax.broadcasted_iota(jnp.int32, (8, 128), 0)

    def unmix(i, carry):
        at = pl.ds(pl.multiple_of(i * 128, 128), 128)
        cat = pl.ds(pl.multiple_of(width + i * 128, 128), 128)
        zi = i // (part // 128)
        inside = pl.ds(pl.multiple_of((i % (part // 128)) * 128, 128), 128)
        taps = small_all[zi, :, inside].astype(full)
        tap0, tap1, tap2 = taps[2:3], taps[3:4], taps[4:5]
        current, lag_one, lag_two = gext[16:, at], gext[15 : rows + 15, at], gext[14 : rows + 14, at]
        mixed = tap0 * current + keep_one * tap1 * lag_one + keep_two * tap2 * lag_two
        back = dz[:, at]
        dp[:, cat] = (back * mixed).astype(low)
        dm = back * proj[:, cat]
        t1, t2 = keep_one * dm, keep_two * dm
        for k, value in ((2, dm * current), (3, t1 * lag_one), (4, t2 * lag_two)):
            sums[k : k + 1, at] = jnp.sum(folded(value), axis=0, keepdims=True)
        s1[:rows] = tap1 * t1
        s2[:rows] = tap2 * t2
        dg[:, at] = tap0 * dm + s1[1 : rows + 1] + s2[2 : rows + 2]
        ret_send[:, at] = jnp.where(
            row8 == 6, s2[0:1], jnp.where(row8 == 7, s1[0:1] + s2[1:2], 0.0)
        )
        return carry

    lax.fori_loop(0, width // 128, unmix, 0)
    back = net.send(ret_send, ret_land, before)

    def norm_one(i, carry):
        at = pl.ds(pl.multiple_of(i * 128, 128), 128)
        xf = x_ref[at].astype(full)
        rate = lax.rsqrt(jnp.mean(xf * xf, axis=-1, keepdims=True) + epsilon)
        ht[:, at] = (xf * rate * gain_one).astype(low).T
        return carry

    lax.fori_loop(0, rows // 128, norm_one, 0)
    weight_chunk(ht, lambda cols: dp[:, pl.ds(pl.multiple_of(width + cols.start, 256), 256)], width)
    sc.append(to_core(1))

    orders = ["z", "xy", "yx", "xy"]
    def spot_of(i, zi, yi, xi):
        return (zi, yi, xi, core, slice(None), cols_of(i))

    def add_core(i):
        sc[i].wait_recv()

        def one(j, carry):
            zi, yi, xi = j // 4, (j // 2) % 2, j % 2
            spot = spot_of(i, zi, yi, xi)
            dwc[spot] = (dwc[spot].astype(full) + cr[i, zi, yi, xi].astype(full)).astype(low)
            return carry

        lax.fori_loop(0, 16, one, 0)
        cols = cols_of(i)
        if orders[i] == "xy":
            return net.send(dwc.at[:, :, 1 - xbit, core, :, cols], r1.at[i], "x")
        if orders[i] == "yx":
            return net.send(dwc.at[:, 1 - ybit, :, core, :, cols], r1.at[i], "y")
        if orders[i] == "z":
            return [
                net.send(dwc.at[zz, :, :, core, :, cols], r1.at[i, pl.ds(2 * k, 2)], "z1")
                for k, zz in enumerate((z1, z3))
            ]
        return [
            net.send(dwc.at[:, yi, xi, core, :, cols], land, seat)
            for yi, xi, land, seat in (
                (ybit, 1 - xbit, r1.at[i, :, 0], "x"),
                (1 - ybit, xbit, r1.at[i, :, 1], "y"),
                (1 - ybit, 1 - xbit, r2.at[i], cross),
            )
        ]

    def add_first(i, copy):
        if orders[i] == "z":
            for c in copy:
                c.wait_recv()

            def pair_of(j, carry):
                yi, xi = j // 2, j % 2
                for k, zz in enumerate((z2, z)):
                    spot = spot_of(i, zz, yi, xi)
                    land = r1[i, 2 - 2 * k + yi, xi]
                    dwc[spot] = (dwc[spot].astype(full) + land.astype(full)).astype(low)
                return carry

            lax.fori_loop(0, 4, pair_of, 0)
            return [
                net.send(
                    dwc.at[z2, yi, :, core, :, cols_of(i)], r2.at[i, pl.ds(2 * yi, 2)], "z2"
                )
                for yi in range(2)
            ]
        copy.wait_recv()

        def one(j, carry):
            zi, oi = j // 2, j % 2
            yi, xi = (oi, xbit) if orders[i] == "xy" else (ybit, oi)
            spot = spot_of(i, zi, yi, xi)
            dwc[spot] = (dwc[spot].astype(full) + r1[i, zi, oi].astype(full)).astype(low)
            return carry

        lax.fori_loop(0, 8, one, 0)
        cols = cols_of(i)
        if orders[i] == "xy":
            return net.send(dwc.at[:, 1 - ybit, xbit, core, :, cols], r2.at[i], "y")
        return net.send(dwc.at[:, ybit, 1 - xbit, core, :, cols], r2.at[i], "x")

    def add_second(i, copy):
        if orders[i] == "z":
            for c in copy:
                c.wait_recv()

            def one_of(j, carry):
                spot = spot_of(i, z, j // 2, j % 2)
                dwc[spot] = (dwc[spot].astype(full) + r2[i, j].astype(full)).astype(low)
                return carry

            lax.fori_loop(0, 4, one_of, 0)
            return [
                net.send(dwc.at[spot_of(i, z, yi, xi)], rz.at[i, k], seat)
                for k, (yi, xi, seat) in enumerate(
                    ((ybit, 1 - xbit, "x"), (1 - ybit, xbit, "y"), (1 - ybit, 1 - xbit, cross))
                )
            ]
        if orders[i] == "all":
            for c in copy:
                c.wait_recv()
        else:
            copy.wait_recv()

        def one(zi, carry):
            spot = spot_of(i, zi, ybit, xbit)
            got = dwc[spot].astype(full) + r2[i, zi].astype(full)
            if orders[i] == "all":
                got = got + r1[i, zi, 0].astype(full) + r1[i, zi, 1].astype(full)
            dwc[spot] = got.astype(low)
            return carry

        lax.fori_loop(0, 4, one, 0)
        return [
            net.send(dwc.at[spot_of(i, zz, ybit, xbit)], rz.at[i, k], seat)
            for k, (zz, seat) in enumerate(((z1, "z1"), (z2, "z2"), (z3, "z3")))
        ]

    def add_z(i, copies):
        for c in copies:
            c.wait_recv()
        own = fin_c.at[i, ybit, xbit, core]
        own[...] = (
            dwc[spot_of(i, z, ybit, xbit)].astype(full)
            + rz[i, 0].astype(full)
            + rz[i, 1].astype(full)
            + rz[i, 2].astype(full)
        ).astype(low)
        plus_upper(own, up_c.at[i], e_ref.at[pl.ds(0, part // 8)])
        return [net.send(own, own, seat) for seat in ("x", "y", cross)]

    def across_c(i, copies):
        for c in copies:
            c.wait_recv()
        return net.send(fin_c.at[i, :, :, core], fin_c.at[i, :, :, core], "core")

    def last_c(i, copy):
        copy.wait_recv()
        target = gout_out if i == 0 else gin_out.at[:, :, :, :, cols_of(i)]
        results.append(net.move(fin_c.at[i], target))

    def last_gu(k, copy):
        copy.wait_recv()
        for q in range(4):
            at = q * hq + k * chunk
            spot = fin_gu.at[k, q // 2, q % 2]
            results.append(net.move(spot.at[:, :, lo], ggu_out.at[:, :, pl.ds(at, chunk)]))
            results.append(
                net.move(spot.at[:, :, hi], ggu_out.at[:, :, pl.ds(hidden + at, chunk)])
            )

    a = {}
    b = {}
    a[0] = add_core(0)
    gu_d = [onward_gu(k, gu_b[k]) for k in range(2)]
    back.wait_recv()
    follows = (me < seq - 1).astype(full)
    dg[rows - 8 :] = dg[rows - 8 :] + ret_land[...] * follows

    def unproject(i, carry):
        at = pl.ds(pl.multiple_of(i * 128, 128), 128)
        xat = pl.ds(pl.multiple_of(2 * width + i * 128, 128), 128)
        dp[:, at] = (dg[:, at] * proj[:, xat]).astype(low)
        dp[:, xat] = (dg[:, at] * proj[:, at]).astype(low)
        return carry

    lax.fori_loop(0, width // 128, unproject, 0)
    weight_chunk(ht, lambda cols: dp[:, cols], 0)
    sc.append(to_core(2))
    a[1] = add_core(1)
    weight_chunk(ht, lambda cols: dp[:, pl.ds(pl.multiple_of(2 * width + cols.start, 256), 256)], 2 * width)
    sc.append(to_core(3))
    a[2] = add_core(2)
    b[0] = add_first(0, a[0])
    a[3] = add_core(3)

    g2s.wait_recv()
    own = fin_gu.at[2, xbit, core, ybit]
    own[...] = (
        g2[z].astype(full) + g2_z1[0].astype(full) + g2_z2[...].astype(full)
    ).astype(low)
    plus_upper(own, up_gu.at[2], e_ref.at[pl.ds(0, half), pl.ds(0, pair)])
    gu_b.append(spread_gu(2))
    dn_second(2)
    dn_third(0)

    load_win.wait()
    dh = dg

    def back_in(i, carry):
        cols = pl.ds(pl.multiple_of(i * part, part), part)
        dh[:, cols] = outer(dp[...], wc[i, :, :, :, : 3 * width].reshape(part, 3 * width))
        return carry

    lax.fori_loop(0, 4, back_in, 0)
    def norm_back(i, total):
        at = pl.ds(pl.multiple_of(i * tile, tile), tile)
        xf = x_ref[at].astype(full)
        rate = lax.rsqrt(jnp.mean(xf * xf, axis=-1, keepdims=True) + epsilon)
        normed = xf * rate
        got = dh[at]
        scaled = got * gain_one
        mean = jnp.mean(scaled * normed, axis=-1, keepdims=True)
        out_ref[at] = (dx1[at] + rate * (scaled - normed * mean)).astype(low)
        return total + folded(got * normed)

    total = lax.fori_loop(0, rows // tile, norm_back, jnp.zeros((8, width), full))
    keep_grad = net.move(out_ref, grad_out)
    sums[0:1, :] = jnp.sum(total, axis=0, keepdims=True)
    small_core = net.send(sums, sums_core, "core")
    b[1] = add_first(1, a[1])
    c = {0: add_second(0, b[0])}
    b[2] = add_first(2, a[2])
    dn_third(1)
    small_core.wait()
    sums[...] = sums[...] + sums_core[...]
    small_plane = [
        net.send(sums, sums_plane.at[i], seat) for i, seat in enumerate(("x", "y", cross))
    ]
    gu_c = [across_gu(k, gu_d[k]) for k in range(2)]
    dn_third(2)
    dn_fourth(0)
    c[1] = add_second(1, b[1])
    b[3] = add_first(3, a[3])
    c[2] = add_second(2, b[2])
    c[3] = add_second(3, b[3])
    dn_fourth(1)
    d = {0: add_z(0, c[0])}
    gu_d.append(onward_gu(2, gu_b[2]))
    dn_fourth(2)
    dn_fifth(0)
    for copy in small_plane:
        copy.wait()
    sums[...] = sums[...] + sums_plane[0] + sums_plane[1] + sums_plane[2]
    for i, seat in enumerate(upper):
        copy = net.send(sums, sums_plane.at[3 + i], seat)
        copy.wait()
        sums[...] = sums[...] + sums_plane[3 + i]

    def slab(zz):
        return sums.at[:, pl.ds(pl.multiple_of(zz * part, part), part)]

    small_z = [
        net.send(slab(zz), sums_z.at[i], seat)
        for i, (zz, seat) in enumerate(((z1, "z1"), (z2, "z2"), (z3, "z3")))
    ]
    d[1] = add_z(1, c[1])
    d[2] = add_z(2, c[2])
    d[3] = add_z(3, c[3])
    f = {0: across_c(0, d[0])}
    last_gu(0, gu_c[0])
    last_gu(1, gu_c[1])
    dn_fifth(1)
    dn_fifth(2)
    gu_c.append(across_gu(2, gu_d[2]))
    for i in (1, 2, 3):
        f[i] = across_c(i, d[i])
    for copy in small_z:
        copy.wait()
    small_out[...] = slab(z)[...] + sums_z[0] + sums_z[1] + sums_z[2]
    keep_small = net.move(small_out, gsmall_out)
    for k in range(3):
        dn_last(k)
    for i in (0, 1, 2, 3):
        last_c(i, f[i])
    last_gu(2, gu_c[2])

    @pl.when(~same0)
    def _():
        for copy in dn1:
            copy.wait_send()

    @pl.when(same0 & ~same1)
    def _():
        for copy in dn2:
            copy.wait_send()

    @pl.when(holder)
    def _():
        for copy in dnx:
            copy.wait_send()

    @pl.when(level)
    def _():
        for copy in dny + dnc:
            copy.wait_send()

    flat = [g1a, g1b, g2s, back, dn0, g1y] + gu_c + sc
    for group in gu_b + gu_d:
        flat += list(group)
    for group in (a, b, c, d, f):
        for copies in group.values():
            flat += copies if isinstance(copies, list) else [copies]
    for copy in flat:
        copy.wait_send()
    for copy in results:
        copy.wait()
    keep_grad.wait()
    keep_small.wait()


def finish(seq, starts, small_all, x, e, first, dh2, proj, zed, gext, wc, gu0, gu1, gu2, dn, dn2):
    rows, width = first.shape
    part = width // 4
    half, pair = gu0.shape
    chunk = pair // 2
    hq = 3 * chunk
    extra = seq.bit_length() - 4
    room = max(extra, 1)
    eighth = part // 8
    shape = jax.ShapeDtypeStruct
    anyspace = pl.BlockSpec(memory_space=pl.ANY)
    vmem = pl.BlockSpec(memory_space=pltpu.VMEM)
    outs = [
        shape((rows, width), low),
        shape((2, 2, 2, eighth, 3 * width), low),
        shape((2, 2, 2, eighth, width), low),
        shape((2, half, 8 * hq), low),
        shape((hq, width), low),
        shape((8, part), full),
    ]
    v = pltpu.VMEM
    outs += [
        shape((4, room, eighth, width), low),
        shape((3, room, half, pair), low),
        shape((3, room, chunk // 2, width), low),
    ]
    scratch = [
        v((4, 4, 2, eighth, 4 * width), low),
        v((rows, width), full),
        v((rows, width), full),
        v((rows, width), low),
        v((rows, width), low),
        v((rows, 3 * width), full),
        v((rows, width), low),
        v((width, rows), low),
        v((rows + 16, width), full),
        v((rows, width), full),
        v((rows, 3 * width), low),
        v((rows + 8, 128), full),
        v((rows + 8, 128), full),
        v((4, 2, 2, 2, eighth, 4 * width), low),
        v((8, width), full),
        v((8, width), full),
        v((8, width), full),
        v((8, width), full),
        v((3 + room, 8, width), full),
        v((3, 8, part), full),
        v((8, part), full),
        v((4, 4, 2, 2, eighth, width), low),
        v((4, 4, 2, eighth, width), low),
        v((4, 4, eighth, width), low),
        v((4, 3, eighth, width), low),
        v((4, 2, 2, 2, eighth, width), low),
        v((3, 2, 2, 2, half, pair), low),
        v((3, 2, chunk // 2, width), low),
        v((4, half, pair), low),
        v((2, half, pair), low),
        v((half, pair), low),
        v((half, pair), low),
        v((half, pair), low),
        v((3, chunk // 2, width), low),
        v((3, chunk // 2, width), low),
        v((3, chunk // 2, width), low),
        v((chunk // 2, width), low),
        v((chunk // 2, width), low),
        pltpu.SemaphoreType.DMA((100 + 12 * extra,)),
        pltpu.SemaphoreType.DMA((100 + 12 * extra,)),
        pltpu.SemaphoreType.DMA((60 + 12 * extra,)),
    ]
    return pl.pallas_call(
        functools.partial(finish_kernel, seq),
        out_shape=outs,
        in_specs=[vmem, vmem] + [anyspace] * 13,
        out_specs=[anyspace] * len(outs),
        scratch_shapes=scratch,
        compiler_params=pltpu.CompilerParams(
            collective_id=2, has_side_effects=True, vmem_limit_bytes=63 * MIB
        ),
        name="finish",
    )(starts, small_all, x, e, first, dh2, proj, zed, gext, wc, gu0, gu1, gu2, dn, dn2)


def cast_kernel(gu_ref, dn_ref, win_ref, wout_ref, res_ref, gx_ref, small_ref, *outs):
    ggu, gdn, gin, gout, res, gx, norm_one, norm_two, taps = outs
    ggu[...] = gu_ref[...].astype(full)
    gdn[...] = dn_ref[...].astype(full)
    gin[...] = win_ref[...].astype(full)
    gout[...] = wout_ref[...].astype(full)
    res[0] = res_ref[...]
    gx[0] = gx_ref[...]
    norm_one[...] = small_ref[0:1]
    norm_two[...] = small_ref[1:2]
    taps[...] = small_ref[2:5]


def cast(gu, dn, win, wout, result, grad_x, small):
    steps = 4
    arrays = (gu, dn, win, wout, result, grad_x)

    def cut(v, lead=False):
        rows, cols = v.shape
        if lead:
            return pl.BlockSpec((1, rows // steps, cols), lambda i: (0, i, 0))
        return pl.BlockSpec((rows // steps, cols), lambda i: (i, 0))

    def whole(shape):
        return pl.BlockSpec(shape, lambda i: (0, 0))

    part = small.shape[1]
    rows = ((1, part), (1, part), (3, part))
    moved = sum(v.size for v in arrays)
    return pl.pallas_call(
        cast_kernel,
        grid=(steps,),
        out_shape=[jax.ShapeDtypeStruct(v.shape, full) for v in arrays[:4]]
        + [jax.ShapeDtypeStruct((1, *v.shape), low) for v in arrays[4:]]
        + [jax.ShapeDtypeStruct(r, full) for r in rows],
        in_specs=[cut(v) for v in arrays] + [whole(small.shape)],
        out_specs=[cut(v) for v in arrays[:4]]
        + [cut(v, True) for v in arrays[4:]]
        + [whole(r) for r in rows],
        cost_estimate=pl.CostEstimate(flops=0, bytes_accessed=6 * moved, transcendentals=0),
        compiler_params=pltpu.CompilerParams(vmem_limit_bytes=63 * MIB),
        name="cast",
    )(*arrays, small)


def build(seq):
    def local(
        tokens,
        doc_start,
        norm1_gain,
        in_weight,
        conv_weight,
        out_weight,
        norm2_gain,
        gate_up_weight,
        down_weight,
        out_grad,
    ):
        x, cot = tokens[0], out_grad[0]
        starts = doc_start
        hq = down_weight.shape[0]
        small = (norm1_gain[None], norm2_gain[None], conv_weight.T)
        w_c, w_gu, w_down, cot_all, second_all, proj, first, zed, gext, small_all = gather(
            seq, x, cot, starts, *small, in_weight, out_weight, gate_up_weight, down_weight
        )
        result, dh2, gu0, gu1, gu2, dn, dn2, _ = feed(
            seq, second_all, cot_all, w_gu, w_down.reshape(hq, x.shape[1]), first
        )
        grad_x, grad_in, grad_out, grad_gu, grad_down, grad_small, *_ = finish(
            seq, starts, small_all, x, cot, first, dh2, proj, zed, gext, w_c, gu0, gu1, gu2, dn, dn2
        )
        grad_gu, grad_down, grad_in, grad_out, result, grad_x, norm_one, norm_two, taps = cast(
            grad_gu.reshape(gate_up_weight.shape),
            grad_down,
            grad_in.reshape(in_weight.shape),
            grad_out.reshape(out_weight.shape),
            result,
            grad_x,
            grad_small,
        )
        return (
            result,
            grad_x,
            norm_one[0],
            grad_in,
            taps.T,
            grad_out,
            norm_two[0],
            grad_gu,
            grad_down,
        )

    return local


def solution(mesh):
    in_specs = (
        P("wsh", "seq", None),
        P("wsh", "seq"),
        P("wsh"),
        P("wsh", None),
        P("wsh", None),
        P("wsh", None),
        P("wsh"),
        P("wsh", None),
        P("wsh", None),
        P("wsh", "seq", None),
    )
    out_specs = (
        P("wsh", "seq", None),
        P("wsh", "seq", None),
        P("wsh"),
        P("wsh", None),
        P("wsh", None),
        P("wsh", None),
        P("wsh"),
        P("wsh", None),
        P("wsh", None),
    )
    local = build(mesh.shape["seq"])
    return jax.shard_map(local, mesh=mesh, in_specs=in_specs, out_specs=out_specs, check_vma=False)
```
